512 devices in a mesh: gx: 8 (over z_hi, y), yz: 64 (over z_lo, x, core).
Axes of the slice: x: 4, y: 4, z: 16 (z_hi: 2, z_lo: 8; z = z_hi * 8 + z_lo), core: 2. Of those that a mesh axis runs over, the one named last changes fastest.
Arguments:
- adjoint: float32 [12, 64, 1024, 128], P(None, 'gx', 'yz'), may hold values from -6 to 6
- forward: float32 [12, 64, 1024, 128], P(None, 'gx', 'yz'), may hold values from -6 to 6
- coarse_model: float32 [8, 67, 7], P('gx'), may hold values from 0.5 to 1.5
- knot_span: int32 [1024], P('yz'), may hold values from 0 to 63, never falling along the last dimension, each value on 1 to 32 neighbouring positions
- knot_frac: float32 [1024], P('yz'), may hold values from 0 to 1
- dof_cell: int32 [4096], replicated, may hold values from 0 to 65535, as said below
- impedance: float32 [64, 4096], P(None, 'yz'), may hold values from -0.75 to 0.75
- history: float32 [63, 4096], P(None, 'yz'), may hold values from -6 to 6
- plate: bfloat16 [4096, 4096], P('yz'), may hold values from -0.09375 to 0.09375
- coupling: float32 [12, 12], replicated, may hold values from -1.5 to 1.5
- damping: float32 [12], replicated, may hold values from 0.05 to 2
Outputs:
- updated: float32 [12, 64, 1024, 128], P(None, 'gx', 'yz')
- coarse_grad: float32 [8, 67, 7], P('gx')
- reaction: float32 [4096], P('yz')
The draws below stay inside these ranges and needn't reach their ends.
Inputs may be any that keep to these rules, and one draw needn't show every extreme that they name: `dof_cell`: distinct surface cells.
All inputs are finite; a program needn't handle non-finite values.
Results may differ from the reference program's by a relative error of at most 0.0025.
Values may be sent and summed in bfloat16 or wider, within the bound.
A program may use at most 64 MiB of HBM per device.

```python
import math
import jax
import jax.numpy as jnp
import numpy as np
from jax import lax

NCOMP = 12
F = 4096
TAPS = 64
HZ = 32
CX = 8
CY = 16
NZ = 128
NX = 64
NY = 1024
KY = 67
KZ = 7
N_GX = 8
N_YZ = 64


def draw_dof_cell(key, part):
    key = jax.random.fold_in(key, 7)
    return jax.random.permutation(key, NX * NY)[:F].astype(jnp.int32)


def shard_levels(stream_key, extent, split, low, largest):
    gain, own = 1.0, jax.random.fold_in(stream_key, 6)
    for position, blocks in split:
        draws = jnp.exp(jax.random.uniform(jax.random.fold_in(own, position), (blocks,), jnp.float32, low / len(split), largest / len(split)))
        gain = gain * jnp.repeat(draws, extent[position] // blocks).reshape([-1 if axis == position else 1 for axis in range(len(extent))])
    return gain


def split_up(amount, total, reach, lean):
    weights = [(1 << 20) // math.isqrt(standing ** lean) + 1 for standing in range(2, amount + 1)]
    surplus, given = total - reach - (amount - 1), [1] * (amount - 1)
    while surplus > 0:
        movable = [i for i in range(amount - 1) if given[i] < reach]
        pool, remaining = sum([weights[i] for i in movable]), surplus
        for i in movable:
            more = min(reach - given[i], max(1, remaining * weights[i] // pool), surplus)
            given[i] = given[i] + more
            surplus = surplus - more
    return np.array([reach] + given)


def ragged_sizes(key, number_of, total, most, slope):
    if number_of == 2:
        one = jax.random.randint(key, (), max(1, total - most), min(most, total - 1) + 1)
        return jnp.stack([one, total - one])
    sizes = jnp.asarray(split_up(number_of, total, most, slope), jnp.int32)
    pairs = (number_of - 1) // 2
    source_of, sink = sizes[1:1 + 2 * pairs:2], sizes[2:2 + 2 * pairs:2]
    margin = jnp.minimum(source_of - 1, most - sink)
    passed = jax.random.randint(jax.random.fold_in(key, 1), (pairs,), 0, 1 << 20) % (margin + 1)
    sizes = sizes.at[1:1 + 2 * pairs:2].set(source_of - passed).at[2:2 + 2 * pairs:2].set(sink + passed)
    return sizes[jax.random.permutation(jax.random.fold_in(key, 2), number_of)]


def scatter_about(key, dims, spread, limit, split=(), held_as=jnp.bfloat16):
    level = shard_levels(key, dims, split, -0.22, 0.18) if split else 1.0
    values = jax.random.normal(key, dims, jnp.float32) * spread * level
    return jnp.minimum(jnp.maximum(values, -limit), limit).astype(held_as)


def setup_inputs(seed: int = 0) -> dict:
    key_of = jax.random.split(jax.random.key(seed), 12)
    adjoint = scatter_about(key_of[0], (NCOMP, NX, NY, NZ), 1.0, 6.0, ((1, 8), (2, 64)), jnp.float32)
    forward = scatter_about(key_of[1], (NCOMP, NX, NY, NZ), 1.0, 6.0, ((1, 8), (2, 64)), jnp.float32)
    coarse_model = jnp.clip(0.5 + 1.0 * jax.random.uniform(key_of[2], (N_GX, KY, KZ), jnp.float32) ** shard_levels(key_of[2], (N_GX, KY, KZ), ((0, 8),), -0.2, 0.2), 0.5, 1.5)
    knot_span = jnp.searchsorted(jnp.cumsum(ragged_sizes(key_of[3], N_YZ, NY, 2 * CY, 0)), jnp.arange(NY), side="right").astype(jnp.int32)
    knot_frac = jnp.clip(1.0 * jax.random.uniform(key_of[4], (NY,), jnp.float32) ** shard_levels(key_of[4], (NY,), ((0, 64),), -0.2, 0.2), 0.0, 1.0)
    dof_cell = draw_dof_cell(jax.random.fold_in(key_of[11], 71), 0)
    impedance = scatter_about(key_of[6], (TAPS, F), TAPS ** -0.5, 0.75, ((1, 64),), jnp.float32)
    history = scatter_about(key_of[7], (TAPS - 1, F), 1.0, 6.0, ((1, 64),), jnp.float32)
    plate = scatter_about(key_of[8], (F, F), F ** -0.5, 0.09375, ((0, 64),))
    coupling = scatter_about(key_of[9], (NCOMP, NCOMP), 0.3, 1.5, (), jnp.float32)
    damping = jnp.clip(jnp.exp(jax.random.uniform(key_of[10], (NCOMP,), jnp.float32, math.log(0.05), math.log(2.0))), 0.05, 2.0)
    return {"adjoint": adjoint, "forward": forward, "coarse_model": coarse_model, "knot_span": knot_span, "knot_frac": knot_frac, "dof_cell": dof_cell, "impedance": impedance, "history": history, "plate": plate, "coupling": coupling, "damping": damping}


time_step = 0.1
surface_gain = 40.0
grad_norm = 20.0


def laplacian(field):
    padded = jnp.pad(field, ((0, 0), (1, 1), (1, 1), (1, 1)))
    result = padded[:, 2:, 1:-1, 1:-1] + padded[:, :-2, 1:-1, 1:-1]
    result = result + padded[:, 1:-1, 2:, 1:-1] + padded[:, 1:-1, :-2, 1:-1]
    result = result + padded[:, 1:-1, 1:-1, 2:] + padded[:, 1:-1, 1:-1, :-2]
    return result - 6.0 * field


def bspline_weights(param):
    inverse = 1.0 - param
    return (inverse ** 3 / 6.0, (3.0 * param ** 3 - 6.0 * param ** 2 + 4.0) / 6.0,
            (-3.0 * param ** 3 + 3.0 * param ** 2 + 3.0 * param + 1.0) / 6.0, param ** 3 / 6.0)


def basis_rows(span, param, count):
    columns = jnp.arange(count, dtype=jnp.int32)[None, :]
    table = jnp.zeros((span.shape[0], count), jnp.float32)
    for shift_index, weight in enumerate(bspline_weights(param)):
        table = table + jnp.where(columns == span[:, None] + shift_index, weight[:, None], 0.0)
    return table


def depth_rows(depth, count):
    positions = jnp.arange(depth, dtype=jnp.int32)
    span = positions // HZ
    param = (positions.astype(jnp.float32) + 0.5) / HZ - span.astype(jnp.float32)
    return basis_rows(span, param, count)


def reference(adjoint, forward, coarse_model, knot_span, knot_frac, dof_cell, impedance, history, plate, coupling, damping):
    high = lax.Precision.HIGHEST
    lap_adj = laplacian(adjoint)
    lap_fwd = laplacian(forward)
    weights_y = basis_rows(knot_span, knot_frac, KY)
    weights_z = depth_rows(NZ, KZ)
    material = jnp.einsum("yi,gij,zj->gyz", weights_y, coarse_model, weights_z, precision=high)
    material = jnp.repeat(material, CX, axis=0)
    sample = adjoint[2, :, :, 0].reshape(-1)[dof_cell]
    impulse = impedance[0] * sample + jnp.sum(impedance[1:] * history, axis=0)
    reaction = impulse + jnp.dot(plate, impulse.astype(jnp.bfloat16), preferred_element_type=jnp.float32)
    forcing = jnp.zeros((NX * NY,), jnp.float32).at[dof_cell].add(reaction).reshape(NX, NY)
    coupled = jnp.einsum("cd,dxyz->cxyz", coupling, lap_adj, precision=high)
    tendency = material[None] * (lap_adj + coupled) - damping[:, None, None, None] * adjoint
    updated = adjoint + time_step * tendency
    updated = updated.at[2, :, :, 0].add(time_step * surface_gain * forcing)
    correlation = jnp.sum(adjoint * lap_fwd, axis=0).reshape(N_GX, CX, NY, NZ).sum(1)
    coarse_grad = jnp.einsum("yi,gyz,zj->gij", weights_y, correlation, weights_z, precision=high)
    coarse_grad = coarse_grad / (grad_norm * (CX * CY * HZ) ** 0.5)
    return updated, coarse_grad, reaction
```

```python
import functools

import jax
import jax.numpy as jnp
from jax import lax
from jax.experimental import pallas as pl
from jax.experimental.pallas import tpu as pltpu
from jax.sharding import PartitionSpec as P

MESH = pl.DeviceIdType.MESH
F32 = jnp.float32
BF16 = jnp.bfloat16
HIGH = lax.Precision.HIGHEST

HZ = 32
time_step = 0.1
surface_gain = 40.0
grad_norm = 20.0

Z_OFFSETS = tuple(sorted(range(-7, 9), key=lambda d: -abs(d)))
NEAR_OFFSETS = tuple(sorted(range(-4, 4), key=lambda d: -abs(d)))
RING_OFFSETS = (2, 1, 3, 0)


def bspline_weights(param):
    inverse = 1.0 - param
    return (
        inverse**3 / 6.0,
        (3.0 * param**3 - 6.0 * param**2 + 4.0) / 6.0,
        (-3.0 * param**3 + 3.0 * param**2 + 3.0 * param + 1.0) / 6.0,
        param**3 / 6.0,
    )


def spread_basis(index, span, param):
    total = 0.0
    for shift, weight in enumerate(bspline_weights(param)):
        total = total + jnp.where(index == span + shift, weight, 0.0)
    return total


def iota(shape, dim):
    return lax.broadcasted_iota(jnp.int32, shape, dim)


def split(values):
    head = values.astype(BF16)
    return head, (values - head.astype(F32)).astype(BF16)


def device_at(z, y, x, c):
    return (lax.div(z, 8) * 4 + y, lax.rem(z, 8) * 8 + x * 2 + c)


def wrap(value, count):
    return lax.rem(value + 2 * count, count)


def kernel(
    adjoint, forward, coarse, span, frac, dof, impedance, history, plate, coupling, damping,
    updated, grad, reaction,
    adj, fwd, upd, plt_buf, cols, surf, taps, taps_all, picked, picked_mate, taps_mate, impulse, one_hot, row_of, react,
    y_out, y_in, corr, x_out, x_in, grad_c, grad_x, grad_z,
    load_sems, send_sems, recv_sems,
):
    gx, yz = lax.axis_index("gx"), lax.axis_index("yz")
    z_hi, y = lax.div(gx, 4), lax.rem(gx, 4)
    z_lo, x, c = lax.div(yz, 8), lax.rem(lax.div(yz, 2), 4), lax.rem(yz, 2)
    z = z_hi * 8 + z_lo
    yx = y * 4 + x
    comps = adj.shape[0]
    has_prev, has_next = gx > 0, gx < 7
    has_left, has_right = yz > 0, yz < 63

    barrier = pltpu.get_barrier_semaphore()

    def greet(device):
        pl.semaphore_signal(barrier, inc=1, device_id=device, device_id_type=MESH)

    greeted = 0
    for d in Z_OFFSETS:
        if abs(d) > 4:
            greet(device_at(wrap(z + d, 16), y, x, c))
            greeted += 1
    for dz in (-4, 4, -3, 3, -2, 2, -1, 1, 0):
        for dx in RING_OFFSETS:
            for dc in (1, 0):
                if (dz, dx, dc) != (0, 0, 0):
                    greet(device_at(wrap(z + dz, 16), y, wrap(x + dx, 4), wrap(c + dc, 2)))
                    greeted += 1
    for dy in (2, 1, 3):
        for dx in RING_OFFSETS:
            greet(device_at(z, wrap(y + dy, 4), wrap(x + dx, 4), c))
            greeted += 1
    jump_up = jnp.logical_and(z_hi == 0, y == 3)
    jump_down = jnp.logical_and(z_hi == 1, y == 0)

    @pl.when(jump_up)
    def _():
        greet((gx + 1, yz))

    @pl.when(jump_down)
    def _():
        greet((gx - 1, yz))

    loads = [
        pltpu.make_async_copy(adjoint.at[2], adj.at[2, pl.ds(1, 8)], load_sems.at[0]),
        pltpu.make_async_copy(adjoint.at[pl.ds(0, 2)], adj.at[pl.ds(0, 2), pl.ds(1, 8)], load_sems.at[1]),
        pltpu.make_async_copy(adjoint.at[pl.ds(3, 9)], adj.at[pl.ds(3, 9), pl.ds(1, 8)], load_sems.at[2]),
        pltpu.make_async_copy(forward, fwd.at[:, pl.ds(1, 8)], load_sems.at[3]),
        pltpu.make_async_copy(plate, plt_buf, load_sems.at[4]),
    ]
    for load in loads:
        load.start()

    tail = jnp.sum(impedance[1:, :] * history[...], axis=0, keepdims=True)
    cols[z, 1:2, :] = jnp.concatenate([impedance[0:1, :], tail], axis=1)
    loads[0].wait()
    surface = adj[2, 1:9].reshape(128, 128)
    cols[z, 0:1, :] = jnp.transpose(surface)[0:1, :]

    pl.semaphore_wait(barrier, greeted + jnp.logical_or(jump_up, jump_down).astype(jnp.int32))

    def remote(src, dst, sem, device):
        return pltpu.make_async_remote_copy(
            src_ref=src, dst_ref=dst, send_sem=send_sems.at[sem], recv_sem=recv_sems.at[sem], device_id=device, device_id_type=MESH
        )

    def arrived(ref, sem):
        pltpu.make_async_copy(ref, ref, recv_sems.at[sem]).wait()

    def sent(ref, sem):
        pltpu.make_async_copy(ref, ref, send_sems.at[sem]).wait()

    for d in Z_OFFSETS:
        if d:
            remote(cols.at[z], cols.at[z], 0, device_at(wrap(z + d, 16), y, x, c)).start()

    for load in loads[1:]:
        load.wait()
    to_prev = remote(adj.at[:, 1], adj.at[:, 9], 1, (lax.max(gx - 1, 0), yz))
    to_next = remote(adj.at[:, 8], adj.at[:, 0], 2, (lax.min(gx + 1, 7), yz))

    @pl.when(has_prev)
    def _():
        to_prev.start()

    @pl.when(has_next)
    def _():
        to_next.start()

    plane = jnp.zeros((16, 128), F32)
    for k in range(comps):
        fwd[k, 0] = plane
        fwd[k, 9] = plane

    @pl.when(gx == 0)
    def _():
        for k in range(comps):
            adj[k, 0] = plane
        x_in[0] = plane

    @pl.when(gx == 7)
    def _():
        for k in range(comps):
            adj[k, 9] = plane
        x_in[1] = plane

    diagonal = iota((16, 16), 0) == iota((16, 16), 1)
    span_col = jnp.sum(jnp.where(diagonal, span[...], 0), axis=1, keepdims=True)
    frac_col = jnp.sum(jnp.where(diagonal, frac[...], 0.0), axis=1, keepdims=True)
    weights_y = spread_basis(iota((16, 128), 1), span_col, frac_col)
    depth = iota((8, 128), 1)
    depth_span = lax.div(depth, HZ)
    weights_z = spread_basis(iota((8, 128), 0), depth_span, (depth.astype(F32) + 0.5) / HZ - depth_span.astype(F32))

    for side, row in ((0, 0), (1, 15)):
        for k in range(comps):
            y_out[side, k] = adj[k, 1:9, row, :]
        y_out[side, comps] = jnp.broadcast_to(weights_y[row : row + 1, :], (8, 128))
    to_left = remote(y_out.at[0], y_in.at[1], 3, (gx, lax.max(yz - 1, 0)))
    to_right = remote(y_out.at[1], y_in.at[0], 4, (gx, lax.min(yz + 1, 63)))

    @pl.when(has_left)
    def _():
        to_left.start()

    @pl.when(has_right)
    def _():
        to_right.start()

    @pl.when(yz == 0)
    def _():
        y_in[0] = jnp.zeros_like(y_in[0])

    @pl.when(yz == 63)
    def _():
        y_in[1] = jnp.zeros_like(y_in[1])

    cell = dof[...]
    cell_x, cell_y = lax.shift_right_logical(cell, 10), lax.bitwise_and(cell, 1023)
    lane = lax.bitwise_and(cell_x, 7) * 16 + lax.bitwise_and(cell_y, 15)
    cell_gx, cell_yz = lax.shift_right_logical(cell_x, 3), lax.shift_right_logical(cell_y, 4)
    cell_row = (
        lax.bitwise_and(cell_gx, 3) * 64
        + lax.bitwise_and(lax.shift_right_logical(cell_yz, 1), 3) * 16
        + lax.shift_right_logical(cell_gx, 2) * 8
        + lax.shift_right_logical(cell_yz, 3)
    )
    row_of[...] = jnp.where(lax.bitwise_and(cell_yz, 1) == c, cell_row, -1)
    for tile in range(16):
        pattern = (iota((128, 256), 0) == lane[:, tile * 256 : tile * 256 + 256]).astype(F32).astype(BF16)
        one_hot[0:128, tile * 256 : tile * 256 + 256] = pattern
        one_hot[128:256, tile * 256 : tile * 256 + 256] = pattern

    cell_rank = iota((128, 1), 0)
    cell_id = (gx * 8 + lax.shift_right_logical(cell_rank, 4)) * 1024 + yz * 16 + lax.bitwise_and(cell_rank, 15)
    found = jnp.zeros((128, 128), F32)
    for tile in range(32):
        label = (iota((1, 128), 1) + (tile * 128 + 1)).astype(F32)
        found = found + jnp.where(cell[:, tile * 128 : tile * 128 + 128] == cell_id, label, 0.0)
    owner = jnp.sum(found, axis=1, keepdims=True).astype(jnp.int32) - 1
    owner_row = lax.shift_right_arithmetic(owner, 6)
    owner_lane = lax.bitwise_and(owner, 127)
    pick_row = (lax.bitwise_and(iota((128, 128), 1), 63) == owner_row).astype(F32).astype(BF16)

    arrived(cols.at[pl.ds(0, 15)], 0)
    surf[yx] = cols[:, 0, :]
    taps_own = cols[0:8, 1, :]
    for k in range(8):
        taps[k, x] = taps_own[k : k + 1, :]
    for dy in RING_OFFSETS:
        for dx in RING_OFFSETS:
            if (dy, dx) != (0, 0):
                remote(surf.at[yx], surf.at[yx], 5, device_at(z, wrap(y + dy, 4), wrap(x + dx, 4), c)).start()
    for dx in (2, 1, 3):
        remote(taps.at[:, x], taps.at[:, x], 6, device_at(z, y, wrap(x + dx, 4), c)).start()

    z_first, z_last = iota((16, 128), 1) == 0, iota((16, 128), 1) == 127
    y_first, y_last = iota((16, 128), 0) == 0, iota((16, 128), 0) == 15

    def laplacian(field, k, i, left, right):
        value = field[k, i]
        total = field[k, i - 1] + field[k, i + 1]
        total = total + jnp.where(z_first, 0.0, pltpu.roll(value, 1, 1)) + jnp.where(z_last, 0.0, pltpu.roll(value, 127, 1))
        total = total + jnp.where(y_first, left, pltpu.roll(value, 1, 0)) + jnp.where(y_last, right, pltpu.roll(value, 15, 0))
        return total - 6.0 * value, value

    def correlate(i, carry):
        for k in range(comps):
            lap, _ = laplacian(fwd, k, i, 0.0, 0.0)
            carry = carry + adj[k, i] * lap
        return carry

    corr[0:16, :] = lax.fori_loop(1, 9, correlate, jnp.zeros((16, 128), F32))

    arrived(taps.at[:, pl.ds(0, 3)], 6)
    for k in range(32):
        taps_all[k : k + 1, :] = taps[k // 4, k % 4]
    mate = (gx, yz + 1 - 2 * c)
    to_mate = remote(taps_all, taps_mate, 7, mate)
    to_mate.start()

    arrived(surf.at[pl.ds(0, 15)], 5)
    head, rest = split(surf[...].reshape(256, 128))
    samples = jnp.concatenate([head, rest], axis=1)
    for tile in range(16):
        lanes = slice(tile * 256, tile * 256 + 256)
        match = jnp.dot(samples, one_hot[:, lanes], preferred_element_type=F32)
        mine = jnp.sum(jnp.where(iota((256, 256), 0) == row_of[:, lanes], match, 0.0), axis=0, keepdims=True)
        picked[2 * tile : 2 * tile + 1, :] = mine[:, 0:128]
        picked[2 * tile + 1 : 2 * tile + 2, :] = mine[:, 128:256]
    picks = remote(picked, picked_mate, 8, mate)
    picks.start()
    to_mate.wait()
    first, second = jnp.where(c == 0, taps_all[...], taps_mate[...]), jnp.where(c == 0, taps_mate[...], taps_all[...])
    low_half = iota((32, 128), 1) < 64
    weight = jnp.where(low_half, first, pltpu.roll(second, 64, 1))
    tails = jnp.where(low_half, pltpu.roll(first, 64, 1), second)
    picks.wait()
    impulse[...] = weight * (picked[...] + picked_mate[...]) + tails

    flat = jnp.concatenate([impulse[k : k + 1, :] for k in range(32)], axis=1).astype(BF16)
    through = lax.dot_general(flat, plt_buf[...], (((1,), (1,)), ((), ())), preferred_element_type=F32)
    through = jnp.concatenate([through, through], axis=1)
    own_half = lax.div(iota((1, 128), 1), 64) == c
    own_row = jnp.where(own_half, through + impulse[pl.ds(lax.div(yz, 2), 1), :], 0.0)
    react[yz] = own_row
    for dz in NEAR_OFFSETS:
        for dx in RING_OFFSETS:
            for dc in (1, 0):
                if (dz, dx, dc) != (0, 0, 0):
                    target = device_at(wrap(z - dz, 16), y, wrap(x + dx, 4), wrap(c + dc, 2))
                    remote(react.at[yz], react.at[yz], 9, target).start()
    reaction[...] = jnp.where(c == 0, own_row[:, 0:64], own_row[:, 64:128])

    @pl.when(has_prev)
    def _():
        arrived(adj.at[:, 0], 2)

    @pl.when(has_next)
    def _():
        arrived(adj.at[:, 9], 1)

    for side, i in ((0, 0), (1, 9)):
        face = jnp.zeros((16, 128), F32)
        for k in range(comps):
            face = face + adj[k, i] * fwd[k, 1 if side == 0 else 8]
        x_out[side] = face
    back_prev = remote(x_out.at[0], x_in.at[1], 10, (lax.max(gx - 1, 0), yz))
    back_next = remote(x_out.at[1], x_in.at[0], 11, (lax.min(gx + 1, 7), yz))

    @pl.when(has_prev)
    def _():
        back_prev.start()

    @pl.when(has_next)
    def _():
        back_next.start()

    @pl.when(has_left)
    def _():
        arrived(y_in.at[0], 4)

    @pl.when(has_right)
    def _():
        arrived(y_in.at[1], 3)

    corr[16:24, :] = jnp.zeros((8, 128), F32)
    for side, row in ((0, 0), (1, 15)):
        edge = jnp.zeros((8, 128), F32)
        for k in range(comps):
            edge = edge + y_in[side, k] * fwd[k, 1:9, row, :]
        corr[16 + side : 17 + side, :] = jnp.sum(edge, axis=0, keepdims=True)

    knots = lax.dot_general(weights_y, coarse[...], (((1,), (1,)), ((), ())), precision=HIGH, preferred_element_type=F32)
    material = time_step * jnp.dot(knots, weights_z, precision=HIGH, preferred_element_type=F32)

    def update(i, _):
        laps = []
        for k in range(comps):
            lap, _ = laplacian(adj, k, i, y_in[0, k, pl.ds(i - 1, 1), :], y_in[1, k, pl.ds(i - 1, 1), :])
            laps.append(lap)
        for k in range(comps):
            mixed = laps[k]
            for m in range(comps):
                mixed = mixed + coupling[k, m] * laps[m]
            value = adj[k, i]
            upd[k, i - 1] = value + material * mixed - (time_step * damping[0, k]) * value
        return 0

    lax.fori_loop(1, 9, update, 0)
    stores = [
        pltpu.make_async_copy(upd.at[pl.ds(0, 2)], updated.at[pl.ds(0, 2)], load_sems.at[5]),
        pltpu.make_async_copy(upd.at[pl.ds(3, 9)], updated.at[pl.ds(3, 9)], load_sems.at[6]),
        pltpu.make_async_copy(upd.at[2], updated.at[2], load_sems.at[7]),
    ]
    stores[0].start()
    stores[1].start()

    arrived(react.at[pl.ds(0, 63)], 9)
    head, rest = split(react[...].reshape(64, 128))
    forces = jnp.dot(pick_row, jnp.concatenate([head, rest], axis=0), preferred_element_type=F32)
    forces = jnp.sum(jnp.where(iota((128, 128), 1) == owner_lane, forces, 0.0), axis=1, keepdims=True)
    forces = (time_step * surface_gain) * forces.reshape(8, 16, 1)
    upd[2] = upd[2] + jnp.where(iota((8, 16, 128), 2) == 0, forces, 0.0)
    stores[2].start()

    @pl.when(has_prev)
    def _():
        arrived(x_in.at[0], 11)

    @pl.when(has_next)
    def _():
        arrived(x_in.at[1], 10)

    corr[0:16, :] = corr[0:16, :] + x_in[0] + x_in[1]
    rows = jnp.concatenate([weights_y, y_in[0, comps, 0:1, :], y_in[1, comps, 0:1, :], jnp.zeros((6, 128), F32)], axis=0)
    part = lax.dot_general(weights_z, corr[...], (((1,), (1,)), ((), ())), precision=HIGH, preferred_element_type=F32)
    grad_c[0] = jnp.dot(part, rows, precision=HIGH, preferred_element_type=F32)
    cores = remote(grad_c.at[0], grad_c.at[1], 12, mate)
    cores.start()
    cores.wait()
    grad_x[x] = grad_c[0] + grad_c[1]
    for dx in (2, 1, 3):
        remote(grad_x.at[x], grad_x.at[x], 13, device_at(z, y, wrap(x + dx, 4), c)).start()
    arrived(grad_x.at[pl.ds(0, 3)], 13)
    grad_z[z_lo] = (grad_x[0] + grad_x[1]) + (grad_x[2] + grad_x[3])
    for d in range(1, 8):
        remote(grad_z.at[z_lo], grad_z.at[z_lo], 14, (gx, lax.rem(z_lo + d, 8) * 8 + x * 2 + c)).start()
    arrived(grad_z.at[pl.ds(0, 7)], 14)
    total = grad_z[0]
    for k in range(1, 8):
        total = total + grad_z[k]
    grad[...] = total / (grad_norm * 4096.0**0.5)

    sent(cols.at[pl.ds(0, 15)], 0)
    sent(surf.at[pl.ds(0, 15)], 5)
    sent(taps.at[:, pl.ds(0, 3)], 6)
    sent(react.at[pl.ds(0, 63)], 9)
    sent(grad_x.at[pl.ds(0, 3)], 13)
    sent(grad_z.at[pl.ds(0, 7)], 14)

    @pl.when(has_prev)
    def _():
        to_prev.wait_send()
        back_prev.wait_send()

    @pl.when(has_next)
    def _():
        to_next.wait_send()
        back_next.wait_send()

    @pl.when(has_left)
    def _():
        to_left.wait_send()

    @pl.when(has_right)
    def _():
        to_right.wait_send()

    for store in stores:
        store.wait()


def on_device(adjoint, forward, coarse_model, knot_span, knot_frac, dof_cell, impedance, history, plate, coupling, damping):
    comps, cells_x, cells_y, depth = adjoint.shape
    knots_y, knots_z = coarse_model.shape[1:]
    coarse = jnp.pad(coarse_model[0].T, ((0, 8 - knots_z), (0, 128 - knots_y)))
    vmem = pl.BlockSpec(memory_space=pltpu.VMEM)
    smem = pl.BlockSpec(memory_space=pltpu.SMEM)
    hbm = pl.BlockSpec(memory_space=pl.ANY)
    updated, grad, reaction = pl.pallas_call(
        kernel,
        out_shape=(
            jax.ShapeDtypeStruct(adjoint.shape, F32),
            jax.ShapeDtypeStruct((8, 128), F32),
            jax.ShapeDtypeStruct((1, 64), F32),
        ),
        in_specs=[hbm, hbm, vmem, vmem, vmem, vmem, vmem, vmem, hbm, smem, smem],
        out_specs=(hbm, vmem, vmem),
        scratch_shapes=[
            pltpu.VMEM((comps, cells_x + 2, cells_y, depth), F32),
            pltpu.VMEM((comps, cells_x + 2, cells_y, depth), F32),
            pltpu.VMEM(adjoint.shape, F32),
            pltpu.VMEM(plate.shape, BF16),
            pltpu.VMEM((16, 2, 128), F32),
            pltpu.VMEM((16, 16, 128), F32),
            pltpu.VMEM((8, 4, 1, 128), F32),
            pltpu.VMEM((32, 128), F32),
            pltpu.VMEM((32, 128), F32),
            pltpu.VMEM((32, 128), F32),
            pltpu.VMEM((32, 128), F32),
            pltpu.VMEM((32, 128), F32),
            pltpu.VMEM((256, 4096), BF16),
            pltpu.VMEM((1, 4096), jnp.int32),
            pltpu.VMEM((64, 1, 128), F32),
            pltpu.VMEM((2, comps + 1, 8, 128), F32),
            pltpu.VMEM((2, comps + 1, 8, 128), F32),
            pltpu.VMEM((24, 128), F32),
            pltpu.VMEM((2, 16, 128), F32),
            pltpu.VMEM((2, 16, 128), F32),
            pltpu.VMEM((2, 8, 128), F32),
            pltpu.VMEM((4, 8, 128), F32),
            pltpu.VMEM((8, 8, 128), F32),
            pltpu.SemaphoreType.DMA((8,)),
            pltpu.SemaphoreType.DMA((15,)),
            pltpu.SemaphoreType.DMA((15,)),
        ],
        compiler_params=pltpu.CompilerParams(collective_id=0, has_side_effects=True, vmem_limit_bytes=40 * 1024 * 1024),
        name="adjoint_step",
    )(
        adjoint, forward, coarse, knot_span.reshape(1, -1), knot_frac.reshape(1, -1), dof_cell.reshape(1, -1),
        impedance, history, plate, coupling, damping.reshape(1, -1),
    )
    return updated, grad[:knots_z, :knots_y].T[None], reaction.reshape(-1)


def solution(mesh):
    return jax.shard_map(
        on_device,
        mesh=mesh,
        in_specs=(
            P(None, "gx", "yz", None),
            P(None, "gx", "yz", None),
            P("gx", None, None),
            P("yz"),
            P("yz"),
            P(),
            P(None, "yz"),
            P(None, "yz"),
            P("yz", None),
            P(),
            P(),
        ),
        out_specs=(P(None, "gx", "yz", None), P("gx", None, None), P("yz")),
        check_vma=False,
    )
```

```python
import functools

import jax
import jax.numpy as jnp
from jax import lax
from jax.experimental import pallas as pl
from jax.experimental.pallas import tpu as pltpu
from jax.sharding import PartitionSpec as P

MESH = pl.DeviceIdType.MESH
F32 = jnp.float32
BF16 = jnp.bfloat16
HIGH = lax.Precision.HIGHEST

HZ = 32
VMEM_BYTES = 16 * 1024 * 1024
time_step = 0.1
surface_gain = 40.0
grad_norm = 20.0

NEAR_OFFSETS = tuple(sorted(range(-4, 4), key=lambda d: -abs(d)))
RING_OFFSETS = (2, 1, 3, 0)


def bspline_weights(param):
    inverse = 1.0 - param
    return (
        inverse**3 / 6.0,
        (3.0 * param**3 - 6.0 * param**2 + 4.0) / 6.0,
        (-3.0 * param**3 + 3.0 * param**2 + 3.0 * param + 1.0) / 6.0,
        param**3 / 6.0,
    )


def spread_basis(index, span, param):
    total = 0.0
    for shift, weight in enumerate(bspline_weights(param)):
        total = total + jnp.where(index == span + shift, weight, 0.0)
    return total


def iota(shape, dim):
    return lax.broadcasted_iota(jnp.int32, shape, dim)


def split(values):
    head = values.astype(BF16)
    return head, (values - head.astype(F32)).astype(BF16)


def device_at(z, y, x, c):
    return (lax.div(z, 8) * 4 + y, lax.rem(z, 8) * 8 + x * 2 + c)


def wrap(value, count):
    return lax.rem(value + 2 * count, count)


def kernel(
    adjoint, forward, coarse_hbm, span_hbm, frac_hbm, dof_hbm, impedance_hbm, history_hbm, plate, coupling_hbm, damping_hbm,
    updated, grad, reaction,
    coarse, span, frac, dof, impedance, history, coupling, damping,
    adj, fwd, plt_buf, cols, surf, taps, taps_all, picked, picked_mate, taps_mate, impulse, one_hot, row_of, react,
    y_out, y_in, corr, x_out, x_in, grad_c, grad_x, grad_z, face_adj, face_fwd, face_weights, weights_out,
    load_sems, send_sems, recv_sems, credit,
):
    gx, yz = lax.axis_index("gx"), lax.axis_index("yz")
    z_hi, y = lax.div(gx, 4), lax.rem(gx, 4)
    z_lo, x, c = lax.div(yz, 8), lax.rem(lax.div(yz, 2), 4), lax.rem(yz, 2)
    z = z_hi * 8 + z_lo
    yx = y * 4 + x
    comps = adj.shape[0]
    has_prev, has_next = gx > 0, gx < 7
    has_left, has_right = yz > 0, yz < 63
    mate = (gx, yz + 1 - 2 * c)

    upper, lower = jnp.logical_and(z_hi == 0, y == 3), jnp.logical_and(z_hi == 1, y == 0)
    jump = jnp.logical_or(upper, lower)
    near_prev, near_next = jnp.logical_and(has_prev, jnp.logical_not(lower)), jnp.logical_and(has_next, jnp.logical_not(upper))
    z_half = lax.rem(z_lo + 4, 8)
    half_way = device_at(z_hi * 8 + z_half, y, x, c)
    across = device_at((1 - z_hi) * 8 + z_half, 3 - y, x, c)

    barrier = pltpu.get_barrier_semaphore()

    def greet(device):
        pl.semaphore_signal(barrier, inc=1, device_id=device, device_id_type=MESH)

    greeted = 24 + has_left.astype(jnp.int32) + has_right.astype(jnp.int32) + jump.astype(jnp.int32)

    @pl.when(jump)
    def _():
        greet(across)

    for d in (4, -4, 3, -3, 2, -2, 1, -1):
        greet(device_at(wrap(z + d, 16), y, x, c))
    for dy in RING_OFFSETS:
        for dx in RING_OFFSETS:
            if (dy, dx) != (0, 0):
                greet(device_at(z, wrap(y + dy, 4), wrap(x + dx, 4), c))
    greet(mate)

    @pl.when(has_left)
    def _():
        greet((gx, yz - 1))

    @pl.when(has_right)
    def _():
        greet((gx, yz + 1))

    loads = [
        pltpu.make_async_copy(adjoint.at[2], adj.at[2, pl.ds(1, 8)], load_sems.at[0]),
        pltpu.make_async_copy(impedance_hbm, impedance, load_sems.at[8]),
        pltpu.make_async_copy(history_hbm, history, load_sems.at[9]),
        pltpu.make_async_copy(adjoint.at[pl.ds(0, 2)], adj.at[pl.ds(0, 2), pl.ds(1, 8)], load_sems.at[1]),
        pltpu.make_async_copy(adjoint.at[pl.ds(3, 9)], adj.at[pl.ds(3, 9), pl.ds(1, 8)], load_sems.at[2]),
        pltpu.make_async_copy(forward, fwd.at[:, pl.ds(1, 8)], load_sems.at[3]),
        pltpu.make_async_copy(plate, plt_buf, load_sems.at[4]),
        pltpu.make_async_copy(coarse_hbm, coarse, load_sems.at[10]),
        pltpu.make_async_copy(span_hbm, span, load_sems.at[11]),
        pltpu.make_async_copy(frac_hbm, frac, load_sems.at[12]),
        pltpu.make_async_copy(dof_hbm, dof, load_sems.at[13]),
        pltpu.make_async_copy(coupling_hbm, coupling, load_sems.at[14]),
        pltpu.make_async_copy(damping_hbm, damping, load_sems.at[15]),
    ]
    for load in loads:
        load.start()

    loads[1].wait()
    loads[2].wait()
    tail = jnp.sum(impedance[1:, :] * history[...], axis=0, keepdims=True)
    cols[z, 1:2, :] = jnp.concatenate([impedance[0:1, :], tail], axis=1)
    loads[0].wait()
    surface = adj[2, 1:9].reshape(128, 128)
    cols[z, 0:1, :] = jnp.transpose(surface)[0:1, :]

    pl.semaphore_wait(barrier, greeted)

    def remote(src, dst, sem, device):
        return pltpu.make_async_remote_copy(
            src_ref=src, dst_ref=dst, send_sem=send_sems.at[sem], recv_sem=recv_sems.at[sem], device_id=device, device_id_type=MESH
        )

    def arrived(ref, sem):
        pltpu.make_async_copy(ref, ref, recv_sems.at[sem]).wait()

    def sent(ref, sem):
        pltpu.make_async_copy(ref, ref, send_sems.at[sem]).wait()

    for d in (4, -4, 3, -3, 2, -2, 1, -1):
        remote(cols.at[z], cols.at[z], 0, device_at(wrap(z + d, 16), y, x, c)).start()

    @pl.when(jump)
    def _():
        pl.semaphore_signal(credit, inc=1, device_id=across, device_id_type=MESH)

    for load in loads[3:]:
        load.wait()
    to_prev = remote(adj.at[:, 1], adj.at[:, 9], 1, (lax.max(gx - 1, 0), yz))
    to_next = remote(adj.at[:, 8], adj.at[:, 0], 2, (lax.min(gx + 1, 7), yz))

    @pl.when(near_prev)
    def _():
        to_prev.start()

    @pl.when(near_next)
    def _():
        to_next.start()

    plane = jnp.zeros((16, 128), F32)
    for k in range(comps):
        fwd[k, 0] = plane
        fwd[k, 9] = plane

    @pl.when(gx == 0)
    def _():
        for k in range(comps):
            adj[k, 0] = plane

    @pl.when(gx == 7)
    def _():
        for k in range(comps):
            adj[k, 9] = plane

    @pl.when(jnp.logical_not(near_prev))
    def _():
        x_in[0] = plane

    @pl.when(jnp.logical_not(near_next))
    def _():
        x_in[1] = plane

    diagonal = iota((16, 16), 0) == iota((16, 16), 1)
    span_col = jnp.sum(jnp.where(diagonal, span[...], 0), axis=1, keepdims=True)
    frac_col = jnp.sum(jnp.where(diagonal, frac[...], 0.0), axis=1, keepdims=True)
    weights_y = spread_basis(iota((16, 128), 1), span_col, frac_col)
    depth = iota((8, 128), 1)
    depth_span = lax.div(depth, HZ)
    weights_z = spread_basis(iota((8, 128), 0), depth_span, (depth.astype(F32) + 0.5) / HZ - depth_span.astype(F32))

    weights_out[...] = weights_y
    for side, row in ((0, 0), (1, 15)):
        for k in range(comps):
            y_out[side, k] = adj[k, 1:9, row, :]
        y_out[side, comps] = jnp.broadcast_to(weights_y[row : row + 1, :], (8, 128))
    to_left = remote(y_out.at[0], y_in.at[1], 3, (gx, lax.max(yz - 1, 0)))
    to_right = remote(y_out.at[1], y_in.at[0], 4, (gx, lax.min(yz + 1, 63)))

    @pl.when(has_left)
    def _():
        to_left.start()

    @pl.when(has_right)
    def _():
        to_right.start()

    face = jnp.where(upper, 8, 1)
    face_copies = (
        remote(adj.at[:, face], face_adj, 15, half_way),
        remote(fwd.at[:, face], face_fwd, 16, across),
        remote(weights_out, face_weights, 17, half_way),
    )

    @pl.when(jump)
    def _():
        for copy in face_copies:
            copy.start()

    @pl.when(yz == 0)
    def _():
        y_in[0] = jnp.zeros_like(y_in[0])

    @pl.when(yz == 63)
    def _():
        y_in[1] = jnp.zeros_like(y_in[1])

    cell = dof[...]
    cell_x, cell_y = lax.shift_right_logical(cell, 10), lax.bitwise_and(cell, 1023)
    lane = lax.bitwise_and(cell_x, 7) * 16 + lax.bitwise_and(cell_y, 15)
    cell_gx, cell_yz = lax.shift_right_logical(cell_x, 3), lax.shift_right_logical(cell_y, 4)
    cell_row = (
        lax.bitwise_and(cell_gx, 3) * 64
        + lax.bitwise_and(lax.shift_right_logical(cell_yz, 1), 3) * 16
        + lax.shift_right_logical(cell_gx, 2) * 8
        + lax.shift_right_logical(cell_yz, 3)
    )
    row_of[...] = jnp.where(lax.bitwise_and(cell_yz, 1) == c, cell_row, -1)
    for tile in range(16):
        pattern = (iota((128, 256), 0) == lane[:, tile * 256 : tile * 256 + 256]).astype(F32).astype(BF16)
        one_hot[0:128, tile * 256 : tile * 256 + 256] = pattern
        one_hot[128:256, tile * 256 : tile * 256 + 256] = pattern

    cell_rank = iota((128, 1), 0)
    cell_id = (gx * 8 + lax.shift_right_logical(cell_rank, 4)) * 1024 + yz * 16 + lax.bitwise_and(cell_rank, 15)
    found = jnp.zeros((128, 128), F32)
    for tile in range(32):
        label = (iota((1, 128), 1) + (tile * 128 + 1)).astype(F32)
        found = found + jnp.where(cell[:, tile * 128 : tile * 128 + 128] == cell_id, label, 0.0)
    owner = jnp.sum(found, axis=1, keepdims=True).astype(jnp.int32) - 1
    owner_row = lax.shift_right_arithmetic(owner, 6)
    owner_lane = lax.bitwise_and(owner, 127)
    pick_row = (lax.bitwise_and(iota((128, 128), 1), 63) == owner_row).astype(F32).astype(BF16)

    arrived(cols.at[pl.ds(0, 8)], 0)
    for d in (4, 3, 2, 1):
        slot = wrap(z + d, 16)
        remote(cols.at[slot], cols.at[slot], 18, device_at(wrap(z - 4, 16), y, x, c)).start()
    for d in (-3, -2, -1):
        slot = wrap(z + d, 16)
        remote(cols.at[slot], cols.at[slot], 18, device_at(wrap(z + 4, 16), y, x, c)).start()

    @pl.when(jump)
    def _():
        pl.semaphore_wait(credit, 1)

    @pl.when(lower)
    def _():
        to_prev.start()

    @pl.when(upper)
    def _():
        to_next.start()

    z_first, z_last = iota((16, 128), 1) == 0, iota((16, 128), 1) == 127
    y_first, y_last = iota((16, 128), 0) == 0, iota((16, 128), 0) == 15

    def laplacian(field, k, i, left, right):
        value = field[k, i]
        total = field[k, i - 1] + field[k, i + 1]
        total = total + jnp.where(z_first, 0.0, pltpu.roll(value, 1, 1)) + jnp.where(z_last, 0.0, pltpu.roll(value, 127, 1))
        total = total + jnp.where(y_first, left, pltpu.roll(value, 1, 0)) + jnp.where(y_last, right, pltpu.roll(value, 15, 0))
        return total - 6.0 * value, value

    def correlate(i, carry):
        for k in range(comps):
            lap, _ = laplacian(fwd, k, i, 0.0, 0.0)
            carry = carry + adj[k, i] * lap
        return carry

    corr[0:16, :] = lax.fori_loop(1, 9, correlate, jnp.zeros((16, 128), F32))

    back_prev = remote(x_out.at[0], x_in.at[1], 10, (lax.max(gx - 1, 0), yz))
    back_next = remote(x_out.at[1], x_in.at[0], 11, (lax.min(gx + 1, 7), yz))

    def send_back(side, halo, sem, inner, copy):
        arrived(adj.at[:, halo], sem)
        product = plane
        for k in range(comps):
            product = product + adj[k, halo] * fwd[k, inner]
        x_out[side] = product
        copy.start()

    @pl.when(near_prev)
    def _():
        send_back(0, 0, 2, 1, back_prev)

    @pl.when(near_next)
    def _():
        send_back(1, 9, 1, 8, back_next)

    arrived(cols.at[pl.ds(0, 7)], 18)
    surf[yx] = cols[:, 0, :]
    taps_own = cols[0:8, 1, :]
    for k in range(8):
        taps[k, x] = taps_own[k : k + 1, :]
    for dy in RING_OFFSETS:
        for dx in RING_OFFSETS:
            if (dy, dx) != (0, 0):
                remote(surf.at[yx], surf.at[yx], 5, device_at(z, wrap(y + dy, 4), wrap(x + dx, 4), c)).start()
    for dx in (2, 1, 3):
        remote(taps.at[:, x], taps.at[:, x], 6, device_at(z, y, wrap(x + dx, 4), c)).start()

    @pl.when(has_left)
    def _():
        arrived(y_in.at[0], 4)

    @pl.when(has_right)
    def _():
        arrived(y_in.at[1], 3)

    corr[16:24, :] = jnp.zeros((8, 128), F32)
    for side, row in ((0, 0), (1, 15)):
        edge = jnp.zeros((8, 128), F32)
        for k in range(comps):
            edge = edge + y_in[side, k] * fwd[k, 1:9, row, :]
        corr[16 + side : 17 + side, :] = jnp.sum(edge, axis=0, keepdims=True)

    knots_z, _, knots_y = coarse.shape
    material = jnp.zeros((16, 128), F32)
    for k in range(knots_z):
        knot = jnp.sum(weights_y[:, 0:knots_y] * coarse[k], axis=1, keepdims=True)
        material = material + knot * weights_z[k : k + 1, :]
    material = time_step * material

    def update(i):
        laps = []
        for k in range(comps):
            lap, _ = laplacian(adj, k, i, y_in[0, k, pl.ds(i - 1, 1), :], y_in[1, k, pl.ds(i - 1, 1), :])
            laps.append(lap)
        for k in range(comps):
            mixed = laps[k]
            for m in range(comps):
                mixed = mixed + coupling[k, m] * laps[m]
            value = adj[k, i]
            updated[k, i - 1] = value + material * mixed - (time_step * damping[0, k]) * value

    @pl.loop(2, 8)
    def _(i):
        update(i)

    arrived(taps.at[:, pl.ds(0, 3)], 6)
    for k in range(32):
        taps_all[k : k + 1, :] = taps[k // 4, k % 4]
    to_mate = remote(taps_all, taps_mate, 7, mate)
    to_mate.start()

    arrived(surf.at[pl.ds(0, 15)], 5)
    head, rest = split(surf[...].reshape(256, 128))
    samples = jnp.concatenate([head, rest], axis=1)
    for tile in range(16):
        lanes = slice(tile * 256, tile * 256 + 256)
        match = jnp.dot(samples, one_hot[:, lanes], preferred_element_type=F32)
        mine = jnp.sum(jnp.where(iota((256, 256), 0) == row_of[:, lanes], match, 0.0), axis=0, keepdims=True)
        picked[2 * tile : 2 * tile + 1, :] = mine[:, 0:128]
        picked[2 * tile + 1 : 2 * tile + 2, :] = mine[:, 128:256]
    picks = remote(picked, picked_mate, 8, mate)
    picks.start()

    @pl.when(near_prev)
    def _():
        arrived(x_in.at[0], 11)

    @pl.when(near_next)
    def _():
        arrived(x_in.at[1], 10)

    def project(cells, rows):
        part = lax.dot_general(weights_z, cells, (((1,), (1,)), ((), ())), precision=HIGH, preferred_element_type=F32)
        return jnp.dot(part, rows, precision=HIGH, preferred_element_type=F32)

    corr[0:16, :] = corr[0:16, :] + x_in[0] + x_in[1]
    rows = jnp.concatenate([weights_y, y_in[0, comps, 0:1, :], y_in[1, comps, 0:1, :], jnp.zeros((6, 128), F32)], axis=0)
    grad_c[0] = project(corr[...], rows)

    @pl.when(jump)
    def _():
        arrived(face_adj, 15)
        arrived(face_fwd, 16)
        arrived(face_weights, 17)
        product = plane
        for k in range(comps):
            product = product + face_adj[k] * face_fwd[k]
        grad_c[0] = grad_c[0] + project(product, face_weights[...])

    cores = remote(grad_c.at[0], grad_c.at[1], 12, mate)
    cores.start()

    to_mate.wait()
    first, second = jnp.where(c == 0, taps_all[...], taps_mate[...]), jnp.where(c == 0, taps_mate[...], taps_all[...])
    low_half = iota((32, 128), 1) < 64
    weight = jnp.where(low_half, first, pltpu.roll(second, 64, 1))
    tails = jnp.where(low_half, pltpu.roll(first, 64, 1), second)
    picks.wait()
    impulse[...] = weight * (picked[...] + picked_mate[...]) + tails

    flat = jnp.concatenate([impulse[k : k + 1, :] for k in range(32)], axis=1).astype(BF16)
    through = lax.dot_general(flat, plt_buf[...], (((1,), (1,)), ((), ())), preferred_element_type=F32)
    through = jnp.concatenate([through, through], axis=1)
    own_half = lax.div(iota((1, 128), 1), 64) == c
    own_row = jnp.where(own_half, through + impulse[pl.ds(lax.div(yz, 2), 1), :], 0.0)
    react[yz] = own_row
    for dz in NEAR_OFFSETS:
        for dx in RING_OFFSETS:
            for dc in (1, 0):
                if (dz, dx, dc) != (0, 0, 0):
                    target = device_at(wrap(z - dz, 16), y, wrap(x + dx, 4), wrap(c + dc, 2))
                    remote(react.at[yz], react.at[yz], 9, target).start()
    reaction[...] = jnp.where(c == 0, own_row[:, 0:64], own_row[:, 64:128])

    cores.wait()
    grad_x[x] = grad_c[0] + grad_c[1]
    for dx in (2, 1, 3):
        remote(grad_x.at[x], grad_x.at[x], 13, device_at(z, y, wrap(x + dx, 4), c)).start()
    arrived(grad_x.at[pl.ds(0, 3)], 13)
    grad_z[z_lo] = (grad_x[0] + grad_x[1]) + (grad_x[2] + grad_x[3])
    for d in (7, 6, 5, 4, 3, 2, 1):
        remote(grad_z.at[z_lo], grad_z.at[z_lo], 14, (gx, lax.rem(z_lo + d, 8) * 8 + x * 2 + c)).start()

    @pl.when(lower)
    def _():
        arrived(adj.at[:, 0], 2)

    @pl.when(upper)
    def _():
        arrived(adj.at[:, 9], 1)

    @pl.loop(0, 2)
    def _(side):
        update(1 + 7 * side)

    arrived(react.at[pl.ds(0, 63)], 9)
    head, rest = split(react[...].reshape(64, 128))
    forces = jnp.dot(pick_row, jnp.concatenate([head, rest], axis=0), preferred_element_type=F32)
    forces = jnp.sum(jnp.where(iota((128, 128), 1) == owner_lane, forces, 0.0), axis=1, keepdims=True)
    forces = (time_step * surface_gain) * forces.reshape(8, 16, 1)
    updated[2] = updated[2] + jnp.where(iota((8, 16, 128), 2) == 0, forces, 0.0)

    arrived(grad_z.at[pl.ds(0, 7)], 14)
    total = grad_z[0]
    for k in range(1, 8):
        total = total + grad_z[k]
    total = total / (grad_norm * 4096.0**0.5)
    for k in range(knots_z):
        grad[k] = total[k : k + 1, 0:knots_y]

    sent(cols.at[pl.ds(0, 8)], 0)
    sent(cols.at[pl.ds(0, 7)], 18)
    sent(surf.at[pl.ds(0, 15)], 5)
    sent(taps.at[:, pl.ds(0, 3)], 6)
    sent(react.at[pl.ds(0, 63)], 9)
    sent(grad_x.at[pl.ds(0, 3)], 13)
    sent(grad_z.at[pl.ds(0, 7)], 14)
    for present, copy in (
        (has_prev, to_prev), (has_next, to_next), (has_left, to_left), (has_right, to_right),
        (near_prev, back_prev), (near_next, back_next),
        (jump, face_copies[0]), (jump, face_copies[1]), (jump, face_copies[2]),
    ):
        pl.when(present)(copy.wait_send)


def store_results(*refs):
    count = len(refs) // 2
    copies = [pltpu.make_async_copy(refs[k], refs[count + k], refs[-1].at[k]) for k in range(count)]
    for copy in copies:
        copy.start()
    for copy in copies:
        copy.wait()


def on_device(adjoint, forward, coarse_model, knot_span, knot_frac, dof_cell, impedance, history, plate, coupling, damping):
    comps, cells_x, cells_y, depth = adjoint.shape
    knots_y, knots_z = coarse_model.shape[1:]
    vmem = pl.BlockSpec(memory_space=pltpu.VMEM)
    hbm = pl.BlockSpec(memory_space=pltpu.HBM)
    anywhere = pl.BlockSpec(memory_space=pl.ANY)
    updated, grad, reaction = pl.pallas_call(
        kernel,
        out_shape=(
            jax.ShapeDtypeStruct(adjoint.shape, F32),
            jax.ShapeDtypeStruct((knots_z, 1, knots_y), F32),
            jax.ShapeDtypeStruct((1, 64), F32),
        ),
        in_specs=[hbm] * 11,
        out_specs=(vmem, vmem, vmem),
        scratch_shapes=[
            pltpu.VMEM((knots_z, 1, knots_y), F32),
            pltpu.VMEM((1, cells_y), jnp.int32),
            pltpu.VMEM((1, cells_y), F32),
            pltpu.VMEM((1, dof_cell.size), jnp.int32),
            pltpu.VMEM(impedance.shape, F32),
            pltpu.VMEM(history.shape, F32),
            pltpu.SMEM(coupling.shape, F32),
            pltpu.SMEM((1, comps), F32),
            pltpu.VMEM((comps, cells_x + 2, cells_y, depth), F32),
            pltpu.VMEM((comps, cells_x + 2, cells_y, depth), F32),
            pltpu.VMEM(plate.shape, BF16),
            pltpu.VMEM((16, 2, 128), F32),
            pltpu.VMEM((16, 16, 128), F32),
            pltpu.VMEM((8, 4, 1, 128), F32),
            pltpu.VMEM((32, 128), F32),
            pltpu.VMEM((32, 128), F32),
            pltpu.VMEM((32, 128), F32),
            pltpu.VMEM((32, 128), F32),
            pltpu.VMEM((32, 128), F32),
            pltpu.VMEM((256, 4096), BF16),
            pltpu.VMEM((1, 4096), jnp.int32),
            pltpu.VMEM((64, 1, 128), F32),
            pltpu.VMEM((2, comps + 1, 8, 128), F32),
            pltpu.VMEM((2, comps + 1, 8, 128), F32),
            pltpu.VMEM((24, 128), F32),
            pltpu.VMEM((2, 16, 128), F32),
            pltpu.VMEM((2, 16, 128), F32),
            pltpu.VMEM((2, 8, 128), F32),
            pltpu.VMEM((4, 8, 128), F32),
            pltpu.VMEM((8, 8, 128), F32),
            pltpu.VMEM((comps, cells_y, depth), F32),
            pltpu.VMEM((comps, cells_y, depth), F32),
            pltpu.VMEM((cells_y, depth), F32),
            pltpu.VMEM((cells_y, depth), F32),
            pltpu.SemaphoreType.DMA((16,)),
            pltpu.SemaphoreType.DMA((19,)),
            pltpu.SemaphoreType.DMA((19,)),
            pltpu.SemaphoreType.REGULAR,
        ],
        compiler_params=pltpu.CompilerParams(collective_id=0, has_side_effects=True, vmem_limit_bytes=VMEM_BYTES),
        name="adjoint_step",
    )(
        *[
            pltpu.with_memory_space_constraint(operand, pltpu.HBM)
            for operand in (
                adjoint, forward, coarse_model.transpose(2, 0, 1), knot_span.reshape(1, -1), knot_frac.reshape(1, -1),
                dof_cell.reshape(1, -1), impedance, history, plate, coupling, damping.reshape(1, -1),
            )
        ]
    )
    results = (updated, grad, reaction)
    updated, grad, reaction = pl.pallas_call(
        store_results,
        out_shape=tuple(jax.ShapeDtypeStruct(a.shape, a.dtype) for a in results),
        in_specs=[anywhere] * 3,
        out_specs=(hbm,) * 3,
        scratch_shapes=[pltpu.SemaphoreType.DMA((3,))],
        name="store_results",
    )(*results)
    return updated, grad.transpose(1, 2, 0), reaction.reshape(-1)


def solution(mesh):
    return jax.shard_map(
        on_device,
        mesh=mesh,
        in_specs=(
            P(None, "gx", "yz", None),
            P(None, "gx", "yz", None),
            P("gx", None, None),
            P("yz"),
            P("yz"),
            P(),
            P(None, "yz"),
            P(None, "yz"),
            P("yz", None),
            P(),
            P(),
        ),
        out_specs=(P(None, "gx", "yz", None), P("gx", None, None), P("yz")),
        check_vma=False,
    )
```

```python
import functools

import jax
import jax.numpy as jnp
from jax import lax
from jax.experimental import pallas as pl
from jax.experimental.pallas import tpu as pltpu
from jax.sharding import PartitionSpec as P

MESH = pl.DeviceIdType.MESH
F32 = jnp.float32
BF16 = jnp.bfloat16
HIGH = lax.Precision.HIGHEST

HZ = 32
VMEM_BYTES = 16 * 1024 * 1024
time_step = 0.1
surface_gain = 40.0
grad_norm = 20.0

NEAR_OFFSETS = tuple(sorted(range(-4, 4), key=lambda d: -abs(d)))
RING_OFFSETS = (2, 1, 3, 0)


def bspline_weights(param):
    inverse = 1.0 - param
    return (
        inverse**3 / 6.0,
        (3.0 * param**3 - 6.0 * param**2 + 4.0) / 6.0,
        (-3.0 * param**3 + 3.0 * param**2 + 3.0 * param + 1.0) / 6.0,
        param**3 / 6.0,
    )


def spread_basis(index, span, param):
    total = 0.0
    for shift, weight in enumerate(bspline_weights(param)):
        total = total + jnp.where(index == span + shift, weight, 0.0)
    return total


def iota(shape, dim):
    return lax.broadcasted_iota(jnp.int32, shape, dim)


def split(values):
    head = values.astype(BF16)
    return head, (values - head.astype(F32)).astype(BF16)


def device_at(z, y, x, c):
    return (lax.div(z, 8) * 4 + y, lax.rem(z, 8) * 8 + x * 2 + c)


def wrap(value, count):
    return lax.rem(value + 2 * count, count)


def kernel(
    adjoint, forward, coarse_hbm, span_hbm, frac_hbm, dof_hbm, impedance_hbm, history_hbm, plate, coupling_hbm, damping_hbm,
    updated, grad, reaction,
    coarse, span, frac, dof, impedance, history, coupling, damping,
    adj, fwd, plt_buf, cols, surf, taps, taps_all, picked, picked_mate, taps_mate, impulse, one_hot, row_of, react,
    y_out, y_in, corr, x_out, x_in, grad_c, grad_x, grad_z, ring_in, far_in, grad_far,
    load_sems, send_sems, recv_sems, credit,
):
    gx, yz = lax.axis_index("gx"), lax.axis_index("yz")
    z_hi, y = lax.div(gx, 4), lax.rem(gx, 4)
    z_lo, x, c = lax.div(yz, 8), lax.rem(lax.div(yz, 2), 4), lax.rem(yz, 2)
    z = z_hi * 8 + z_lo
    yx = y * 4 + x
    comps = adj.shape[0]
    has_prev, has_next = gx > 0, gx < 7
    has_left, has_right = yz > 0, yz < 63
    mate = (gx, yz + 1 - 2 * c)

    upper, lower = jnp.logical_and(z_hi == 0, y == 3), jnp.logical_and(z_hi == 1, y == 0)
    jump = jnp.logical_or(upper, lower)
    near_prev, near_next = jnp.logical_and(has_prev, jnp.logical_not(lower)), jnp.logical_and(has_next, jnp.logical_not(upper))
    facing = device_at(wrap(z + 8, 16), y, x, c)

    barrier = pltpu.get_barrier_semaphore()

    def greet(device):
        pl.semaphore_signal(barrier, inc=1, device_id=device, device_id_type=MESH)

    greeted = 24 + has_left.astype(jnp.int32) + has_right.astype(jnp.int32)

    for d in (4, -4, 3, -3, 2, -2, 1, -1):
        greet(device_at(wrap(z + d, 16), y, x, c))
    for dy in RING_OFFSETS:
        for dx in RING_OFFSETS:
            if (dy, dx) != (0, 0):
                greet(device_at(z, wrap(y + dy, 4), wrap(x + dx, 4), c))
    greet(mate)

    @pl.when(has_left)
    def _():
        greet((gx, yz - 1))

    @pl.when(has_right)
    def _():
        greet((gx, yz + 1))

    loads = [
        pltpu.make_async_copy(adjoint.at[2], adj.at[2, pl.ds(1, 8)], load_sems.at[0]),
        pltpu.make_async_copy(impedance_hbm, impedance, load_sems.at[8]),
        pltpu.make_async_copy(history_hbm, history, load_sems.at[9]),
        pltpu.make_async_copy(adjoint.at[pl.ds(0, 2)], adj.at[pl.ds(0, 2), pl.ds(1, 8)], load_sems.at[1]),
        pltpu.make_async_copy(adjoint.at[pl.ds(3, 9)], adj.at[pl.ds(3, 9), pl.ds(1, 8)], load_sems.at[2]),
        pltpu.make_async_copy(forward, fwd.at[:, pl.ds(1, 8)], load_sems.at[3]),
        pltpu.make_async_copy(plate, plt_buf, load_sems.at[4]),
        pltpu.make_async_copy(coarse_hbm, coarse, load_sems.at[10]),
        pltpu.make_async_copy(span_hbm, span, load_sems.at[11]),
        pltpu.make_async_copy(frac_hbm, frac, load_sems.at[12]),
        pltpu.make_async_copy(dof_hbm, dof, load_sems.at[13]),
        pltpu.make_async_copy(coupling_hbm, coupling, load_sems.at[14]),
        pltpu.make_async_copy(damping_hbm, damping, load_sems.at[15]),
    ]
    for load in loads:
        load.start()

    loads[1].wait()
    loads[2].wait()
    tail = jnp.sum(impedance[1:, :] * history[...], axis=0, keepdims=True)
    cols[z, 1:2, :] = jnp.concatenate([impedance[0:1, :], tail], axis=1)
    loads[0].wait()
    surface = adj[2, 1:9].reshape(128, 128)
    cols[z, 0:1, :] = jnp.transpose(surface)[0:1, :]

    pl.semaphore_wait(barrier, greeted)

    def remote(src, dst, sem, device):
        return pltpu.make_async_remote_copy(
            src_ref=src, dst_ref=dst, send_sem=send_sems.at[sem], recv_sem=recv_sems.at[sem], device_id=device, device_id_type=MESH
        )

    def arrived(ref, sem):
        pltpu.make_async_copy(ref, ref, recv_sems.at[sem]).wait()

    def sent(ref, sem):
        pltpu.make_async_copy(ref, ref, send_sems.at[sem]).wait()

    for d in (4, -4, 3, -3, 2, -2, 1, -1):
        remote(cols.at[z], cols.at[z], 0, device_at(wrap(z + d, 16), y, x, c)).start()

    quarter = comps // 4
    for ring in range(4):
        part = pl.ds(ring * quarter, quarter)
        if ring != 3:
            pl.when(upper)(remote(adjoint.at[part, 7], ring_in, 15, (z_hi * 4 + ring, yz)).start)
        if ring != 0:
            pl.when(lower)(remote(adjoint.at[part, 0], ring_in, 15, (z_hi * 4 + ring, yz)).start)

    pl.semaphore_signal(credit, inc=1, device_id=device_at(wrap(z - 4, 16), y, x, c), device_id_type=MESH)

    for load in loads[3:]:
        load.wait()
    to_prev = remote(adj.at[:, 1], adj.at[:, 9], 1, (lax.max(gx - 1, 0), yz))
    to_next = remote(adj.at[:, 8], adj.at[:, 0], 2, (lax.min(gx + 1, 7), yz))

    @pl.when(near_prev)
    def _():
        to_prev.start()

    @pl.when(near_next)
    def _():
        to_next.start()

    plane = jnp.zeros((16, 128), F32)
    for k in range(comps):
        fwd[k, 0] = plane
        fwd[k, 9] = plane

    @pl.when(gx == 0)
    def _():
        for k in range(comps):
            adj[k, 0] = plane

    @pl.when(gx == 7)
    def _():
        for k in range(comps):
            adj[k, 9] = plane

    @pl.when(jnp.logical_not(near_prev))
    def _():
        x_in[0] = plane

    @pl.when(jnp.logical_not(near_next))
    def _():
        x_in[1] = plane

    diagonal = iota((16, 16), 0) == iota((16, 16), 1)
    span_col = jnp.sum(jnp.where(diagonal, span[...], 0), axis=1, keepdims=True)
    frac_col = jnp.sum(jnp.where(diagonal, frac[...], 0.0), axis=1, keepdims=True)
    weights_y = spread_basis(iota((16, 128), 1), span_col, frac_col)
    depth = iota((8, 128), 1)
    depth_span = lax.div(depth, HZ)
    weights_z = spread_basis(iota((8, 128), 0), depth_span, (depth.astype(F32) + 0.5) / HZ - depth_span.astype(F32))

    for side, row in ((0, 0), (1, 15)):
        for k in range(comps):
            y_out[side, k] = adj[k, 1:9, row, :]
        y_out[side, comps] = jnp.broadcast_to(weights_y[row : row + 1, :], (8, 128))
    to_left = remote(y_out.at[0], y_in.at[1], 3, (gx, lax.max(yz - 1, 0)))
    to_right = remote(y_out.at[1], y_in.at[0], 4, (gx, lax.min(yz + 1, 63)))

    @pl.when(has_left)
    def _():
        to_left.start()

    @pl.when(has_right)
    def _():
        to_right.start()

    @pl.when(yz == 0)
    def _():
        y_in[0] = jnp.zeros_like(y_in[0])

    @pl.when(yz == 63)
    def _():
        y_in[1] = jnp.zeros_like(y_in[1])

    cell = dof[...]
    cell_x, cell_y = lax.shift_right_logical(cell, 10), lax.bitwise_and(cell, 1023)
    lane = lax.bitwise_and(cell_x, 7) * 16 + lax.bitwise_and(cell_y, 15)
    cell_gx, cell_yz = lax.shift_right_logical(cell_x, 3), lax.shift_right_logical(cell_y, 4)
    cell_row = (
        lax.bitwise_and(cell_gx, 3) * 64
        + lax.bitwise_and(lax.shift_right_logical(cell_yz, 1), 3) * 16
        + lax.shift_right_logical(cell_gx, 2) * 8
        + lax.shift_right_logical(cell_yz, 3)
    )
    row_of[...] = jnp.where(lax.bitwise_and(cell_yz, 1) == c, cell_row, -1)
    for tile in range(16):
        pattern = (iota((128, 256), 0) == lane[:, tile * 256 : tile * 256 + 256]).astype(F32).astype(BF16)
        one_hot[0:128, tile * 256 : tile * 256 + 256] = pattern
        one_hot[128:256, tile * 256 : tile * 256 + 256] = pattern

    cell_rank = iota((128, 1), 0)
    cell_id = (gx * 8 + lax.shift_right_logical(cell_rank, 4)) * 1024 + yz * 16 + lax.bitwise_and(cell_rank, 15)
    found = jnp.zeros((128, 128), F32)
    for tile in range(32):
        label = (iota((1, 128), 1) + (tile * 128 + 1)).astype(F32)
        found = found + jnp.where(cell[:, tile * 128 : tile * 128 + 128] == cell_id, label, 0.0)
    owner = jnp.sum(found, axis=1, keepdims=True).astype(jnp.int32) - 1
    owner_row = lax.shift_right_arithmetic(owner, 6)
    owner_lane = lax.bitwise_and(owner, 127)
    pick_row = (lax.bitwise_and(iota((128, 128), 1), 63) == owner_row).astype(F32).astype(BF16)

    arrived(cols.at[pl.ds(0, 8)], 0)
    for d in (4, 3, 2, 1):
        slot = wrap(z + d, 16)
        remote(cols.at[slot], cols.at[slot], 19, device_at(wrap(z - 4, 16), y, x, c)).start()
    for d in (-3, -2, -1):
        slot = wrap(z + d, 16)
        remote(cols.at[slot], cols.at[slot], 19, device_at(wrap(z + 4, 16), y, x, c)).start()

    @pl.when(upper)
    def _():
        ring_in[...] = adj[3 * quarter : 4 * quarter, 8]

    @pl.when(lower)
    def _():
        ring_in[...] = adj[0:quarter, 1]

    @pl.when(jnp.logical_not(jump))
    def _():
        arrived(ring_in, 15)

    pl.semaphore_wait(credit, 1)
    around = remote(ring_in, far_in, 16, facing)
    around.start()

    z_first, z_last = iota((16, 128), 1) == 0, iota((16, 128), 1) == 127
    y_first, y_last = iota((16, 128), 0) == 0, iota((16, 128), 0) == 15

    def laplacian(field, k, i, left, right):
        value = field[k, i]
        total = field[k, i - 1] + field[k, i + 1]
        total = total + jnp.where(z_first, 0.0, pltpu.roll(value, 1, 1)) + jnp.where(z_last, 0.0, pltpu.roll(value, 127, 1))
        total = total + jnp.where(y_first, left, pltpu.roll(value, 1, 0)) + jnp.where(y_last, right, pltpu.roll(value, 15, 0))
        return total - 6.0 * value, value

    def correlate(i, carry):
        for k in range(comps):
            lap, _ = laplacian(fwd, k, i, 0.0, 0.0)
            carry = carry + adj[k, i] * lap
        return carry

    corr[0:16, :] = lax.fori_loop(1, 9, correlate, jnp.zeros((16, 128), F32))

    back_prev = remote(x_out.at[0], x_in.at[1], 10, (lax.max(gx - 1, 0), yz))
    back_next = remote(x_out.at[1], x_in.at[0], 11, (lax.min(gx + 1, 7), yz))

    def send_back(side, halo, sem, inner, copy):
        arrived(adj.at[:, halo], sem)
        product = plane
        for k in range(comps):
            product = product + adj[k, halo] * fwd[k, inner]
        x_out[side] = product
        copy.start()

    @pl.when(near_prev)
    def _():
        send_back(0, 0, 2, 1, back_prev)

    @pl.when(near_next)
    def _():
        send_back(1, 9, 1, 8, back_next)

    arrived(cols.at[pl.ds(0, 7)], 19)
    surf[yx] = cols[:, 0, :]
    taps_own = cols[0:8, 1, :]
    for k in range(8):
        taps[k, x] = taps_own[k : k + 1, :]
    for dy in RING_OFFSETS:
        for dx in RING_OFFSETS:
            if (dy, dx) != (0, 0):
                remote(surf.at[yx], surf.at[yx], 5, device_at(z, wrap(y + dy, 4), wrap(x + dx, 4), c)).start()
    for dx in (2, 1, 3):
        remote(taps.at[:, x], taps.at[:, x], 6, device_at(z, y, wrap(x + dx, 4), c)).start()

    @pl.when(has_left)
    def _():
        arrived(y_in.at[0], 4)

    @pl.when(has_right)
    def _():
        arrived(y_in.at[1], 3)

    corr[16:24, :] = jnp.zeros((8, 128), F32)
    for side, row in ((0, 0), (1, 15)):
        edge = jnp.zeros((8, 128), F32)
        for k in range(comps):
            edge = edge + y_in[side, k] * fwd[k, 1:9, row, :]
        corr[16 + side : 17 + side, :] = jnp.sum(edge, axis=0, keepdims=True)

    knots_z, _, knots_y = coarse.shape
    material = jnp.zeros((16, 128), F32)
    for k in range(knots_z):
        knot = jnp.sum(weights_y[:, 0:knots_y] * coarse[k], axis=1, keepdims=True)
        material = material + knot * weights_z[k : k + 1, :]
    material = time_step * material

    def update(i):
        laps = []
        for k in range(comps):
            lap, _ = laplacian(adj, k, i, y_in[0, k, pl.ds(i - 1, 1), :], y_in[1, k, pl.ds(i - 1, 1), :])
            laps.append(lap)
        for k in range(comps):
            mixed = laps[k]
            for m in range(comps):
                mixed = mixed + coupling[k, m] * laps[m]
            value = adj[k, i]
            updated[k, i - 1] = value + material * mixed - (time_step * damping[0, k]) * value

    @pl.loop(2, 8)
    def _(i):
        update(i)

    arrived(taps.at[:, pl.ds(0, 3)], 6)
    for k in range(32):
        taps_all[k : k + 1, :] = taps[k // 4, k % 4]
    to_mate = remote(taps_all, taps_mate, 7, mate)
    to_mate.start()

    arrived(surf.at[pl.ds(0, 15)], 5)
    head, rest = split(surf[...].reshape(256, 128))
    samples = jnp.concatenate([head, rest], axis=1)
    for tile in range(16):
        lanes = slice(tile * 256, tile * 256 + 256)
        match = jnp.dot(samples, one_hot[:, lanes], preferred_element_type=F32)
        mine = jnp.sum(jnp.where(iota((256, 256), 0) == row_of[:, lanes], match, 0.0), axis=0, keepdims=True)
        picked[2 * tile : 2 * tile + 1, :] = mine[:, 0:128]
        picked[2 * tile + 1 : 2 * tile + 2, :] = mine[:, 128:256]
    picks = remote(picked, picked_mate, 8, mate)
    picks.start()

    @pl.when(near_prev)
    def _():
        arrived(x_in.at[0], 11)

    @pl.when(near_next)
    def _():
        arrived(x_in.at[1], 10)

    def project(cells, rows):
        part = lax.dot_general(weights_z, cells, (((1,), (1,)), ((), ())), precision=HIGH, preferred_element_type=F32)
        return jnp.dot(part, rows, precision=HIGH, preferred_element_type=F32)

    corr[0:16, :] = corr[0:16, :] + x_in[0] + x_in[1]
    rows = jnp.concatenate([weights_y, y_in[0, comps, 0:1, :], y_in[1, comps, 0:1, :], jnp.zeros((6, 128), F32)], axis=0)
    grad_c[0, 0] = project(corr[...], rows)
    grad_c[0, 1] = jnp.zeros((8, 128), F32)

    to_mate.wait()
    first, second = jnp.where(c == 0, taps_all[...], taps_mate[...]), jnp.where(c == 0, taps_mate[...], taps_all[...])
    low_half = iota((32, 128), 1) < 64
    weight = jnp.where(low_half, first, pltpu.roll(second, 64, 1))
    tails = jnp.where(low_half, pltpu.roll(first, 64, 1), second)
    picks.wait()
    impulse[...] = weight * (picked[...] + picked_mate[...]) + tails

    flat = jnp.concatenate([impulse[k : k + 1, :] for k in range(32)], axis=1).astype(BF16)
    through = lax.dot_general(flat, plt_buf[...], (((1,), (1,)), ((), ())), preferred_element_type=F32)
    through = jnp.concatenate([through, through], axis=1)
    own_half = lax.div(iota((1, 128), 1), 64) == c
    own_row = jnp.where(own_half, through + impulse[pl.ds(lax.div(yz, 2), 1), :], 0.0)
    react[yz] = own_row
    for dz in NEAR_OFFSETS:
        for dx in RING_OFFSETS:
            for dc in (1, 0):
                if (dz, dx, dc) != (0, 0, 0):
                    target = device_at(wrap(z - dz, 16), y, wrap(x + dx, 4), wrap(c + dc, 2))
                    remote(react.at[yz], react.at[yz], 9, target).start()
    reaction[...] = jnp.where(c == 0, own_row[:, 0:64], own_row[:, 64:128])

    arrived(far_in, 16)
    from_upper, from_lower = z_hi == 1, z_hi == 0
    for ring in range(4):
        part = pl.ds(ring * quarter, quarter)
        here = y == ring
        if ring != 0:
            pl.when(jnp.logical_and(here, from_upper))(remote(far_in, adj.at[part, 0], 17, (z_hi * 4, yz)).start)
        if ring != 3:
            pl.when(jnp.logical_and(here, from_lower))(remote(far_in, adj.at[part, 9], 17, (z_hi * 4 + 3, yz)).start)

    @pl.when(lower)
    def _():
        adj[0:quarter, 0] = far_in[...]
        arrived(adj.at[pl.ds(quarter, 3 * quarter), 0], 17)
        product = plane
        for k in range(comps):
            product = product + adj[k, 0] * fwd[k, 1]
        grad_c[0, 1] = project(product, weights_y)

    @pl.when(upper)
    def _():
        adj[3 * quarter : 4 * quarter, 9] = far_in[...]
        arrived(adj.at[pl.ds(0, 3 * quarter), 9], 17)
        product = plane
        for k in range(comps):
            product = product + adj[k, 9] * fwd[k, 8]
        grad_c[0, 1] = project(product, weights_y)

    cores = remote(grad_c.at[0], grad_c.at[1], 12, mate)
    cores.start()
    cores.wait()
    grad_x[x] = grad_c[0] + grad_c[1]
    for dx in (2, 1, 3):
        remote(grad_x.at[x], grad_x.at[x], 13, device_at(z, y, wrap(x + dx, 4), c)).start()
    arrived(grad_x.at[pl.ds(0, 3)], 13)
    both = (grad_x[0] + grad_x[1]) + (grad_x[2] + grad_x[3])
    grad_z[z_lo] = both[0]
    grad_far[...] = both[1]
    across = [
        remote(grad_far, grad_z.at[8 + z_lo], 18, device_at((1 - z_hi) * 8 + k, 3 - y, x, c))
        for k in range(8)
    ]

    @pl.when(jump)
    def _():
        for copy in across:
            copy.start()

    for d in (7, 6, 5, 4, 3, 2, 1):
        remote(grad_z.at[z_lo], grad_z.at[z_lo], 14, (gx, lax.rem(z_lo + d, 8) * 8 + x * 2 + c)).start()

    @pl.loop(0, 2)
    def _(side):
        update(1 + 7 * side)

    arrived(react.at[pl.ds(0, 63)], 9)
    head, rest = split(react[...].reshape(64, 128))
    forces = jnp.dot(pick_row, jnp.concatenate([head, rest], axis=0), preferred_element_type=F32)
    forces = jnp.sum(jnp.where(iota((128, 128), 1) == owner_lane, forces, 0.0), axis=1, keepdims=True)
    forces = (time_step * surface_gain) * forces.reshape(8, 16, 1)
    updated[2] = updated[2] + jnp.where(iota((8, 16, 128), 2) == 0, forces, 0.0)

    arrived(grad_z.at[pl.ds(0, 7)], 14)
    total = grad_z[0]
    for k in range(1, 8):
        total = total + grad_z[k]

    def put(values):
        values = values / (grad_norm * 4096.0**0.5)
        for k in range(knots_z):
            grad[k] = values[k : k + 1, 0:knots_y]

    @pl.when(jnp.logical_not(jump))
    def _():
        put(total)

    @pl.when(jump)
    def _():
        arrived(grad_z.at[pl.ds(8, 8)], 18)
        values = total
        for k in range(8, 16):
            values = values + grad_z[k]
        put(values)

    sent(cols.at[pl.ds(0, 8)], 0)
    sent(cols.at[pl.ds(0, 7)], 19)
    sent(far_in, 16)
    sent(surf.at[pl.ds(0, 15)], 5)
    sent(taps.at[:, pl.ds(0, 3)], 6)
    sent(react.at[pl.ds(0, 63)], 9)
    sent(grad_x.at[pl.ds(0, 3)], 13)
    sent(grad_z.at[pl.ds(0, 7)], 14)
    for present, copy in (
        (near_prev, to_prev), (near_next, to_next), (has_left, to_left), (has_right, to_right),
        (near_prev, back_prev), (near_next, back_next),
    ):
        pl.when(present)(copy.wait_send)

    @pl.when(jump)
    def _():
        sent(adj.at[pl.ds(0, 3 * quarter), 0], 15)
        sent(grad_z.at[pl.ds(0, 8)], 18)

    @pl.when(jnp.logical_not(jump))
    def _():
        sent(far_in, 17)


def store_results(*refs):
    count = len(refs) // 2
    copies = [pltpu.make_async_copy(refs[k], refs[count + k], refs[-1].at[k]) for k in range(count)]
    for copy in copies:
        copy.start()
    for copy in copies:
        copy.wait()


def on_device(adjoint, forward, coarse_model, knot_span, knot_frac, dof_cell, impedance, history, plate, coupling, damping):
    comps, cells_x, cells_y, depth = adjoint.shape
    knots_y, knots_z = coarse_model.shape[1:]
    vmem = pl.BlockSpec(memory_space=pltpu.VMEM)
    hbm = pl.BlockSpec(memory_space=pltpu.HBM)
    updated, grad, reaction = pl.pallas_call(
        kernel,
        out_shape=(
            jax.ShapeDtypeStruct(adjoint.shape, F32),
            jax.ShapeDtypeStruct((knots_z, 1, knots_y), F32),
            jax.ShapeDtypeStruct((1, 64), F32),
        ),
        in_specs=[hbm] * 11,
        out_specs=(vmem, vmem, vmem),
        scratch_shapes=[
            pltpu.VMEM((knots_z, 1, knots_y), F32),
            pltpu.VMEM((1, cells_y), jnp.int32),
            pltpu.VMEM((1, cells_y), F32),
            pltpu.VMEM((1, dof_cell.size), jnp.int32),
            pltpu.VMEM(impedance.shape, F32),
            pltpu.VMEM(history.shape, F32),
            pltpu.SMEM(coupling.shape, F32),
            pltpu.SMEM((1, comps), F32),
            pltpu.VMEM((comps, cells_x + 2, cells_y, depth), F32),
            pltpu.VMEM((comps, cells_x + 2, cells_y, depth), F32),
            pltpu.VMEM(plate.shape, BF16),
            pltpu.VMEM((16, 2, 128), F32),
            pltpu.VMEM((16, 16, 128), F32),
            pltpu.VMEM((8, 4, 1, 128), F32),
            pltpu.VMEM((32, 128), F32),
            pltpu.VMEM((32, 128), F32),
            pltpu.VMEM((32, 128), F32),
            pltpu.VMEM((32, 128), F32),
            pltpu.VMEM((32, 128), F32),
            pltpu.VMEM((256, 4096), BF16),
            pltpu.VMEM((1, 4096), jnp.int32),
            pltpu.VMEM((64, 1, 128), F32),
            pltpu.VMEM((2, comps + 1, 8, 128), F32),
            pltpu.VMEM((2, comps + 1, 8, 128), F32),
            pltpu.VMEM((24, 128), F32),
            pltpu.VMEM((2, 16, 128), F32),
            pltpu.VMEM((2, 16, 128), F32),
            pltpu.VMEM((2, 2, 8, 128), F32),
            pltpu.VMEM((4, 2, 8, 128), F32),
            pltpu.VMEM((16, 8, 128), F32),
            pltpu.VMEM((comps // 4, cells_y, depth), F32),
            pltpu.VMEM((comps // 4, cells_y, depth), F32),
            pltpu.VMEM((8, 128), F32),
            pltpu.SemaphoreType.DMA((16,)),
            pltpu.SemaphoreType.DMA((20,)),
            pltpu.SemaphoreType.DMA((20,)),
            pltpu.SemaphoreType.REGULAR,
        ],
        compiler_params=pltpu.CompilerParams(collective_id=0, has_side_effects=True, vmem_limit_bytes=VMEM_BYTES),
        name="adjoint_step",
    )(
        *[
            pltpu.with_memory_space_constraint(operand, pltpu.HBM)
            for operand in (
                adjoint, forward, coarse_model.transpose(2, 0, 1), knot_span.reshape(1, -1), knot_frac.reshape(1, -1),
                dof_cell.reshape(1, -1), impedance, history, plate, coupling, damping.reshape(1, -1),
            )
        ]
    )
    results = (updated, grad, reaction)
    updated, grad, reaction = pl.pallas_call(
        store_results,
        out_shape=tuple(jax.ShapeDtypeStruct(a.shape, a.dtype) for a in results),
        in_specs=[vmem] * 3,
        out_specs=(hbm,) * 3,
        scratch_shapes=[pltpu.SemaphoreType.DMA((3,))],
        name="store_results",
    )(*results)
    return updated, grad.transpose(1, 2, 0), reaction.reshape(-1)


def solution(mesh):
    return jax.shard_map(
        on_device,
        mesh=mesh,
        in_specs=(
            P(None, "gx", "yz", None),
            P(None, "gx", "yz", None),
            P("gx", None, None),
            P("yz"),
            P("yz"),
            P(),
            P(None, "yz"),
            P(None, "yz"),
            P("yz", None),
            P(),
            P(),
        ),
        out_specs=(P(None, "gx", "yz", None), P("gx", None, None), P("yz")),
        check_vma=False,
    )
```

```python
import functools

import jax
import jax.numpy as jnp
from jax import lax
from jax.experimental import pallas as pl
from jax.experimental.pallas import tpu as pltpu
from jax.sharding import PartitionSpec as P

MESH = pl.DeviceIdType.MESH
F32 = jnp.float32
BF16 = jnp.bfloat16
HIGH = lax.Precision.HIGHEST

HZ = 32
VMEM_BYTES = 16 * 1024 * 1024
STORE_VMEM_BYTES = 4 * 1024 * 1024
time_step = 0.1
surface_gain = 40.0
grad_norm = 20.0

NEAR_OFFSETS = tuple(sorted(range(-4, 4), key=lambda d: -abs(d)))
RING_OFFSETS = (2, 1, 3, 0)


def bspline_weights(param):
    inverse = 1.0 - param
    return (
        inverse**3 / 6.0,
        (3.0 * param**3 - 6.0 * param**2 + 4.0) / 6.0,
        (-3.0 * param**3 + 3.0 * param**2 + 3.0 * param + 1.0) / 6.0,
        param**3 / 6.0,
    )


def spread_basis(index, span, param):
    total = 0.0
    for shift, weight in enumerate(bspline_weights(param)):
        total = total + jnp.where(index == span + shift, weight, 0.0)
    return total


def iota(shape, dim):
    return lax.broadcasted_iota(jnp.int32, shape, dim)


def split(values):
    head = values.astype(BF16)
    return head, (values - head.astype(F32)).astype(BF16)


def device_at(z, y, x, c):
    return (lax.div(z, 8) * 4 + y, lax.rem(z, 8) * 8 + x * 2 + c)


def wrap(value, count):
    return lax.rem(value + 2 * count, count)


def kernel(
    adjoint, forward, coarse_hbm, span_hbm, frac_hbm, dof_hbm, impedance_hbm, history_hbm, plate, coupling_hbm, damping_hbm,
    updated, grad, reaction,
    coarse, span, frac, dof, impedance, history, coupling, damping,
    adj, fwd, plt_buf, cols, surf, taps, taps_all, picked, picked_mate, taps_mate, impulse, one_hot, row_of, react,
    y_out, y_in, corr, x_out, x_in, grad_c, grad_x, grad_z, ring_adj, ring_fwd, far_in, grad_far, grad_far_in,
    load_sems, send_sems, recv_sems, credit,
):
    gx, yz = lax.axis_index("gx"), lax.axis_index("yz")
    z_hi, y = lax.div(gx, 4), lax.rem(gx, 4)
    z_lo, x, c = lax.div(yz, 8), lax.rem(lax.div(yz, 2), 4), lax.rem(yz, 2)
    z = z_hi * 8 + z_lo
    yx = y * 4 + x
    comps = adj.shape[0]
    has_prev, has_next = gx > 0, gx < 7
    has_left, has_right = yz > 0, yz < 63
    mate = (gx, yz + 1 - 2 * c)

    upper, lower = jnp.logical_and(z_hi == 0, y == 3), jnp.logical_and(z_hi == 1, y == 0)
    jump = jnp.logical_or(upper, lower)
    near_prev, near_next = jnp.logical_and(has_prev, jnp.logical_not(lower)), jnp.logical_and(has_next, jnp.logical_not(upper))
    facing = device_at(wrap(z + 8, 16), y, x, c)

    loads = [
        pltpu.make_async_copy(adjoint.at[2], adj.at[2, pl.ds(1, 8)], load_sems.at[0]),
        pltpu.make_async_copy(impedance_hbm, impedance, load_sems.at[8]),
        pltpu.make_async_copy(history_hbm, history, load_sems.at[9]),
        pltpu.make_async_copy(adjoint.at[pl.ds(0, 2)], adj.at[pl.ds(0, 2), pl.ds(1, 8)], load_sems.at[1]),
        pltpu.make_async_copy(adjoint.at[pl.ds(3, 9)], adj.at[pl.ds(3, 9), pl.ds(1, 8)], load_sems.at[2]),
        pltpu.make_async_copy(forward, fwd.at[:, pl.ds(1, 8)], load_sems.at[3]),
        pltpu.make_async_copy(plate, plt_buf, load_sems.at[4]),
        pltpu.make_async_copy(coarse_hbm, coarse, load_sems.at[10]),
        pltpu.make_async_copy(span_hbm, span, load_sems.at[11]),
        pltpu.make_async_copy(frac_hbm, frac, load_sems.at[12]),
        pltpu.make_async_copy(dof_hbm, dof, load_sems.at[13]),
        pltpu.make_async_copy(coupling_hbm, coupling, load_sems.at[14]),
        pltpu.make_async_copy(damping_hbm, damping, load_sems.at[15]),
    ]
    for load in loads:
        load.start()

    barrier = pltpu.get_barrier_semaphore()

    def greet(device):
        pl.semaphore_signal(barrier, inc=1, device_id=device, device_id_type=MESH)

    greeted = 24 + has_left.astype(jnp.int32) + has_right.astype(jnp.int32)

    for d in (4, -4, 3, -3, 2, -2, 1, -1):
        greet(device_at(wrap(z + d, 16), y, x, c))
    for dy in RING_OFFSETS:
        for dx in RING_OFFSETS:
            if (dy, dx) != (0, 0):
                greet(device_at(z, wrap(y + dy, 4), wrap(x + dx, 4), c))
    greet(mate)

    @pl.when(has_left)
    def _():
        greet((gx, yz - 1))

    @pl.when(has_right)
    def _():
        greet((gx, yz + 1))

    loads[1].wait()
    loads[2].wait()
    tail = jnp.sum(impedance[1:, :] * history[...], axis=0, keepdims=True)
    cols[z, 1:2, :] = jnp.concatenate([impedance[0:1, :], tail], axis=1)
    loads[0].wait()
    surface = adj[2, 1:9].reshape(128, 128)
    cols[z, 0:1, :] = jnp.transpose(surface)[0:1, :]

    pl.semaphore_wait(barrier, greeted)

    def remote(src, dst, sem, device):
        return pltpu.make_async_remote_copy(
            src_ref=src, dst_ref=dst, send_sem=send_sems.at[sem], recv_sem=recv_sems.at[sem], device_id=device, device_id_type=MESH
        )

    def arrived(ref, sem):
        pltpu.make_async_copy(ref, ref, recv_sems.at[sem]).wait()

    def sent(ref, sem):
        pltpu.make_async_copy(ref, ref, send_sems.at[sem]).wait()

    for d in (4, -4, 3, -3, 2, -2, 1, -1):
        remote(cols.at[z], cols.at[z], 0, device_at(wrap(z + d, 16), y, x, c)).start()

    quarter = comps // 4
    for field, buffer, sem in ((adjoint, ring_adj, 15), (forward, ring_fwd, 1)):
        for ring in range(4):
            part = pl.ds(ring * quarter, quarter)
            if ring != 3:
                pl.when(upper)(remote(field.at[part, 7], buffer, sem, (z_hi * 4 + ring, yz)).start)
            if ring != 0:
                pl.when(lower)(remote(field.at[part, 0], buffer, sem, (z_hi * 4 + ring, yz)).start)

    pl.semaphore_signal(credit, inc=1, device_id=device_at(wrap(z - 4, 16), y, x, c), device_id_type=MESH)

    for load in loads[3:]:
        load.wait()
    to_prev = remote(adj.at[:, 1], adj.at[:, 9], 20, (lax.max(gx - 1, 0), yz))
    to_next = remote(adj.at[:, 8], adj.at[:, 0], 2, (lax.min(gx + 1, 7), yz))

    @pl.when(near_prev)
    def _():
        to_prev.start()

    @pl.when(near_next)
    def _():
        to_next.start()

    plane = jnp.zeros((16, 128), F32)
    for k in range(comps):
        fwd[k, 0] = plane
        fwd[k, 9] = plane

    @pl.when(gx == 0)
    def _():
        for k in range(comps):
            adj[k, 0] = plane

    @pl.when(gx == 7)
    def _():
        for k in range(comps):
            adj[k, 9] = plane

    @pl.when(jnp.logical_not(near_prev))
    def _():
        x_in[0] = plane

    @pl.when(jnp.logical_not(near_next))
    def _():
        x_in[1] = plane

    diagonal = iota((16, 16), 0) == iota((16, 16), 1)
    span_col = jnp.sum(jnp.where(diagonal, span[...], 0), axis=1, keepdims=True)
    frac_col = jnp.sum(jnp.where(diagonal, frac[...], 0.0), axis=1, keepdims=True)
    weights_y = spread_basis(iota((16, 128), 1), span_col, frac_col)
    depth = iota((8, 128), 1)
    depth_span = lax.div(depth, HZ)
    weights_z = spread_basis(iota((8, 128), 0), depth_span, (depth.astype(F32) + 0.5) / HZ - depth_span.astype(F32))

    for side, row in ((0, 0), (1, 15)):
        for k in range(comps):
            y_out[side, k] = adj[k, 1:9, row, :]
        y_out[side, comps] = jnp.broadcast_to(weights_y[row : row + 1, :], (8, 128))
    to_left = remote(y_out.at[0], y_in.at[1], 3, (gx, lax.max(yz - 1, 0)))
    to_right = remote(y_out.at[1], y_in.at[0], 4, (gx, lax.min(yz + 1, 63)))

    @pl.when(has_left)
    def _():
        to_left.start()

    @pl.when(has_right)
    def _():
        to_right.start()

    @pl.when(yz == 0)
    def _():
        y_in[0] = jnp.zeros_like(y_in[0])

    @pl.when(yz == 63)
    def _():
        y_in[1] = jnp.zeros_like(y_in[1])

    cell = dof[...]
    cell_x, cell_y = lax.shift_right_logical(cell, 10), lax.bitwise_and(cell, 1023)
    lane = lax.bitwise_and(cell_x, 7) * 16 + lax.bitwise_and(cell_y, 15)
    cell_gx, cell_yz = lax.shift_right_logical(cell_x, 3), lax.shift_right_logical(cell_y, 4)
    cell_row = (
        lax.bitwise_and(cell_gx, 3) * 64
        + lax.bitwise_and(lax.shift_right_logical(cell_yz, 1), 3) * 16
        + lax.shift_right_logical(cell_gx, 2) * 8
        + lax.shift_right_logical(cell_yz, 3)
    )
    row_of[...] = jnp.where(lax.bitwise_and(cell_yz, 1) == c, cell_row, -1)
    for tile in range(16):
        pattern = (iota((128, 256), 0) == lane[:, tile * 256 : tile * 256 + 256]).astype(F32).astype(BF16)
        one_hot[0:128, tile * 256 : tile * 256 + 256] = pattern
        one_hot[128:256, tile * 256 : tile * 256 + 256] = pattern

    cell_rank = iota((128, 1), 0)
    cell_id = (gx * 8 + lax.shift_right_logical(cell_rank, 4)) * 1024 + yz * 16 + lax.bitwise_and(cell_rank, 15)
    found = jnp.zeros((128, 128), F32)
    for tile in range(32):
        label = (iota((1, 128), 1) + (tile * 128 + 1)).astype(F32)
        found = found + jnp.where(cell[:, tile * 128 : tile * 128 + 128] == cell_id, label, 0.0)
    owner = jnp.sum(found, axis=1, keepdims=True).astype(jnp.int32) - 1
    owner_row = lax.shift_right_arithmetic(owner, 6)
    owner_lane = lax.bitwise_and(owner, 127)
    pick_row = (lax.bitwise_and(iota((128, 128), 1), 63) == owner_row).astype(F32).astype(BF16)

    @pl.when(upper)
    def _():
        ring_adj[...] = adj[3 * quarter : 4 * quarter, 8]
        ring_fwd[...] = fwd[3 * quarter : 4 * quarter, 8]

    @pl.when(lower)
    def _():
        ring_adj[...] = adj[0:quarter, 1]
        ring_fwd[...] = fwd[0:quarter, 1]

    @pl.when(jnp.logical_not(jump))
    def _():
        arrived(ring_adj, 15)

    pl.semaphore_wait(credit, 1)
    around = remote(ring_adj, far_in, 16, facing)
    around.start()

    arrived(cols.at[pl.ds(0, 8)], 0)
    for d in (4, 3, 2, 1):
        slot = wrap(z + d, 16)
        remote(cols.at[slot], cols.at[slot], 19, device_at(wrap(z - 4, 16), y, x, c)).start()
    for d in (-3, -2, -1):
        slot = wrap(z + d, 16)
        remote(cols.at[slot], cols.at[slot], 19, device_at(wrap(z + 4, 16), y, x, c)).start()

    z_first, z_last = iota((16, 128), 1) == 0, iota((16, 128), 1) == 127
    y_first, y_last = iota((16, 128), 0) == 0, iota((16, 128), 0) == 15

    def laplacian(field, k, i, left, right):
        value = field[k, i]
        total = field[k, i - 1] + field[k, i + 1]
        total = total + jnp.where(z_first, 0.0, pltpu.roll(value, 1, 1)) + jnp.where(z_last, 0.0, pltpu.roll(value, 127, 1))
        total = total + jnp.where(y_first, left, pltpu.roll(value, 1, 0)) + jnp.where(y_last, right, pltpu.roll(value, 15, 0))
        return total - 6.0 * value, value

    def correlate(i, carry):
        for k in range(comps):
            lap, _ = laplacian(fwd, k, i, 0.0, 0.0)
            carry = carry + adj[k, i] * lap
        return carry

    corr[0:16, :] = lax.fori_loop(1, 9, correlate, jnp.zeros((16, 128), F32))

    back_prev = remote(x_out.at[0], x_in.at[1], 10, (lax.max(gx - 1, 0), yz))
    back_next = remote(x_out.at[1], x_in.at[0], 11, (lax.min(gx + 1, 7), yz))

    def send_back(side, halo, sem, inner, copy):
        arrived(adj.at[:, halo], sem)
        product = plane
        for k in range(comps):
            product = product + adj[k, halo] * fwd[k, inner]
        x_out[side] = product
        copy.start()

    @pl.when(near_prev)
    def _():
        send_back(0, 0, 2, 1, back_prev)

    @pl.when(near_next)
    def _():
        send_back(1, 9, 20, 8, back_next)

    arrived(cols.at[pl.ds(0, 7)], 19)
    surf[yx] = cols[:, 0, :]
    taps_own = cols[0:8, 1, :]
    for k in range(8):
        taps[k, x] = taps_own[k : k + 1, :]
    for dy in RING_OFFSETS:
        for dx in RING_OFFSETS:
            if (dy, dx) != (0, 0):
                remote(surf.at[yx], surf.at[yx], 5, device_at(z, wrap(y + dy, 4), wrap(x + dx, 4), c)).start()
    for dx in (2, 1, 3):
        remote(taps.at[:, x], taps.at[:, x], 6, device_at(z, y, wrap(x + dx, 4), c)).start()

    @pl.when(has_left)
    def _():
        arrived(y_in.at[0], 4)

    @pl.when(has_right)
    def _():
        arrived(y_in.at[1], 3)

    corr[16:24, :] = jnp.zeros((8, 128), F32)
    for side, row in ((0, 0), (1, 15)):
        edge = jnp.zeros((8, 128), F32)
        for k in range(comps):
            edge = edge + y_in[side, k] * fwd[k, 1:9, row, :]
        corr[16 + side : 17 + side, :] = jnp.sum(edge, axis=0, keepdims=True)

    knots_z, _, knots_y = coarse.shape
    material = jnp.zeros((16, 128), F32)
    for k in range(knots_z):
        knot = jnp.sum(weights_y[:, 0:knots_y] * coarse[k], axis=1, keepdims=True)
        material = material + knot * weights_z[k : k + 1, :]
    material = time_step * material

    def update(i):
        laps = []
        for k in range(comps):
            lap, _ = laplacian(adj, k, i, y_in[0, k, pl.ds(i - 1, 1), :], y_in[1, k, pl.ds(i - 1, 1), :])
            laps.append(lap)
        for k in range(comps):
            mixed = laps[k]
            for m in range(comps):
                mixed = mixed + coupling[k, m] * laps[m]
            value = adj[k, i]
            updated[k, i - 1] = value + material * mixed - (time_step * damping[0, k]) * value

    @pl.loop(2, 8)
    def _(i):
        update(i)

    arrived(taps.at[:, pl.ds(0, 3)], 6)
    for k in range(32):
        taps_all[k : k + 1, :] = taps[k // 4, k % 4]
    to_mate = remote(taps_all, taps_mate, 7, mate)
    to_mate.start()

    arrived(surf.at[pl.ds(0, 15)], 5)
    head, rest = split(surf[...].reshape(256, 128))
    samples = jnp.concatenate([head, rest], axis=1)
    for tile in range(16):
        lanes = slice(tile * 256, tile * 256 + 256)
        match = jnp.dot(samples, one_hot[:, lanes], preferred_element_type=F32)
        mine = jnp.sum(jnp.where(iota((256, 256), 0) == row_of[:, lanes], match, 0.0), axis=0, keepdims=True)
        picked[2 * tile : 2 * tile + 1, :] = mine[:, 0:128]
        picked[2 * tile + 1 : 2 * tile + 2, :] = mine[:, 128:256]
    picks = remote(picked, picked_mate, 8, mate)
    picks.start()

    @pl.when(near_prev)
    def _():
        arrived(x_in.at[0], 11)

    @pl.when(near_next)
    def _():
        arrived(x_in.at[1], 10)

    def project(cells, rows):
        part = lax.dot_general(weights_z, cells, (((1,), (1,)), ((), ())), precision=HIGH, preferred_element_type=F32)
        return jnp.dot(part, rows, precision=HIGH, preferred_element_type=F32)

    corr[0:16, :] = corr[0:16, :] + x_in[0] + x_in[1]
    rows = jnp.concatenate([weights_y, y_in[0, comps, 0:1, :], y_in[1, comps, 0:1, :], jnp.zeros((6, 128), F32)], axis=0)
    grad_c[0, 0] = project(corr[...], rows)

    arrived(far_in, 16)
    for ring in range(4):
        part = pl.ds(ring * quarter, quarter)
        here = y == ring
        if ring != 0:
            pl.when(jnp.logical_and(here, z_hi == 1))(remote(far_in, adj.at[part, 0], 17, (z_hi * 4, yz)).start)
        if ring != 3:
            pl.when(jnp.logical_and(here, z_hi == 0))(remote(far_in, adj.at[part, 9], 17, (z_hi * 4 + 3, yz)).start)

    @pl.when(lower)
    def _():
        adj[0:quarter, 0] = far_in[...]

    @pl.when(upper)
    def _():
        adj[3 * quarter : 4 * quarter, 9] = far_in[...]

    @pl.when(jnp.logical_not(jump))
    def _():
        arrived(ring_fwd, 1)

    product = plane
    for k in range(quarter):
        product = product + far_in[k] * ring_fwd[k]
    grad_c[0, 1] = project(product, weights_y)

    cores = remote(grad_c.at[0], grad_c.at[1], 12, mate)
    cores.start()

    to_mate.wait()
    first, second = jnp.where(c == 0, taps_all[...], taps_mate[...]), jnp.where(c == 0, taps_mate[...], taps_all[...])
    low_half = iota((32, 128), 1) < 64
    weight = jnp.where(low_half, first, pltpu.roll(second, 64, 1))
    tails = jnp.where(low_half, pltpu.roll(first, 64, 1), second)
    picks.wait()
    impulse[...] = weight * (picked[...] + picked_mate[...]) + tails

    cores.wait()
    grad_x[x] = grad_c[0] + grad_c[1]
    for dx in (2, 1, 3):
        remote(grad_x.at[x], grad_x.at[x], 13, device_at(z, y, wrap(x + dx, 4), c)).start()

    flat = jnp.concatenate([impulse[k : k + 1, :] for k in range(32)], axis=1).astype(BF16)
    through = lax.dot_general(flat, plt_buf[...], (((1,), (1,)), ((), ())), preferred_element_type=F32)
    through = jnp.concatenate([through, through], axis=1)
    own_half = lax.div(iota((1, 128), 1), 64) == c
    own_row = jnp.where(own_half, through + impulse[pl.ds(lax.div(yz, 2), 1), :], 0.0)
    react[yz] = own_row
    for dz in NEAR_OFFSETS:
        for dx in RING_OFFSETS:
            for dc in (1, 0):
                if (dz, dx, dc) != (0, 0, 0):
                    target = device_at(wrap(z - dz, 16), y, wrap(x + dx, 4), wrap(c + dc, 2))
                    remote(react.at[yz], react.at[yz], 9, target).start()
    reaction[...] = jnp.where(c == 0, own_row[:, 0:64], own_row[:, 64:128])

    arrived(grad_x.at[pl.ds(0, 3)], 13)
    both = (grad_x[0] + grad_x[1]) + (grad_x[2] + grad_x[3])
    grad_z[z_lo] = both[0]
    grad_far[...] = both[1]
    for k in range(8):
        target = device_at((1 - z_hi) * 8 + k, jnp.where(z_hi == 1, 3, 0), x, c)
        remote(grad_far, grad_far_in.at[z_lo * 4 + y], 18, target).start()
    for d in (7, 6, 5, 4, 3, 2, 1):
        remote(grad_z.at[z_lo], grad_z.at[z_lo], 14, (gx, lax.rem(z_lo + d, 8) * 8 + x * 2 + c)).start()

    @pl.when(lower)
    def _():
        arrived(adj.at[pl.ds(quarter, 3 * quarter), 0], 17)

    @pl.when(upper)
    def _():
        arrived(adj.at[pl.ds(0, 3 * quarter), 9], 17)

    @pl.loop(0, 2)
    def _(side):
        update(1 + 7 * side)

    arrived(react.at[pl.ds(0, 63)], 9)
    head, rest = split(react[...].reshape(64, 128))
    forces = jnp.dot(pick_row, jnp.concatenate([head, rest], axis=0), preferred_element_type=F32)
    forces = jnp.sum(jnp.where(iota((128, 128), 1) == owner_lane, forces, 0.0), axis=1, keepdims=True)
    forces = (time_step * surface_gain) * forces.reshape(8, 16, 1)
    updated[2] = updated[2] + jnp.where(iota((8, 16, 128), 2) == 0, forces, 0.0)

    arrived(grad_z.at[pl.ds(0, 7)], 14)
    total = grad_z[0]
    for k in range(1, 8):
        total = total + grad_z[k]

    def put(values):
        values = values / (grad_norm * 4096.0**0.5)
        for k in range(knots_z):
            grad[k] = values[k : k + 1, 0:knots_y]

    @pl.when(jnp.logical_not(jump))
    def _():
        put(total)

    @pl.when(jump)
    def _():
        arrived(grad_far_in, 18)
        put(total + jnp.sum(grad_far_in[...], axis=0))

    sent(cols.at[pl.ds(0, 8)], 0)
    sent(cols.at[pl.ds(0, 7)], 19)
    sent(far_in, 16)
    sent(surf.at[pl.ds(0, 15)], 5)
    sent(taps.at[:, pl.ds(0, 3)], 6)
    sent(react.at[pl.ds(0, 63)], 9)
    sent(grad_x.at[pl.ds(0, 3)], 13)
    sent(grad_z.at[pl.ds(0, 7)], 14)
    for present, copy in (
        (near_prev, to_prev), (near_next, to_next), (has_left, to_left), (has_right, to_right),
        (near_prev, back_prev), (near_next, back_next),
    ):
        pl.when(present)(copy.wait_send)

    sent(grad_far_in.at[pl.ds(0, 8)], 18)

    @pl.when(jump)
    def _():
        sent(adj.at[pl.ds(0, 3 * quarter), 0], 15)
        sent(adj.at[pl.ds(0, 3 * quarter), 0], 1)

    @pl.when(jnp.logical_not(jump))
    def _():
        sent(far_in, 17)


def store_results(*refs):
    count = len(refs) // 2
    copies = [pltpu.make_async_copy(refs[k], refs[count + k], refs[-1].at[k]) for k in range(count)]
    for copy in copies:
        copy.start()
    for copy in copies:
        copy.wait()


def on_device(adjoint, forward, coarse_model, knot_span, knot_frac, dof_cell, impedance, history, plate, coupling, damping):
    comps, cells_x, cells_y, depth = adjoint.shape
    knots_y, knots_z = coarse_model.shape[1:]
    vmem = pl.BlockSpec(memory_space=pltpu.VMEM)
    hbm = pl.BlockSpec(memory_space=pltpu.HBM)
    updated, grad, reaction = pl.pallas_call(
        kernel,
        out_shape=(
            jax.ShapeDtypeStruct(adjoint.shape, F32),
            jax.ShapeDtypeStruct((knots_z, 1, knots_y), F32),
            jax.ShapeDtypeStruct((1, 64), F32),
        ),
        in_specs=[hbm] * 11,
        out_specs=(vmem, vmem, vmem),
        scratch_shapes=[
            pltpu.VMEM((knots_z, 1, knots_y), F32),
            pltpu.VMEM((1, cells_y), jnp.int32),
            pltpu.VMEM((1, cells_y), F32),
            pltpu.VMEM((1, dof_cell.size), jnp.int32),
            pltpu.VMEM(impedance.shape, F32),
            pltpu.VMEM(history.shape, F32),
            pltpu.SMEM(coupling.shape, F32),
            pltpu.SMEM((1, comps), F32),
            pltpu.VMEM((comps, cells_x + 2, cells_y, depth), F32),
            pltpu.VMEM((comps, cells_x + 2, cells_y, depth), F32),
            pltpu.VMEM(plate.shape, BF16),
            pltpu.VMEM((16, 2, 128), F32),
            pltpu.VMEM((16, 16, 128), F32),
            pltpu.VMEM((8, 4, 1, 128), F32),
            pltpu.VMEM((32, 128), F32),
            pltpu.VMEM((32, 128), F32),
            pltpu.VMEM((32, 128), F32),
            pltpu.VMEM((32, 128), F32),
            pltpu.VMEM((32, 128), F32),
            pltpu.VMEM((256, 4096), BF16),
            pltpu.VMEM((1, 4096), jnp.int32),
            pltpu.VMEM((64, 1, 128), F32),
            pltpu.VMEM((2, comps + 1, 8, 128), F32),
            pltpu.VMEM((2, comps + 1, 8, 128), F32),
            pltpu.VMEM((24, 128), F32),
            pltpu.VMEM((2, 16, 128), F32),
            pltpu.VMEM((2, 16, 128), F32),
            pltpu.VMEM((2, 2, 8, 128), F32),
            pltpu.VMEM((4, 2, 8, 128), F32),
            pltpu.VMEM((8, 8, 128), F32),
            pltpu.VMEM((comps // 4, cells_y, depth), F32),
            pltpu.VMEM((comps // 4, cells_y, depth), F32),
            pltpu.VMEM((comps // 4, cells_y, depth), F32),
            pltpu.VMEM((8, 128), F32),
            pltpu.VMEM((32, 8, 128), F32),
            pltpu.SemaphoreType.DMA((16,)),
            pltpu.SemaphoreType.DMA((21,)),
            pltpu.SemaphoreType.DMA((21,)),
            pltpu.SemaphoreType.REGULAR,
        ],
        compiler_params=pltpu.CompilerParams(collective_id=0, has_side_effects=True, vmem_limit_bytes=VMEM_BYTES),
        name="adjoint_step",
    )(
        *[
            pltpu.with_memory_space_constraint(operand, pltpu.HBM)
            for operand in (
                adjoint, forward, coarse_model.transpose(2, 0, 1), knot_span.reshape(1, -1), knot_frac.reshape(1, -1),
                dof_cell.reshape(1, -1), impedance, history, plate, coupling, damping.reshape(1, -1),
            )
        ]
    )
    results = (updated, grad, reaction)
    updated, grad, reaction = pl.pallas_call(
        store_results,
        out_shape=tuple(jax.ShapeDtypeStruct(a.shape, a.dtype) for a in results),
        in_specs=[vmem] * 3,
        out_specs=(hbm,) * 3,
        scratch_shapes=[pltpu.SemaphoreType.DMA((3,))],
        compiler_params=pltpu.CompilerParams(vmem_limit_bytes=STORE_VMEM_BYTES),
        name="store_results",
    )(*results)
    return updated, grad.transpose(1, 2, 0), reaction.reshape(-1)


def solution(mesh):
    return jax.shard_map(
        on_device,
        mesh=mesh,
        in_specs=(
            P(None, "gx", "yz", None),
            P(None, "gx", "yz", None),
            P("gx", None, None),
            P("yz"),
            P("yz"),
            P(),
            P(None, "yz"),
            P(None, "yz"),
            P("yz", None),
            P(),
            P(),
        ),
        out_specs=(P(None, "gx", "yz", None), P("gx", None, None), P("yz")),
        check_vma=False,
    )
```

```python
import functools

import jax
import jax.numpy as jnp
from jax import lax
from jax.experimental import pallas as pl
from jax.experimental.pallas import tpu as pltpu
from jax.sharding import PartitionSpec as P

MESH = pl.DeviceIdType.MESH
F32 = jnp.float32
BF16 = jnp.bfloat16
HIGH = lax.Precision.HIGHEST

HZ = 32
VMEM_BYTES = 16 * 1024 * 1024
STORE_VMEM_BYTES = 4 * 1024 * 1024
time_step = 0.1
surface_gain = 40.0
grad_norm = 20.0

NEAR_OFFSETS = tuple(sorted(range(-4, 4), key=lambda d: -abs(d)))
RING_OFFSETS = (2, 1, 3, 0)
Z_NEAR = (4, -4, 3, -3, 2, -2, 1, -1)


def bspline_weights(param):
    inverse = 1.0 - param
    return (
        inverse**3 / 6.0,
        (3.0 * param**3 - 6.0 * param**2 + 4.0) / 6.0,
        (-3.0 * param**3 + 3.0 * param**2 + 3.0 * param + 1.0) / 6.0,
        param**3 / 6.0,
    )


def spread_basis(index, span, param):
    total = 0.0
    for shift, weight in enumerate(bspline_weights(param)):
        total = total + jnp.where(index == span + shift, weight, 0.0)
    return total


def iota(shape, dim):
    return lax.broadcasted_iota(jnp.int32, shape, dim)


def split(values):
    head = values.astype(BF16)
    return head, (values - head.astype(F32)).astype(BF16)


def device_at(z, y, x, c):
    return (lax.div(z, 8) * 4 + y, lax.rem(z, 8) * 8 + x * 2 + c)


def wrap(value, count):
    return lax.rem(value + 2 * count, count)


def kernel(
    adjoint, forward, coarse_hbm, span_hbm, frac_hbm, dof_hbm, impedance_hbm, history_hbm, plate, coupling_hbm, damping_hbm,
    updated, grad, reaction,
    coarse, span, frac, dof, impedance, history, coupling, damping,
    adj, fwd, plt_buf, cols, surf, taps, taps_all, picked, impulse, one_hot, row_of, react,
    y_out, y_in, corr, x_out, x_in, grad_c, grad_x, grad_z, ring_adj, ring_fwd, mid_adj, mid_fwd, mid_weights, weights_out, far_in, grad_far, grad_far_in,
    load_sems, send_sems, recv_sems, credit,
):
    gx, yz = lax.axis_index("gx"), lax.axis_index("yz")
    z_hi, y = lax.div(gx, 4), lax.rem(gx, 4)
    z_lo, x, c = lax.div(yz, 8), lax.rem(lax.div(yz, 2), 4), lax.rem(yz, 2)
    z = z_hi * 8 + z_lo
    yx = y * 4 + x
    comps = adj.shape[0]
    has_prev, has_next = gx > 0, gx < 7
    has_left, has_right = yz > 0, yz < 63
    mate = (gx, yz + 1 - 2 * c)

    upper, lower = jnp.logical_and(z_hi == 0, y == 3), jnp.logical_and(z_hi == 1, y == 0)
    jump = jnp.logical_or(upper, lower)
    near_prev, near_next = jnp.logical_and(has_prev, jnp.logical_not(lower)), jnp.logical_and(has_next, jnp.logical_not(upper))
    z_half = lax.rem(z_lo + 4, 8)
    half_way, across = device_at(z_hi * 8 + z_half, y, x, c), device_at((1 - z_hi) * 8 + z_half, y, x, c)

    loads = [
        pltpu.make_async_copy(adjoint.at[2], adj.at[2, pl.ds(1, 8)], load_sems.at[0]),
        pltpu.make_async_copy(impedance_hbm, impedance, load_sems.at[8]),
        pltpu.make_async_copy(history_hbm, history, load_sems.at[9]),
        pltpu.make_async_copy(adjoint.at[pl.ds(0, 2)], adj.at[pl.ds(0, 2), pl.ds(1, 8)], load_sems.at[1]),
        pltpu.make_async_copy(adjoint.at[pl.ds(3, 9)], adj.at[pl.ds(3, 9), pl.ds(1, 8)], load_sems.at[2]),
        pltpu.make_async_copy(forward, fwd.at[:, pl.ds(1, 8)], load_sems.at[3]),
        pltpu.make_async_copy(coarse_hbm, coarse, load_sems.at[10]),
        pltpu.make_async_copy(span_hbm, span, load_sems.at[11]),
        pltpu.make_async_copy(frac_hbm, frac, load_sems.at[12]),
        pltpu.make_async_copy(dof_hbm, dof, load_sems.at[13]),
        pltpu.make_async_copy(coupling_hbm, coupling, load_sems.at[14]),
        pltpu.make_async_copy(damping_hbm, damping, load_sems.at[15]),
    ]
    for load in loads:
        load.start()
    leads, follows = c == 1, c == 0
    share = plate.shape[0]
    own_plate = pltpu.make_async_copy(plate, plt_buf.at[pl.ds(share, share)], load_sems.at[4])
    pl.when(leads)(own_plate.start)

    barrier = pltpu.get_barrier_semaphore()

    def greet(device):
        pl.semaphore_signal(barrier, inc=1, device_id=device, device_id_type=MESH)

    greeted = jnp.where(leads, 24, 17) + has_left.astype(jnp.int32) + has_right.astype(jnp.int32)

    @pl.when(leads)
    def _():
        for d in Z_NEAR:
            greet(device_at(wrap(z + d, 16), y, x, 1))
            greet(device_at(wrap(z + d, 16), y, x, 0))
        for dy in RING_OFFSETS:
            for dx in RING_OFFSETS:
                if (dy, dx) != (0, 0):
                    greet(device_at(z, wrap(y + dy, 4), wrap(x + dx, 4), 1))

    @pl.when(follows)
    def _():
        for d in (4, -4):
            greet(device_at(wrap(z + d, 16), y, x, 0))
        for d in (2, 1, 3):
            greet(device_at(z, wrap(y + d, 4), x, 0))
            greet(device_at(z, y, wrap(x + d, 4), 0))

    greet(mate)

    @pl.when(has_left)
    def _():
        greet((gx, yz - 1))

    @pl.when(has_right)
    def _():
        greet((gx, yz + 1))

    loads[1].wait()
    loads[2].wait()
    tail = jnp.sum(impedance[1:, :] * history[...], axis=0, keepdims=True)
    cols[c, z, 1:2, :] = jnp.concatenate([impedance[0:1, :], tail], axis=1)
    loads[0].wait()
    surface = adj[2, 1:9].reshape(128, 128)
    cols[c, z, 0:1, :] = jnp.transpose(surface)[0:1, :]

    pl.semaphore_wait(barrier, greeted)

    def remote(src, dst, sem, device):
        return pltpu.make_async_remote_copy(
            src_ref=src, dst_ref=dst, send_sem=send_sems.at[sem], recv_sem=recv_sems.at[sem], device_id=device, device_id_type=MESH
        )

    def arrived(ref, sem):
        pltpu.make_async_copy(ref, ref, recv_sems.at[sem]).wait()

    def sent(ref, sem):
        pltpu.make_async_copy(ref, ref, send_sems.at[sem]).wait()

    for core, sem in ((1, 0), (0, 24)):
        for d in Z_NEAR:
            pl.when(c == core)(remote(cols.at[core, z], cols.at[core, z], sem, device_at(wrap(z + d, 16), y, x, 1)).start)
    plate_up = remote(plate, plt_buf.at[pl.ds(0, share)], 7, mate)

    @pl.when(follows)
    def _():
        remote(cols.at[0, z], cols.at[0, z], 24, mate).start()
        plate_up.start()

    quarter = comps // 4
    for field, buffer, sem in ((adjoint, ring_adj, 15), (forward, ring_fwd, 1)):
        for ring in range(4):
            part = pl.ds(ring * quarter, quarter)
            if ring != 3:
                pl.when(upper)(remote(field.at[part, 7], buffer, sem, (z_hi * 4 + ring, yz)).start)
            if ring != 0:
                pl.when(lower)(remote(field.at[part, 0], buffer, sem, (z_hi * 4 + ring, yz)).start)

    for load in loads[3:]:
        load.wait()
    to_prev = remote(adj.at[:, 1], adj.at[:, 9], 20, (lax.max(gx - 1, 0), yz))
    to_next = remote(adj.at[:, 8], adj.at[:, 0], 2, (lax.min(gx + 1, 7), yz))

    @pl.when(near_prev)
    def _():
        to_prev.start()

    @pl.when(near_next)
    def _():
        to_next.start()

    @pl.when(leads)
    def _():
        arrived(cols.at[1, pl.ds(0, 8)], 0)
        arrived(cols.at[0, pl.ds(0, 9)], 24)
        for d, way in ((4, -4), (3, -4), (2, -4), (1, -4), (-3, 4), (-2, 4), (-1, 4)):
            slot = wrap(z + d, 16)
            remote(cols.at[:, slot], cols.at[:, slot], 19, device_at(wrap(z + way, 16), y, x, 1)).start()

    plane = jnp.zeros((16, 128), F32)
    for k in range(comps):
        fwd[k, 0] = plane
        fwd[k, 9] = plane

    @pl.when(gx == 0)
    def _():
        for k in range(comps):
            adj[k, 0] = plane

    @pl.when(gx == 7)
    def _():
        for k in range(comps):
            adj[k, 9] = plane

    @pl.when(jnp.logical_not(near_prev))
    def _():
        x_in[0] = plane

    @pl.when(jnp.logical_not(near_next))
    def _():
        x_in[1] = plane

    diagonal = iota((16, 16), 0) == iota((16, 16), 1)
    span_col = jnp.sum(jnp.where(diagonal, span[...], 0), axis=1, keepdims=True)
    frac_col = jnp.sum(jnp.where(diagonal, frac[...], 0.0), axis=1, keepdims=True)
    weights_y = spread_basis(iota((16, 128), 1), span_col, frac_col)
    depth = iota((8, 128), 1)
    depth_span = lax.div(depth, HZ)
    weights_z = spread_basis(iota((8, 128), 0), depth_span, (depth.astype(F32) + 0.5) / HZ - depth_span.astype(F32))

    for side, row in ((0, 0), (1, 15)):
        for k in range(comps):
            y_out[side, k] = adj[k, 1:9, row, :]
        y_out[side, comps] = jnp.broadcast_to(weights_y[row : row + 1, :], (8, 128))
    to_left = remote(y_out.at[0], y_in.at[1], 3, (gx, lax.max(yz - 1, 0)))
    to_right = remote(y_out.at[1], y_in.at[0], 4, (gx, lax.min(yz + 1, 63)))

    @pl.when(has_left)
    def _():
        to_left.start()

    @pl.when(has_right)
    def _():
        to_right.start()

    @pl.when(yz == 0)
    def _():
        y_in[0] = jnp.zeros_like(y_in[0])

    @pl.when(yz == 63)
    def _():
        y_in[1] = jnp.zeros_like(y_in[1])

    @pl.when(upper)
    def _():
        ring_adj[...] = adj[3 * quarter : 4 * quarter, 8]
        ring_fwd[...] = fwd[3 * quarter : 4 * quarter, 8]

    @pl.when(lower)
    def _():
        ring_adj[...] = adj[0:quarter, 1]
        ring_fwd[...] = fwd[0:quarter, 1]

    @pl.when(jnp.logical_not(jump))
    def _():
        arrived(ring_adj, 15)
        arrived(ring_fwd, 1)

    weights_out[...] = weights_y
    remote(ring_adj, mid_adj, 21, half_way).start()
    remote(ring_fwd, mid_fwd, 22, across).start()
    remote(weights_out, mid_weights, 23, half_way).start()

    cell = dof[...]

    @pl.when(leads)
    def _():
        cell_x, cell_y = lax.shift_right_logical(cell, 10), lax.bitwise_and(cell, 1023)
        lane = lax.bitwise_and(cell_x, 7) * 16 + lax.bitwise_and(cell_y, 15)
        cell_gx, cell_yz = lax.shift_right_logical(cell_x, 3), lax.shift_right_logical(cell_y, 4)
        cell_row = (
            lax.bitwise_and(cell_gx, 3) * 64
            + lax.bitwise_and(lax.shift_right_logical(cell_yz, 1), 3) * 16
            + lax.shift_right_logical(cell_gx, 2) * 8
            + lax.shift_right_logical(cell_yz, 3)
        )
        row_of[...] = lax.bitwise_and(cell_yz, 1) * 256 + cell_row
        for tile in range(16):
            pattern = (iota((128, 256), 0) == lane[:, tile * 256 : tile * 256 + 256]).astype(F32).astype(BF16)
            one_hot[0:128, tile * 256 : tile * 256 + 256] = pattern
            one_hot[128:256, tile * 256 : tile * 256 + 256] = pattern

    cell_rank = iota((128, 1), 0)
    cell_id = (gx * 8 + lax.shift_right_logical(cell_rank, 4)) * 1024 + yz * 16 + lax.bitwise_and(cell_rank, 15)
    found = jnp.zeros((128, 128), F32)
    for tile in range(32):
        label = (iota((1, 128), 1) + (tile * 128 + 1)).astype(F32)
        found = found + jnp.where(cell[:, tile * 128 : tile * 128 + 128] == cell_id, label, 0.0)
    owner = jnp.sum(found, axis=1, keepdims=True).astype(jnp.int32) - 1
    owner_row = lax.shift_right_arithmetic(owner, 7)
    owner_lane = lax.bitwise_and(owner, 127)
    pick_row = (lax.bitwise_and(iota((128, 64), 1), 31) == owner_row).astype(F32).astype(BF16)

    def project(cells, rows):
        part = lax.dot_general(weights_z, cells, (((1,), (1,)), ((), ())), precision=HIGH, preferred_element_type=F32)
        return jnp.dot(part, rows, precision=HIGH, preferred_element_type=F32)

    z_first, z_last = iota((16, 128), 1) == 0, iota((16, 128), 1) == 127
    y_first, y_last = iota((16, 128), 0) == 0, iota((16, 128), 0) == 15

    def laplacian(field, k, i, left, right):
        value = field[k, i]
        total = field[k, i - 1] + field[k, i + 1]
        total = total + jnp.where(z_first, 0.0, pltpu.roll(value, 1, 1)) + jnp.where(z_last, 0.0, pltpu.roll(value, 127, 1))
        total = total + jnp.where(y_first, left, pltpu.roll(value, 1, 0)) + jnp.where(y_last, right, pltpu.roll(value, 15, 0))
        return total - 6.0 * value, value

    def correlate(i, carry):
        for k in range(comps):
            lap, _ = laplacian(fwd, k, i, 0.0, 0.0)
            carry = carry + adj[k, i] * lap
        return carry

    corr[0:16, :] = lax.fori_loop(1, 9, correlate, jnp.zeros((16, 128), F32))

    back_prev = remote(x_out.at[0], x_in.at[1], 10, (lax.max(gx - 1, 0), yz))
    back_next = remote(x_out.at[1], x_in.at[0], 11, (lax.min(gx + 1, 7), yz))

    def send_back(side, halo, sem, inner, copy):
        arrived(adj.at[:, halo], sem)
        product = plane
        for k in range(comps):
            product = product + adj[k, halo] * fwd[k, inner]
        x_out[side] = product
        copy.start()

    @pl.when(near_prev)
    def _():
        send_back(0, 0, 2, 1, back_prev)

    @pl.when(near_next)
    def _():
        send_back(1, 9, 20, 8, back_next)

    @pl.when(leads)
    def _():
        arrived(cols.at[:, pl.ds(0, 7)], 19)
        for core in (0, 1):
            surf[core, yx] = cols[core, :, 0, :]
        for dy in RING_OFFSETS:
            for dx in RING_OFFSETS:
                if (dy, dx) != (0, 0):
                    remote(surf.at[:, yx], surf.at[:, yx], 5, device_at(z, wrap(y + dy, 4), wrap(x + dx, 4), 1)).start()
        for core in (0, 1):
            taps_own = cols[core, 0:8, 1, :]
            for k in range(8):
                taps[k, x, core : core + 1, :] = taps_own[k : k + 1, :]
        for dx in (2, 1, 3):
            remote(taps.at[:, x], taps.at[:, x], 6, device_at(z, y, wrap(x + dx, 4), 1)).start()

    @pl.when(has_left)
    def _():
        arrived(y_in.at[0], 4)

    @pl.when(has_right)
    def _():
        arrived(y_in.at[1], 3)

    corr[16:24, :] = jnp.zeros((8, 128), F32)
    for side, row in ((0, 0), (1, 15)):
        edge = jnp.zeros((8, 128), F32)
        for k in range(comps):
            edge = edge + y_in[side, k] * fwd[k, 1:9, row, :]
        corr[16 + side : 17 + side, :] = jnp.sum(edge, axis=0, keepdims=True)

    knots_z, _, knots_y = coarse.shape
    material = jnp.zeros((16, 128), F32)
    for k in range(knots_z):
        knot = jnp.sum(weights_y[:, 0:knots_y] * coarse[k], axis=1, keepdims=True)
        material = material + knot * weights_z[k : k + 1, :]
    material = time_step * material

    def update(i):
        laps = []
        for k in range(comps):
            lap, _ = laplacian(adj, k, i, y_in[0, k, pl.ds(i - 1, 1), :], y_in[1, k, pl.ds(i - 1, 1), :])
            laps.append(lap)
        for k in range(comps):
            mixed = laps[k]
            for m in range(comps):
                mixed = mixed + coupling[k, m] * laps[m]
            value = adj[k, i]
            updated[k, i - 1] = value + material * mixed - (time_step * damping[0, k]) * value

    @pl.loop(2, 8)
    def _(i):
        update(i)

    arrived(mid_adj, 21)
    onward = remote(mid_adj, far_in, 16, across)
    onward.start()
    arrived(mid_fwd, 22)
    arrived(mid_weights, 23)
    product = plane
    for k in range(quarter):
        product = product + mid_adj[k] * mid_fwd[k]
    grad_c[0, 1] = project(product, mid_weights[...])

    @pl.when(near_prev)
    def _():
        arrived(x_in.at[0], 11)

    @pl.when(near_next)
    def _():
        arrived(x_in.at[1], 10)

    corr[0:16, :] = corr[0:16, :] + x_in[0] + x_in[1]
    rows = jnp.concatenate([weights_y, y_in[0, comps, 0:1, :], y_in[1, comps, 0:1, :], jnp.zeros((6, 128), F32)], axis=0)
    grad_c[0, 0] = project(corr[...], rows)

    from_mate = remote(grad_c.at[0], grad_c.at[1], 12, mate)
    pl.when(leads)(from_mate.start)

    flat_row = lax.div(yz, 2)

    @pl.when(leads)
    def _():
        arrived(taps.at[:, pl.ds(0, 3)], 6)
        for k in range(32):
            for core in (0, 1):
                taps_all[core, k : k + 1, :] = taps[k // 4, k % 4, core : core + 1, :]
        first, second = taps_all[0], taps_all[1]
        low_half = iota((32, 128), 1) < 64
        taps_all[0] = jnp.where(low_half, first, pltpu.roll(second, 64, 1))
        taps_all[1] = jnp.where(low_half, pltpu.roll(first, 64, 1), second)

        arrived(surf.at[:, pl.ds(0, 15)], 5)
        pl.semaphore_signal(credit, inc=1, device_id=mate, device_id_type=MESH)
        head, rest = split(surf[...].reshape(512, 128))
        samples = jnp.concatenate([head, rest], axis=1)
        for tile in range(16):
            lanes = slice(tile * 256, tile * 256 + 256)
            match = jnp.dot(samples, one_hot[:, lanes], preferred_element_type=F32)
            mine = jnp.sum(jnp.where(iota((512, 256), 0) == row_of[:, lanes], match, 0.0), axis=0, keepdims=True)
            picked[2 * tile : 2 * tile + 1, :] = mine[:, 0:128]
            picked[2 * tile + 1 : 2 * tile + 2, :] = mine[:, 128:256]
        impulse[...] = taps_all[0] * picked[...] + taps_all[1]
        flat = jnp.concatenate([impulse[k : k + 1, :] for k in range(32)], axis=1).astype(BF16)
        own_plate.wait()
        arrived(plt_buf.at[pl.ds(0, share)], 7)
        through = lax.dot_general(flat, plt_buf[...], (((1,), (1,)), ((), ())), preferred_element_type=F32)
        react[flat_row] = through + impulse[pl.ds(flat_row, 1), :]
        for dz in NEAR_OFFSETS:
            for dx in RING_OFFSETS:
                for core in (0, 1):
                    if (dz, dx, core) != (0, 0, 1):
                        target = device_at(wrap(z - dz, 16), y, wrap(x + dx, 4), core)
                        remote(react.at[flat_row], react.at[flat_row], 9, target).start()

    @pl.when(follows)
    def _():
        from_mate.wait_recv()
        grad_x[x] = grad_c[0] + grad_c[1]
        for dx in (2, 1, 3):
            remote(grad_x.at[x], grad_x.at[x], 13, device_at(z, y, wrap(x + dx, 4), c)).start()

    @pl.when(follows)
    def _():
        arrived(grad_x.at[pl.ds(0, 3)], 13)
        pl.semaphore_wait(credit, 1)
        both = (grad_x[0] + grad_x[1]) + (grad_x[2] + grad_x[3])
        grad_z[z_lo] = jnp.where(jump, both[0] + both[1], both[0])
        grad_far[...] = both[1]

        @pl.when(jnp.logical_not(jump))
        def _():
            for k in range(8):
                for core in (0, 1):
                    target = device_at(z_hi * 8 + k, jnp.where(z_hi == 0, 3, 0), x, core)
                    remote(grad_far, grad_far_in.at[z_lo * 3 + y - z_hi], 18, target).start()

        for d in (7, 6, 5, 4, 3, 2, 1, 0):
            for core in (0, 1):
                if (d, core) != (0, 0):
                    remote(grad_z.at[z_lo], grad_z.at[z_lo], 14, (gx, lax.rem(z_lo + d, 8) * 8 + x * 2 + core)).start()

    arrived(far_in, 16)
    for ring in range(4):
        part = pl.ds(ring * quarter, quarter)
        here = y == ring
        if ring != 0:
            pl.when(jnp.logical_and(here, z_hi == 1))(remote(far_in, adj.at[part, 0], 17, (z_hi * 4, yz)).start)
        if ring != 3:
            pl.when(jnp.logical_and(here, z_hi == 0))(remote(far_in, adj.at[part, 9], 17, (z_hi * 4 + 3, yz)).start)

    @pl.when(lower)
    def _():
        adj[0:quarter, 0] = far_in[...]

    @pl.when(upper)
    def _():
        adj[3 * quarter : 4 * quarter, 9] = far_in[...]

    @pl.when(lower)
    def _():
        arrived(adj.at[pl.ds(quarter, 3 * quarter), 0], 17)

    @pl.when(upper)
    def _():
        arrived(adj.at[pl.ds(0, 3 * quarter), 9], 17)

    @pl.loop(0, 2)
    def _(side):
        update(1 + 7 * side)

    @pl.when(follows)
    def _():
        arrived(react, 9)

    @pl.when(leads)
    def _():
        arrived(react.at[pl.ds(0, 31)], 9)

    own_row = react[flat_row]
    reaction[...] = jnp.where(follows, own_row[:, 0:64], own_row[:, 64:128])
    head, rest = split(react[...].reshape(32, 128))
    forces = jnp.dot(pick_row, jnp.concatenate([head, rest], axis=0), preferred_element_type=F32)
    forces = jnp.sum(jnp.where(iota((128, 128), 1) == owner_lane, forces, 0.0), axis=1, keepdims=True)
    forces = (time_step * surface_gain) * forces.reshape(8, 16, 1)
    updated[2] = updated[2] + jnp.where(iota((8, 16, 128), 2) == 0, forces, 0.0)

    @pl.when(leads)
    def _():
        arrived(grad_z, 14)

    @pl.when(follows)
    def _():
        arrived(grad_z.at[pl.ds(0, 7)], 14)

    total = grad_z[0]
    for k in range(1, 8):
        total = total + grad_z[k]

    def put(values):
        values = values / (grad_norm * 4096.0**0.5)
        for k in range(knots_z):
            grad[k] = values[k : k + 1, 0:knots_y]

    @pl.when(jnp.logical_not(jump))
    def _():
        put(total)

    @pl.when(jump)
    def _():
        arrived(grad_far_in, 18)
        put(total + jnp.sum(grad_far_in[...], axis=0))

    @pl.when(leads)
    def _():
        sent(cols.at[1, pl.ds(0, 8)], 0)
        sent(cols.at[:, pl.ds(0, 7)], 19)
        sent(surf.at[:, pl.ds(0, 15)], 5)
        sent(taps.at[:, pl.ds(0, 3)], 6)
        sent(react.at[pl.ds(0, 31)], 9)
        sent(react, 9)
        from_mate.wait_send()

    @pl.when(follows)
    def _():
        sent(cols.at[0, pl.ds(0, 9)], 24)
        sent(plt_buf.at[pl.ds(0, share)], 7)
        sent(grad_x.at[pl.ds(0, 3)], 13)
        sent(grad_far_in.at[pl.ds(0, 15)], 14)

        @pl.when(jnp.logical_not(jump))
        def _():
            sent(grad_far_in.at[pl.ds(0, 16)], 18)

    sent(far_in, 16)
    sent(ring_adj, 21)
    sent(ring_fwd, 22)
    sent(weights_out, 23)
    for present, copy in (
        (near_prev, to_prev), (near_next, to_next), (has_left, to_left), (has_right, to_right),
        (near_prev, back_prev), (near_next, back_next),
    ):
        pl.when(present)(copy.wait_send)


    @pl.when(jump)
    def _():
        sent(adj.at[pl.ds(0, 3 * quarter), 0], 15)
        sent(adj.at[pl.ds(0, 3 * quarter), 0], 1)

    @pl.when(jnp.logical_not(jump))
    def _():
        sent(far_in, 17)


def store_results(*refs):
    count = len(refs) // 2
    copies = [pltpu.make_async_copy(refs[k], refs[count + k], refs[-1].at[k]) for k in range(count)]
    for copy in copies:
        copy.start()
    for copy in copies:
        copy.wait()


def on_device(adjoint, forward, coarse_model, knot_span, knot_frac, dof_cell, impedance, history, plate, coupling, damping):
    comps, cells_x, cells_y, depth = adjoint.shape
    knots_y, knots_z = coarse_model.shape[1:]
    vmem = pl.BlockSpec(memory_space=pltpu.VMEM)
    hbm = pl.BlockSpec(memory_space=pltpu.HBM)
    updated, grad, reaction = pl.pallas_call(
        kernel,
        out_shape=(
            jax.ShapeDtypeStruct(adjoint.shape, F32),
            jax.ShapeDtypeStruct((knots_z, 1, knots_y), F32),
            jax.ShapeDtypeStruct((1, 64), F32),
        ),
        in_specs=[hbm] * 11,
        out_specs=(vmem, vmem, vmem),
        scratch_shapes=[
            pltpu.VMEM((knots_z, 1, knots_y), F32),
            pltpu.VMEM((1, cells_y), jnp.int32),
            pltpu.VMEM((1, cells_y), F32),
            pltpu.VMEM((1, dof_cell.size), jnp.int32),
            pltpu.VMEM(impedance.shape, F32),
            pltpu.VMEM(history.shape, F32),
            pltpu.SMEM(coupling.shape, F32),
            pltpu.SMEM((1, comps), F32),
            pltpu.VMEM((comps, cells_x + 2, cells_y, depth), F32),
            pltpu.VMEM((comps, cells_x + 2, cells_y, depth), F32),
            pltpu.VMEM((2 * plate.shape[0], plate.shape[1]), BF16),
            pltpu.VMEM((2, 16, 2, 128), F32),
            pltpu.VMEM((2, 16, 16, 128), F32),
            pltpu.VMEM((8, 4, 2, 128), F32),
            pltpu.VMEM((2, 32, 128), F32),
            pltpu.VMEM((32, 128), F32),
            pltpu.VMEM((32, 128), F32),
            pltpu.VMEM((256, 4096), BF16),
            pltpu.VMEM((1, 4096), jnp.int32),
            pltpu.VMEM((32, 1, 128), F32),
            pltpu.VMEM((2, comps + 1, 8, 128), F32),
            pltpu.VMEM((2, comps + 1, 8, 128), F32),
            pltpu.VMEM((24, 128), F32),
            pltpu.VMEM((2, 16, 128), F32),
            pltpu.VMEM((2, 16, 128), F32),
            pltpu.VMEM((2, 2, 8, 128), F32),
            pltpu.VMEM((4, 2, 8, 128), F32),
            pltpu.VMEM((8, 8, 128), F32),
            pltpu.VMEM((comps // 4, cells_y, depth), F32),
            pltpu.VMEM((comps // 4, cells_y, depth), F32),
            pltpu.VMEM((comps // 4, cells_y, depth), F32),
            pltpu.VMEM((comps // 4, cells_y, depth), F32),
            pltpu.VMEM((cells_y, depth), F32),
            pltpu.VMEM((cells_y, depth), F32),
            pltpu.VMEM((comps // 4, cells_y, depth), F32),
            pltpu.VMEM((8, 128), F32),
            pltpu.VMEM((24, 8, 128), F32),
            pltpu.SemaphoreType.DMA((16,)),
            pltpu.SemaphoreType.DMA((25,)),
            pltpu.SemaphoreType.DMA((25,)),
            pltpu.SemaphoreType.REGULAR,
        ],
        compiler_params=pltpu.CompilerParams(collective_id=0, has_side_effects=True, vmem_limit_bytes=VMEM_BYTES),
        name="adjoint_step",
    )(
        *[
            pltpu.with_memory_space_constraint(operand, pltpu.HBM)
            for operand in (
                adjoint, forward, coarse_model.transpose(2, 0, 1), knot_span.reshape(1, -1), knot_frac.reshape(1, -1),
                dof_cell.reshape(1, -1), impedance, history, plate, coupling, damping.reshape(1, -1),
            )
        ]
    )
    results = (updated, grad, reaction)
    updated, grad, reaction = pl.pallas_call(
        store_results,
        out_shape=tuple(jax.ShapeDtypeStruct(a.shape, a.dtype) for a in results),
        in_specs=[vmem] * 3,
        out_specs=(hbm,) * 3,
        scratch_shapes=[pltpu.SemaphoreType.DMA((3,))],
        compiler_params=pltpu.CompilerParams(vmem_limit_bytes=STORE_VMEM_BYTES),
        name="store_results",
    )(*results)
    return updated, grad.transpose(1, 2, 0), reaction.reshape(-1)


def solution(mesh):
    return jax.shard_map(
        on_device,
        mesh=mesh,
        in_specs=(
            P(None, "gx", "yz", None),
            P(None, "gx", "yz", None),
            P("gx", None, None),
            P("yz"),
            P("yz"),
            P(),
            P(None, "yz"),
            P(None, "yz"),
            P("yz", None),
            P(),
            P(),
        ),
        out_specs=(P(None, "gx", "yz", None), P("gx", None, None), P("yz")),
        check_vma=False,
    )
```

```python
import functools

import jax
import jax.numpy as jnp
from jax import lax
from jax.experimental import pallas as pl
from jax.experimental.pallas import tpu as pltpu
from jax.sharding import PartitionSpec as P

MESH = pl.DeviceIdType.MESH
F32 = jnp.float32
BF16 = jnp.bfloat16
HIGH = lax.Precision.HIGHEST

HZ = 32
VMEM_BYTES = 16 * 1024 * 1024
STORE_VMEM_BYTES = 4 * 1024 * 1024
time_step = 0.1
surface_gain = 40.0
grad_norm = 20.0

NEAR_OFFSETS = tuple(sorted(range(-4, 4), key=lambda d: -abs(d)))
RING_OFFSETS = (2, 1, 3, 0)
Z_NEAR = (4, -4, 3, -3, 2, -2, 1, -1)


def bspline_weights(param):
    inverse = 1.0 - param
    return (
        inverse**3 / 6.0,
        (3.0 * param**3 - 6.0 * param**2 + 4.0) / 6.0,
        (-3.0 * param**3 + 3.0 * param**2 + 3.0 * param + 1.0) / 6.0,
        param**3 / 6.0,
    )


def spread_basis(index, span, param):
    total = 0.0
    for shift, weight in enumerate(bspline_weights(param)):
        total = total + jnp.where(index == span + shift, weight, 0.0)
    return total


def iota(shape, dim):
    return lax.broadcasted_iota(jnp.int32, shape, dim)


def split(values):
    head = values.astype(BF16)
    return head, (values - head.astype(F32)).astype(BF16)


def device_at(z, y, x, c):
    return (lax.div(z, 8) * 4 + y, lax.rem(z, 8) * 8 + x * 2 + c)


def wrap(value, count):
    return lax.rem(value + 2 * count, count)


def kernel(
    adjoint, forward, coarse_hbm, span_hbm, frac_hbm, dof_hbm, impedance_hbm, history_hbm, plate, coupling_hbm, damping_hbm,
    updated, grad, reaction,
    coarse, span, frac, dof, impedance, history, coupling, damping,
    adj, fwd, plt_buf, cols, taps, taps_all, picked, impulse, one_hot, row_of, react,
    y_out, y_in, corr, x_out, x_in, grad_c, grad_x, grad_z, ring_adj, ring_fwd, mid_adj, mid_fwd, mid_weights, weights_out, far_in, grad_plane,
    load_sems, send_sems, recv_sems,
):
    gx, yz = lax.axis_index("gx"), lax.axis_index("yz")
    z_hi, y = lax.div(gx, 4), lax.rem(gx, 4)
    z_lo, x, c = lax.div(yz, 8), lax.rem(lax.div(yz, 2), 4), lax.rem(yz, 2)
    z = z_hi * 8 + z_lo
    yx = y * 4 + x
    comps = adj.shape[0]
    has_prev, has_next = gx > 0, gx < 7
    has_left, has_right = yz > 0, yz < 63
    mate = (gx, yz + 1 - 2 * c)

    upper, lower = jnp.logical_and(z_hi == 0, y == 3), jnp.logical_and(z_hi == 1, y == 0)
    jump = jnp.logical_or(upper, lower)
    near_prev, near_next = jnp.logical_and(has_prev, jnp.logical_not(lower)), jnp.logical_and(has_next, jnp.logical_not(upper))
    z_half = lax.rem(z_lo + 4, 8)
    half_way, across = z_hi * 8 + z_half, (1 - z_hi) * 8 + z_half
    far_y = jnp.where(z_hi == 0, 3, 0)

    loads = [
        pltpu.make_async_copy(adjoint.at[2], adj.at[2, pl.ds(1, 8)], load_sems.at[0]),
        pltpu.make_async_copy(impedance_hbm, impedance, load_sems.at[8]),
        pltpu.make_async_copy(history_hbm, history, load_sems.at[9]),
        pltpu.make_async_copy(adjoint.at[pl.ds(0, 2)], adj.at[pl.ds(0, 2), pl.ds(1, 8)], load_sems.at[1]),
        pltpu.make_async_copy(adjoint.at[pl.ds(3, 9)], adj.at[pl.ds(3, 9), pl.ds(1, 8)], load_sems.at[2]),
        pltpu.make_async_copy(forward, fwd.at[:, pl.ds(1, 8)], load_sems.at[3]),
        pltpu.make_async_copy(coarse_hbm, coarse, load_sems.at[10]),
        pltpu.make_async_copy(span_hbm, span, load_sems.at[11]),
        pltpu.make_async_copy(frac_hbm, frac, load_sems.at[12]),
        pltpu.make_async_copy(dof_hbm, dof, load_sems.at[13]),
        pltpu.make_async_copy(coupling_hbm, coupling, load_sems.at[14]),
        pltpu.make_async_copy(damping_hbm, damping, load_sems.at[15]),
    ]
    for load in loads:
        load.start()
    leads, follows = c == 1, c == 0
    share = plate.shape[0]
    own_plate = pltpu.make_async_copy(plate, plt_buf.at[pl.ds(share, share)], load_sems.at[4])
    pl.when(leads)(own_plate.start)

    barrier = pltpu.get_barrier_semaphore()

    def greet(device):
        pl.semaphore_signal(barrier, inc=1, device_id=device, device_id_type=MESH)

    greeted = jnp.where(leads, 24, 26) + has_left.astype(jnp.int32) + has_right.astype(jnp.int32)

    @pl.when(leads)
    def _():
        for d in Z_NEAR:
            greet(device_at(wrap(z + d, 16), y, x, 1))
            greet(device_at(wrap(z + d, 16), y, x, 0))

    @pl.when(follows)
    def _():
        for d in (4, -4):
            greet(device_at(wrap(z + d, 16), y, x, 0))

    for dy in RING_OFFSETS:
        for dx in RING_OFFSETS:
            if (dy, dx) != (0, 0):
                greet(device_at(z, wrap(y + dy, 4), wrap(x + dx, 4), c))
    greet(mate)

    @pl.when(has_left)
    def _():
        greet((gx, yz - 1))

    @pl.when(has_right)
    def _():
        greet((gx, yz + 1))

    loads[1].wait()
    loads[2].wait()
    tail = jnp.sum(impedance[1:, :] * history[...], axis=0, keepdims=True)
    cols[c, z, 1:2, :] = jnp.concatenate([impedance[0:1, :], tail], axis=1)
    loads[0].wait()
    surface = adj[2, 1:9].reshape(128, 128)
    cols[c, z, 0:1, :] = jnp.transpose(surface)[0:1, :]

    pl.semaphore_wait(barrier, greeted)

    def remote(src, dst, sem, device):
        return pltpu.make_async_remote_copy(
            src_ref=src, dst_ref=dst, send_sem=send_sems.at[sem], recv_sem=recv_sems.at[sem], device_id=device, device_id_type=MESH
        )

    def arrived(ref, sem):
        pltpu.make_async_copy(ref, ref, recv_sems.at[sem]).wait()

    def sent(ref, sem):
        pltpu.make_async_copy(ref, ref, send_sems.at[sem]).wait()

    for core, sem in ((1, 0), (0, 24)):
        for d in Z_NEAR:
            pl.when(c == core)(remote(cols.at[core, z], cols.at[core, z], sem, device_at(wrap(z + d, 16), y, x, 1)).start)
    plate_up = remote(plate, plt_buf.at[pl.ds(0, share)], 7, mate)

    @pl.when(follows)
    def _():
        remote(cols.at[0, z], cols.at[0, z], 24, mate).start()
        plate_up.start()

    quarter = comps // 4
    for field, buffer, sem in ((adjoint, ring_adj, 15), (forward, ring_fwd, 1)):
        for ring in range(4):
            part = pl.ds(ring * quarter, quarter)
            if ring != 3:
                pl.when(upper)(remote(field.at[part, 7], buffer, sem, (z_hi * 4 + ring, yz)).start)
            if ring != 0:
                pl.when(lower)(remote(field.at[part, 0], buffer, sem, (z_hi * 4 + ring, yz)).start)

    for load in loads[3:]:
        load.wait()
    to_prev = remote(adj.at[:, 1], adj.at[:, 9], 20, (lax.max(gx - 1, 0), yz))
    to_next = remote(adj.at[:, 8], adj.at[:, 0], 2, (lax.min(gx + 1, 7), yz))

    @pl.when(near_prev)
    def _():
        to_prev.start()

    @pl.when(near_next)
    def _():
        to_next.start()

    @pl.when(leads)
    def _():
        arrived(cols.at[1, pl.ds(0, 8)], 0)
        arrived(cols.at[0, pl.ds(0, 9)], 24)
        for d, way in ((4, -4), (3, -4), (2, -4), (1, -4), (-3, 4), (-2, 4), (-1, 4)):
            slot = wrap(z + d, 16)
            remote(cols.at[:, slot], cols.at[:, slot], 19, device_at(wrap(z + way, 16), y, x, 1)).start()

    plane = jnp.zeros((16, 128), F32)
    for k in range(comps):
        fwd[k, 0] = plane
        fwd[k, 9] = plane

    @pl.when(gx == 0)
    def _():
        for k in range(comps):
            adj[k, 0] = plane

    @pl.when(gx == 7)
    def _():
        for k in range(comps):
            adj[k, 9] = plane

    @pl.when(jnp.logical_not(near_prev))
    def _():
        x_in[0] = plane

    @pl.when(jnp.logical_not(near_next))
    def _():
        x_in[1] = plane

    diagonal = iota((16, 16), 0) == iota((16, 16), 1)
    span_col = jnp.sum(jnp.where(diagonal, span[...], 0), axis=1, keepdims=True)
    frac_col = jnp.sum(jnp.where(diagonal, frac[...], 0.0), axis=1, keepdims=True)
    weights_y = spread_basis(iota((16, 128), 1), span_col, frac_col)
    depth = iota((8, 128), 1)
    depth_span = lax.div(depth, HZ)
    weights_z = spread_basis(iota((8, 128), 0), depth_span, (depth.astype(F32) + 0.5) / HZ - depth_span.astype(F32))

    for side, row in ((0, 0), (1, 15)):
        for k in range(comps):
            y_out[side, k] = adj[k, 1:9, row, :]
        y_out[side, comps] = jnp.broadcast_to(weights_y[row : row + 1, :], (8, 128))
    to_left = remote(y_out.at[0], y_in.at[1], 3, (gx, lax.max(yz - 1, 0)))
    to_right = remote(y_out.at[1], y_in.at[0], 4, (gx, lax.min(yz + 1, 63)))

    @pl.when(has_left)
    def _():
        to_left.start()

    @pl.when(has_right)
    def _():
        to_right.start()

    @pl.when(yz == 0)
    def _():
        y_in[0] = jnp.zeros_like(y_in[0])

    @pl.when(yz == 63)
    def _():
        y_in[1] = jnp.zeros_like(y_in[1])

    @pl.when(upper)
    def _():
        ring_adj[...] = adj[3 * quarter : 4 * quarter, 8]
        ring_fwd[...] = fwd[3 * quarter : 4 * quarter, 8]

    @pl.when(lower)
    def _():
        ring_adj[...] = adj[0:quarter, 1]
        ring_fwd[...] = fwd[0:quarter, 1]

    @pl.when(jnp.logical_not(jump))
    def _():
        arrived(ring_adj, 15)
        arrived(ring_fwd, 1)

    weights_out[...] = weights_y
    remote(ring_adj, mid_adj.at[c], 21, device_at(half_way, y, x, 0)).start()
    remote(ring_fwd, mid_fwd.at[c], 22, device_at(across, y, x, 0)).start()
    remote(weights_out, mid_weights.at[c], 23, device_at(half_way, y, x, 0)).start()

    cell = dof[...]

    @pl.when(leads)
    def _():
        cell_x, cell_y = lax.shift_right_logical(cell, 10), lax.bitwise_and(cell, 1023)
        lane = lax.bitwise_and(cell_x, 7) * 16 + lax.bitwise_and(cell_y, 15)
        cell_gx, cell_yz = lax.shift_right_logical(cell_x, 3), lax.shift_right_logical(cell_y, 4)
        in_column = jnp.logical_and(lax.bitwise_and(cell_gx, 3) == y, lax.bitwise_and(lax.shift_right_logical(cell_yz, 1), 3) == x)
        depth_of = lax.shift_right_logical(cell_gx, 2) * 8 + lax.shift_right_logical(cell_yz, 3)
        row_of[...] = jnp.where(in_column, depth_of, -1)
        lane = lax.bitwise_and(cell_yz, 1) * 128 + lane
        for tile in range(16):
            lanes = slice(tile * 256, tile * 256 + 256)
            one_hot[:, lanes] = (iota((256, 256), 0) == lane[:, lanes]).astype(F32).astype(BF16)

    cell_rank = iota((128, 1), 0)
    cell_id = (gx * 8 + lax.shift_right_logical(cell_rank, 4)) * 1024 + yz * 16 + lax.bitwise_and(cell_rank, 15)
    found = jnp.zeros((128, 128), F32)
    for tile in range(32):
        label = (iota((1, 128), 1) + (tile * 128 + 1)).astype(F32)
        found = found + jnp.where(cell[:, tile * 128 : tile * 128 + 128] == cell_id, label, 0.0)
    owner = jnp.sum(found, axis=1, keepdims=True).astype(jnp.int32) - 1
    owner_row = lax.shift_right_arithmetic(owner, 7)
    owner_lane = lax.bitwise_and(owner, 127)
    pick_row = (lax.bitwise_and(iota((128, 64), 1), 31) == owner_row).astype(F32).astype(BF16)

    def project(cells, rows):
        part = lax.dot_general(weights_z, cells, (((1,), (1,)), ((), ())), precision=HIGH, preferred_element_type=F32)
        return jnp.dot(part, rows, precision=HIGH, preferred_element_type=F32)

    z_first, z_last = iota((16, 128), 1) == 0, iota((16, 128), 1) == 127
    y_first, y_last = iota((16, 128), 0) == 0, iota((16, 128), 0) == 15

    def laplacian(field, k, i, left, right):
        value = field[k, i]
        total = field[k, i - 1] + field[k, i + 1]
        total = total + jnp.where(z_first, 0.0, pltpu.roll(value, 1, 1)) + jnp.where(z_last, 0.0, pltpu.roll(value, 127, 1))
        total = total + jnp.where(y_first, left, pltpu.roll(value, 1, 0)) + jnp.where(y_last, right, pltpu.roll(value, 15, 0))
        return total - 6.0 * value, value

    def correlate(i, carry):
        for k in range(comps):
            lap, _ = laplacian(fwd, k, i, 0.0, 0.0)
            carry = carry + adj[k, i] * lap
        return carry

    corr[0:16, :] = lax.fori_loop(1, 9, correlate, jnp.zeros((16, 128), F32))

    back_prev = remote(x_out.at[0], x_in.at[1], 10, (lax.max(gx - 1, 0), yz))
    back_next = remote(x_out.at[1], x_in.at[0], 11, (lax.min(gx + 1, 7), yz))

    def send_back(side, halo, sem, inner, copy):
        arrived(adj.at[:, halo], sem)
        product = plane
        for k in range(comps):
            product = product + adj[k, halo] * fwd[k, inner]
        x_out[side] = product
        copy.start()

    @pl.when(near_prev)
    def _():
        send_back(0, 0, 2, 1, back_prev)

    @pl.when(near_next)
    def _():
        send_back(1, 9, 20, 8, back_next)

    @pl.when(leads)
    def _():
        arrived(cols.at[:, pl.ds(0, 7)], 19)
        cells = jnp.concatenate(split(jnp.concatenate([cols[0, :, 0, :], cols[1, :, 0, :]], axis=1)), axis=0)
        for tile in range(16):
            lanes = slice(tile * 256, tile * 256 + 256)
            match = jnp.dot(cells, one_hot[:, lanes], preferred_element_type=F32)
            match = jnp.where(iota((16, 256), 0) == row_of[:, lanes], match[:16] + match[16:], 0.0)
            mine = jnp.sum(match, axis=0, keepdims=True)
            picked[yx, 2 * tile : 2 * tile + 1, :] = mine[:, 0:128]
            picked[yx, 2 * tile + 1 : 2 * tile + 2, :] = mine[:, 128:256]
        for dy in RING_OFFSETS:
            for dx in RING_OFFSETS:
                if (dy, dx) != (0, 0):
                    remote(picked.at[yx], picked.at[yx], 5, device_at(z, wrap(y + dy, 4), wrap(x + dx, 4), 1)).start()
        for core in (0, 1):
            taps_own = cols[core, 0:8, 1, :]
            for k in range(8):
                taps[k, x, core : core + 1, :] = taps_own[k : k + 1, :]
        for dx in (2, 1, 3):
            remote(taps.at[:, x], taps.at[:, x], 6, device_at(z, y, wrap(x + dx, 4), 1)).start()

    @pl.when(has_left)
    def _():
        arrived(y_in.at[0], 4)

    @pl.when(has_right)
    def _():
        arrived(y_in.at[1], 3)

    corr[16:24, :] = jnp.zeros((8, 128), F32)
    for side, row in ((0, 0), (1, 15)):
        edge = jnp.zeros((8, 128), F32)
        for k in range(comps):
            edge = edge + y_in[side, k] * fwd[k, 1:9, row, :]
        corr[16 + side : 17 + side, :] = jnp.sum(edge, axis=0, keepdims=True)

    @pl.when(near_prev)
    def _():
        arrived(x_in.at[0], 11)

    @pl.when(near_next)
    def _():
        arrived(x_in.at[1], 10)

    corr[0:16, :] = corr[0:16, :] + x_in[0] + x_in[1]
    rows = jnp.concatenate([weights_y, y_in[0, comps, 0:1, :], y_in[1, comps, 0:1, :], jnp.zeros((6, 128), F32)], axis=0)
    grad_c[0] = project(corr[...], rows)

    from_mate = remote(grad_c.at[0], grad_c.at[1], 12, mate)
    pl.when(leads)(from_mate.start)

    @pl.when(follows)
    def _():
        from_mate.wait_recv()
        grad_x[x] = grad_c[0] + grad_c[1]
        for dx in (2, 1, 3):
            remote(grad_x.at[x], grad_x.at[x], 13, device_at(z, y, wrap(x + dx, 4), 0)).start()
        arrived(mid_adj, 21)
        for core in (0, 1):
            remote(mid_adj.at[core], far_in, 16, device_at(across, y, x, core)).start()
        arrived(mid_fwd, 22)
        arrived(mid_weights, 23)
        far_part = jnp.zeros((8, 128), F32)
        for core in (0, 1):
            product = plane
            for k in range(quarter):
                product = product + mid_adj[core, k] * mid_fwd[core, k]
            far_part = far_part + project(product, mid_weights[core])
        grad_plane[yx] = far_part
        for k in range(4):
            target = remote(grad_plane.at[yx], grad_plane.at[yx], 18, device_at(z, far_y, k, 0))
            pl.when(jnp.logical_not(jnp.logical_and(jump, x == k)))(target.start)

    def sum_over_z():
        arrived(grad_x.at[pl.ds(0, 3)], 13)
        grad_z[z_lo] = (grad_x[0] + grad_x[1]) + (grad_x[2] + grad_x[3])

        @pl.when(jump)
        def _():
            arrived(grad_plane.at[pl.ds(0, 15)], 18)
            grad_z[z_lo] = grad_z[z_lo] + jnp.sum(grad_plane[...], axis=0)

        for d in (7, 6, 5, 4, 3, 2, 1, 0):
            for core in (0, 1):
                if (d, core) != (0, 0):
                    remote(grad_z.at[z_lo], grad_z.at[z_lo], 14, (gx, lax.rem(z_lo + d, 8) * 8 + x * 2 + core)).start()

    pl.when(jnp.logical_and(follows, jnp.logical_not(jump)))(sum_over_z)

    knots_z, _, knots_y = coarse.shape
    material = jnp.zeros((16, 128), F32)
    for k in range(knots_z):
        knot = jnp.sum(weights_y[:, 0:knots_y] * coarse[k], axis=1, keepdims=True)
        material = material + knot * weights_z[k : k + 1, :]
    material = time_step * material

    def update(i):
        laps = []
        for k in range(comps):
            lap, _ = laplacian(adj, k, i, y_in[0, k, pl.ds(i - 1, 1), :], y_in[1, k, pl.ds(i - 1, 1), :])
            laps.append(lap)
        for k in range(comps):
            mixed = laps[k]
            for m in range(comps):
                mixed = mixed + coupling[k, m] * laps[m]
            value = adj[k, i]
            updated[k, i - 1] = value + material * mixed - (time_step * damping[0, k]) * value

    @pl.loop(2, 8)
    def _(i):
        update(i)

    pl.when(jnp.logical_and(follows, jump))(sum_over_z)

    flat_row = lax.div(yz, 2)

    @pl.when(leads)
    def _():
        arrived(taps.at[:, pl.ds(0, 3)], 6)
        for k in range(32):
            for core in (0, 1):
                taps_all[core, k : k + 1, :] = taps[k // 4, k % 4, core : core + 1, :]
        first, second = taps_all[0], taps_all[1]
        low_half = iota((32, 128), 1) < 64
        taps_all[0] = jnp.where(low_half, first, pltpu.roll(second, 64, 1))
        taps_all[1] = jnp.where(low_half, pltpu.roll(first, 64, 1), second)

        arrived(picked.at[pl.ds(0, 15)], 5)
        samples = picked[0]
        for k in range(1, 16):
            samples = samples + picked[k]
        impulse[...] = taps_all[0] * samples + taps_all[1]
        flat = jnp.concatenate([impulse[k : k + 1, :] for k in range(32)], axis=1).astype(BF16)
        own_plate.wait()
        arrived(plt_buf.at[pl.ds(0, share)], 7)
        through = lax.dot_general(flat, plt_buf[...], (((1,), (1,)), ((), ())), preferred_element_type=F32)
        react[flat_row] = through + impulse[pl.ds(flat_row, 1), :]
        for dz in NEAR_OFFSETS:
            for dx in RING_OFFSETS:
                for core in (0, 1):
                    if (dz, dx, core) != (0, 0, 1):
                        target = device_at(wrap(z - dz, 16), y, wrap(x + dx, 4), core)
                        remote(react.at[flat_row], react.at[flat_row], 9, target).start()

    arrived(far_in, 16)
    for ring in range(4):
        part = pl.ds(ring * quarter, quarter)
        here = y == ring
        if ring != 0:
            pl.when(jnp.logical_and(here, z_hi == 1))(remote(far_in, adj.at[part, 0], 17, (z_hi * 4, yz)).start)
        if ring != 3:
            pl.when(jnp.logical_and(here, z_hi == 0))(remote(far_in, adj.at[part, 9], 17, (z_hi * 4 + 3, yz)).start)

    @pl.when(lower)
    def _():
        adj[0:quarter, 0] = far_in[...]

    @pl.when(upper)
    def _():
        adj[3 * quarter : 4 * quarter, 9] = far_in[...]

    @pl.when(lower)
    def _():
        arrived(adj.at[pl.ds(quarter, 3 * quarter), 0], 17)

    @pl.when(upper)
    def _():
        arrived(adj.at[pl.ds(0, 3 * quarter), 9], 17)

    @pl.loop(0, 2)
    def _(side):
        update(1 + 7 * side)

    @pl.when(follows)
    def _():
        arrived(react, 9)

    @pl.when(leads)
    def _():
        arrived(react.at[pl.ds(0, 31)], 9)

    own_row = react[flat_row]
    reaction[...] = jnp.where(follows, own_row[:, 0:64], own_row[:, 64:128])
    head, rest = split(react[...].reshape(32, 128))
    forces = jnp.dot(pick_row, jnp.concatenate([head, rest], axis=0), preferred_element_type=F32)
    forces = jnp.sum(jnp.where(iota((128, 128), 1) == owner_lane, forces, 0.0), axis=1, keepdims=True)
    forces = (time_step * surface_gain) * forces.reshape(8, 16, 1)
    updated[2] = updated[2] + jnp.where(iota((8, 16, 128), 2) == 0, forces, 0.0)

    @pl.when(leads)
    def _():
        arrived(grad_z, 14)

    @pl.when(follows)
    def _():
        arrived(grad_z.at[pl.ds(0, 7)], 14)

    total = grad_z[0]
    for k in range(1, 8):
        total = total + grad_z[k]

    total = total / (grad_norm * 4096.0**0.5)
    for k in range(knots_z):
        grad[k] = total[k : k + 1, 0:knots_y]

    @pl.when(leads)
    def _():
        sent(cols.at[1, pl.ds(0, 8)], 0)
        sent(cols.at[:, pl.ds(0, 7)], 19)
        sent(picked.at[pl.ds(0, 15)], 5)
        sent(taps.at[:, pl.ds(0, 3)], 6)
        sent(react.at[pl.ds(0, 31)], 9)
        sent(react, 9)
        from_mate.wait_send()

    @pl.when(follows)
    def _():
        sent(cols.at[0, pl.ds(0, 9)], 24)
        sent(plt_buf.at[pl.ds(0, share)], 7)
        sent(grad_x.at[pl.ds(0, 3)], 13)
        sent(grad_plane.at[pl.ds(0, 15)], 14)
        sent(grad_plane.at[pl.ds(0, 3)], 18)
        pl.when(jnp.logical_not(jump))(lambda: sent(grad_plane.at[0], 18))
        sent(mid_adj, 16)

    sent(ring_adj, 21)
    sent(ring_fwd, 22)
    sent(weights_out, 23)
    for present, copy in (
        (near_prev, to_prev), (near_next, to_next), (has_left, to_left), (has_right, to_right),
        (near_prev, back_prev), (near_next, back_next),
    ):
        pl.when(present)(copy.wait_send)


    @pl.when(jump)
    def _():
        sent(adj.at[pl.ds(0, 3 * quarter), 0], 15)
        sent(adj.at[pl.ds(0, 3 * quarter), 0], 1)

    @pl.when(jnp.logical_not(jump))
    def _():
        sent(far_in, 17)


def store_results(*refs):
    count = len(refs) // 2
    copies = [pltpu.make_async_copy(refs[k], refs[count + k], refs[-1].at[k]) for k in range(count)]
    for copy in copies:
        copy.start()
    for copy in copies:
        copy.wait()


def on_device(adjoint, forward, coarse_model, knot_span, knot_frac, dof_cell, impedance, history, plate, coupling, damping):
    comps, cells_x, cells_y, depth = adjoint.shape
    knots_y, knots_z = coarse_model.shape[1:]
    vmem = pl.BlockSpec(memory_space=pltpu.VMEM)
    hbm = pl.BlockSpec(memory_space=pltpu.HBM)
    updated, grad, reaction = pl.pallas_call(
        kernel,
        out_shape=(
            jax.ShapeDtypeStruct(adjoint.shape, F32),
            jax.ShapeDtypeStruct((knots_z, 1, knots_y), F32),
            jax.ShapeDtypeStruct((1, 64), F32),
        ),
        in_specs=[hbm] * 11,
        out_specs=(vmem, vmem, vmem),
        scratch_shapes=[
            pltpu.VMEM((knots_z, 1, knots_y), F32),
            pltpu.VMEM((1, cells_y), jnp.int32),
            pltpu.VMEM((1, cells_y), F32),
            pltpu.VMEM((1, dof_cell.size), jnp.int32),
            pltpu.VMEM(impedance.shape, F32),
            pltpu.VMEM(history.shape, F32),
            pltpu.SMEM(coupling.shape, F32),
            pltpu.SMEM((1, comps), F32),
            pltpu.VMEM((comps, cells_x + 2, cells_y, depth), F32),
            pltpu.VMEM((comps, cells_x + 2, cells_y, depth), F32),
            pltpu.VMEM((2 * plate.shape[0], plate.shape[1]), BF16),
            pltpu.VMEM((2, 16, 2, 128), F32),
            pltpu.VMEM((8, 4, 2, 128), F32),
            pltpu.VMEM((2, 32, 128), F32),
            pltpu.VMEM((16, 32, 128), F32),
            pltpu.VMEM((32, 128), F32),
            pltpu.VMEM((256, 4096), BF16),
            pltpu.VMEM((1, 4096), jnp.int32),
            pltpu.VMEM((32, 1, 128), F32),
            pltpu.VMEM((2, comps + 1, 8, 128), F32),
            pltpu.VMEM((2, comps + 1, 8, 128), F32),
            pltpu.VMEM((24, 128), F32),
            pltpu.VMEM((2, 16, 128), F32),
            pltpu.VMEM((2, 16, 128), F32),
            pltpu.VMEM((2, 8, 128), F32),
            pltpu.VMEM((4, 8, 128), F32),
            pltpu.VMEM((8, 8, 128), F32),
            pltpu.VMEM((comps // 4, cells_y, depth), F32),
            pltpu.VMEM((comps // 4, cells_y, depth), F32),
            pltpu.VMEM((2, comps // 4, cells_y, depth), F32),
            pltpu.VMEM((2, comps // 4, cells_y, depth), F32),
            pltpu.VMEM((2, cells_y, depth), F32),
            pltpu.VMEM((cells_y, depth), F32),
            pltpu.VMEM((comps // 4, cells_y, depth), F32),
            pltpu.VMEM((16, 8, 128), F32),
            pltpu.SemaphoreType.DMA((16,)),
            pltpu.SemaphoreType.DMA((25,)),
            pltpu.SemaphoreType.DMA((25,)),
        ],
        compiler_params=pltpu.CompilerParams(collective_id=0, has_side_effects=True, vmem_limit_bytes=VMEM_BYTES),
        name="adjoint_step",
    )(
        *[
            pltpu.with_memory_space_constraint(operand, pltpu.HBM)
            for operand in (
                adjoint, forward, coarse_model.transpose(2, 0, 1), knot_span.reshape(1, -1), knot_frac.reshape(1, -1),
                dof_cell.reshape(1, -1), impedance, history, plate, coupling, damping.reshape(1, -1),
            )
        ]
    )
    results = (updated, grad, reaction)
    updated, grad, reaction = pl.pallas_call(
        store_results,
        out_shape=tuple(jax.ShapeDtypeStruct(a.shape, a.dtype) for a in results),
        in_specs=[vmem] * 3,
        out_specs=(hbm,) * 3,
        scratch_shapes=[pltpu.SemaphoreType.DMA((3,))],
        compiler_params=pltpu.CompilerParams(vmem_limit_bytes=STORE_VMEM_BYTES),
        name="store_results",
    )(*results)
    return updated, grad.transpose(1, 2, 0), reaction.reshape(-1)


def solution(mesh):
    return jax.shard_map(
        on_device,
        mesh=mesh,
        in_specs=(
            P(None, "gx", "yz", None),
            P(None, "gx", "yz", None),
            P("gx", None, None),
            P("yz"),
            P("yz"),
            P(),
            P(None, "yz"),
            P(None, "yz"),
            P("yz", None),
            P(),
            P(),
        ),
        out_specs=(P(None, "gx", "yz", None), P("gx", None, None), P("yz")),
        check_vma=False,
    )
```

```python
import functools

import jax
import jax.numpy as jnp
from jax import lax
from jax.experimental import pallas as pl
from jax.experimental.pallas import tpu as pltpu
from jax.sharding import PartitionSpec as P

MESH = pl.DeviceIdType.MESH
F32 = jnp.float32
BF16 = jnp.bfloat16
HIGH = lax.Precision.HIGHEST

HZ = 32
VMEM_BYTES = 16 * 1024 * 1024
STORE_VMEM_BYTES = 4 * 1024 * 1024
time_step = 0.1
surface_gain = 40.0
grad_norm = 20.0

NEAR_OFFSETS = tuple(sorted(range(-4, 4), key=lambda d: -abs(d)))
RING_OFFSETS = (2, 1, 3, 0)
Z_NEAR = (4, -4, 3, -3, 2, -2, 1, -1)


def bspline_weights(param):
    inverse = 1.0 - param
    return (
        inverse**3 / 6.0,
        (3.0 * param**3 - 6.0 * param**2 + 4.0) / 6.0,
        (-3.0 * param**3 + 3.0 * param**2 + 3.0 * param + 1.0) / 6.0,
        param**3 / 6.0,
    )


def spread_basis(index, span, param):
    total = 0.0
    for shift, weight in enumerate(bspline_weights(param)):
        total = total + jnp.where(index == span + shift, weight, 0.0)
    return total


def iota(shape, dim):
    return lax.broadcasted_iota(jnp.int32, shape, dim)


def split(values):
    head = values.astype(BF16)
    return head, (values - head.astype(F32)).astype(BF16)


def device_at(z, y, x, c):
    return (lax.div(z, 8) * 4 + y, lax.rem(z, 8) * 8 + x * 2 + c)


def wrap(value, count):
    return lax.rem(value + 2 * count, count)


def kernel(
    adjoint, forward, coarse_hbm, span_hbm, frac_hbm, dof_hbm, impedance_hbm, history_hbm, plate, coupling_hbm, damping_hbm,
    updated, grad, reaction,
    coarse, span, frac, dof, impedance, history, coupling, damping,
    adj, fwd, plt_buf, cols, taps, taps_all, picked, impulse, one_hot, row_of, react,
    y_out, y_in, corr, x_out, x_in, grad_c, grad_x, grad_z, ring_adj, ring_fwd, mid_adj, mid_fwd, mid_weights, weights_out, grad_plane,
    load_sems, send_sems, recv_sems,
):
    gx, yz = lax.axis_index("gx"), lax.axis_index("yz")
    z_hi, y = lax.div(gx, 4), lax.rem(gx, 4)
    z_lo, x, c = lax.div(yz, 8), lax.rem(lax.div(yz, 2), 4), lax.rem(yz, 2)
    z = z_hi * 8 + z_lo
    yx = y * 4 + x
    comps = adj.shape[0]
    has_prev, has_next = gx > 0, gx < 7
    has_left, has_right = yz > 0, yz < 63
    mate = (gx, yz + 1 - 2 * c)

    upper, lower = jnp.logical_and(z_hi == 0, y == 3), jnp.logical_and(z_hi == 1, y == 0)
    jump = jnp.logical_or(upper, lower)
    near_prev, near_next = jnp.logical_and(has_prev, jnp.logical_not(lower)), jnp.logical_and(has_next, jnp.logical_not(upper))
    z_half = lax.rem(z_lo + 4, 8)
    half_way, across = z_hi * 8 + z_half, (1 - z_hi) * 8 + z_half
    far_y = jnp.where(z_hi == 0, 3, 0)

    loads = [
        pltpu.make_async_copy(adjoint.at[2], adj.at[2, pl.ds(1, 8)], load_sems.at[0]),
        pltpu.make_async_copy(impedance_hbm, impedance, load_sems.at[8]),
        pltpu.make_async_copy(history_hbm, history, load_sems.at[9]),
        pltpu.make_async_copy(adjoint.at[pl.ds(0, 2)], adj.at[pl.ds(0, 2), pl.ds(1, 8)], load_sems.at[1]),
        pltpu.make_async_copy(adjoint.at[pl.ds(3, 9)], adj.at[pl.ds(3, 9), pl.ds(1, 8)], load_sems.at[2]),
        pltpu.make_async_copy(forward, fwd.at[:, pl.ds(1, 8)], load_sems.at[3]),
        pltpu.make_async_copy(coarse_hbm, coarse, load_sems.at[10]),
        pltpu.make_async_copy(span_hbm, span, load_sems.at[11]),
        pltpu.make_async_copy(frac_hbm, frac, load_sems.at[12]),
        pltpu.make_async_copy(dof_hbm, dof, load_sems.at[13]),
        pltpu.make_async_copy(coupling_hbm, coupling, load_sems.at[14]),
        pltpu.make_async_copy(damping_hbm, damping, load_sems.at[15]),
    ]
    for load in loads[:3]:
        load.start()
    leads, follows = c == 1, c == 0
    share = plate.shape[0]
    own_plate = pltpu.make_async_copy(plate, plt_buf.at[pl.ds(share, share)], load_sems.at[4])

    barrier = pltpu.get_barrier_semaphore()

    def greet(device):
        pl.semaphore_signal(barrier, inc=1, device_id=device, device_id_type=MESH)

    greeted = jnp.where(leads, 24, 26) + has_left.astype(jnp.int32) + has_right.astype(jnp.int32)

    @pl.when(leads)
    def _():
        for d in Z_NEAR:
            greet(device_at(wrap(z + d, 16), y, x, 1))
            greet(device_at(wrap(z + d, 16), y, x, 0))

    @pl.when(follows)
    def _():
        for d in (4, -4):
            greet(device_at(wrap(z + d, 16), y, x, 0))

    for dy in RING_OFFSETS:
        for dx in RING_OFFSETS:
            if (dy, dx) != (0, 0):
                greet(device_at(z, wrap(y + dy, 4), wrap(x + dx, 4), c))
    greet(mate)

    @pl.when(has_left)
    def _():
        greet((gx, yz - 1))

    @pl.when(has_right)
    def _():
        greet((gx, yz + 1))

    for load in loads[3:]:
        load.start()
    pl.when(leads)(own_plate.start)

    loads[1].wait()
    loads[2].wait()
    tail = jnp.sum(impedance[1:, :] * history[...], axis=0, keepdims=True)
    cols[c, z, 1:2, :] = jnp.concatenate([impedance[0:1, :], tail], axis=1)
    loads[0].wait()
    surface = adj[2, 1:9].reshape(128, 128)
    cols[c, z, 0:1, :] = jnp.transpose(surface)[0:1, :]

    pl.semaphore_wait(barrier, greeted)

    def remote(src, dst, sem, device):
        return pltpu.make_async_remote_copy(
            src_ref=src, dst_ref=dst, send_sem=send_sems.at[sem], recv_sem=recv_sems.at[sem], device_id=device, device_id_type=MESH
        )

    def arrived(ref, sem):
        pltpu.make_async_copy(ref, ref, recv_sems.at[sem]).wait()

    def sent(ref, sem):
        pltpu.make_async_copy(ref, ref, send_sems.at[sem]).wait()

    for core, sem in ((1, 0), (0, 24)):
        for d in Z_NEAR:
            pl.when(c == core)(remote(cols.at[core, z], cols.at[core, z], sem, device_at(wrap(z + d, 16), y, x, 1)).start)
    plate_up = remote(plate, plt_buf.at[pl.ds(0, share)], 7, mate)

    @pl.when(follows)
    def _():
        remote(cols.at[0, z], cols.at[0, z], 24, mate).start()

    quarter = comps // 4
    for field, buffer, sem in ((adjoint, ring_adj, 15), (forward, ring_fwd, 1)):
        for ring in (1, 2, 0, 3):
            part = pl.ds(ring * quarter, quarter)
            if ring != 3:
                pl.when(upper)(remote(field.at[part, 7], buffer, sem, (z_hi * 4 + ring, yz)).start)
            if ring != 0:
                pl.when(lower)(remote(field.at[part, 0], buffer, sem, (z_hi * 4 + ring, yz)).start)

    for load in loads[3:]:
        load.wait()
    to_prev = remote(adj.at[:, 1], adj.at[:, 9], 20, (lax.max(gx - 1, 0), yz))
    to_next = remote(adj.at[:, 8], adj.at[:, 0], 2, (lax.min(gx + 1, 7), yz))

    def send_near():
        pl.when(near_prev)(to_prev.start)
        pl.when(near_next)(to_next.start)

    pl.when(follows)(send_near)

    @pl.when(leads)
    def _():
        arrived(cols.at[1, pl.ds(0, 8)], 0)
        arrived(cols.at[0, pl.ds(0, 9)], 24)
        for d, way in ((4, -4), (3, -4), (2, -4), (1, -4), (-3, 4), (-2, 4), (-1, 4)):
            slot = wrap(z + d, 16)
            remote(cols.at[:, slot], cols.at[:, slot], 19, device_at(wrap(z + way, 16), y, x, 1)).start()
        send_near()

    plane = jnp.zeros((16, 128), F32)
    for k in range(comps):
        fwd[k, 0] = plane
        fwd[k, 9] = plane

    @pl.when(gx == 0)
    def _():
        for k in range(comps):
            adj[k, 0] = plane

    @pl.when(gx == 7)
    def _():
        for k in range(comps):
            adj[k, 9] = plane

    @pl.when(jnp.logical_not(near_prev))
    def _():
        x_in[0] = plane

    @pl.when(jnp.logical_not(near_next))
    def _():
        x_in[1] = plane

    diagonal = iota((16, 16), 0) == iota((16, 16), 1)
    span_col = jnp.sum(jnp.where(diagonal, span[...], 0), axis=1, keepdims=True)
    frac_col = jnp.sum(jnp.where(diagonal, frac[...], 0.0), axis=1, keepdims=True)
    weights_y = spread_basis(iota((16, 128), 1), span_col, frac_col)
    depth = iota((8, 128), 1)
    depth_span = lax.div(depth, HZ)
    weights_z = spread_basis(iota((8, 128), 0), depth_span, (depth.astype(F32) + 0.5) / HZ - depth_span.astype(F32))

    for side, row in ((0, 0), (1, 15)):
        for k in range(comps):
            y_out[side, k] = adj[k, 1:9, row, :]
        y_out[side, comps] = jnp.broadcast_to(weights_y[row : row + 1, :], (8, 128))
    to_left = remote(y_out.at[0], y_in.at[1], 3, (gx, lax.max(yz - 1, 0)))
    to_right = remote(y_out.at[1], y_in.at[0], 4, (gx, lax.min(yz + 1, 63)))

    @pl.when(has_left)
    def _():
        to_left.start()

    @pl.when(has_right)
    def _():
        to_right.start()

    @pl.when(yz == 0)
    def _():
        y_in[0] = jnp.zeros_like(y_in[0])

    @pl.when(yz == 63)
    def _():
        y_in[1] = jnp.zeros_like(y_in[1])

    @pl.when(upper)
    def _():
        ring_adj[...] = adj[3 * quarter : 4 * quarter, 8]
        ring_fwd[...] = fwd[3 * quarter : 4 * quarter, 8]

    @pl.when(lower)
    def _():
        ring_adj[...] = adj[0:quarter, 1]
        ring_fwd[...] = fwd[0:quarter, 1]

    @pl.when(jnp.logical_not(jump))
    def _():
        arrived(ring_adj, 15)
        arrived(ring_fwd, 1)

    weights_out[...] = weights_y
    remote(ring_adj, mid_adj.at[c], 21, device_at(half_way, y, x, 0)).start()
    remote(ring_fwd, mid_fwd.at[c], 22, device_at(across, y, x, 0)).start()
    remote(weights_out, mid_weights.at[c], 23, device_at(half_way, y, x, 0)).start()

    pl.when(follows)(plate_up.start)
    cell = dof[...]

    @pl.when(leads)
    def _():
        cell_x, cell_y = lax.shift_right_logical(cell, 10), lax.bitwise_and(cell, 1023)
        lane = lax.bitwise_and(cell_x, 7) * 16 + lax.bitwise_and(cell_y, 15)
        cell_gx, cell_yz = lax.shift_right_logical(cell_x, 3), lax.shift_right_logical(cell_y, 4)
        in_column = jnp.logical_and(lax.bitwise_and(cell_gx, 3) == y, lax.bitwise_and(lax.shift_right_logical(cell_yz, 1), 3) == x)
        depth_of = lax.shift_right_logical(cell_gx, 2) * 8 + lax.shift_right_logical(cell_yz, 3)
        row_of[...] = jnp.where(in_column, depth_of, -1)
        lane = lax.bitwise_and(cell_yz, 1) * 128 + lane
        for tile in range(16):
            lanes = slice(tile * 256, tile * 256 + 256)
            one_hot[:, lanes] = (iota((256, 256), 0) == lane[:, lanes]).astype(F32).astype(BF16)

    cell_rank = iota((128, 1), 0)
    cell_id = (gx * 8 + lax.shift_right_logical(cell_rank, 4)) * 1024 + yz * 16 + lax.bitwise_and(cell_rank, 15)
    found = jnp.zeros((128, 128), F32)
    for tile in range(32):
        label = (iota((1, 128), 1) + (tile * 128 + 1)).astype(F32)
        found = found + jnp.where(cell[:, tile * 128 : tile * 128 + 128] == cell_id, label, 0.0)
    owner = jnp.sum(found, axis=1, keepdims=True).astype(jnp.int32) - 1
    owner_row = lax.shift_right_arithmetic(owner, 7)
    owner_lane = lax.bitwise_and(owner, 127)
    pick_row = (lax.bitwise_and(iota((128, 64), 1), 31) == owner_row).astype(F32).astype(BF16)

    def project(cells, rows):
        part = lax.dot_general(weights_z, cells, (((1,), (1,)), ((), ())), precision=HIGH, preferred_element_type=F32)
        return jnp.dot(part, rows, precision=HIGH, preferred_element_type=F32)

    z_first, z_last = iota((16, 128), 1) == 0, iota((16, 128), 1) == 127
    y_first, y_last = iota((16, 128), 0) == 0, iota((16, 128), 0) == 15

    def laplacian(field, k, i, left, right):
        value = field[k, i]
        total = field[k, i - 1] + field[k, i + 1]
        total = total + jnp.where(z_first, 0.0, pltpu.roll(value, 1, 1)) + jnp.where(z_last, 0.0, pltpu.roll(value, 127, 1))
        total = total + jnp.where(y_first, left, pltpu.roll(value, 1, 0)) + jnp.where(y_last, right, pltpu.roll(value, 15, 0))
        return total - 6.0 * value, value

    def correlate(i, carry):
        for k in range(comps):
            lap, _ = laplacian(fwd, k, i, 0.0, 0.0)
            carry = carry + adj[k, i] * lap
        return carry

    corr[0:16, :] = lax.fori_loop(1, 9, correlate, jnp.zeros((16, 128), F32))

    back_prev = remote(x_out.at[0], x_in.at[1], 10, (lax.max(gx - 1, 0), yz))
    back_next = remote(x_out.at[1], x_in.at[0], 11, (lax.min(gx + 1, 7), yz))

    def send_back(side, halo, sem, inner, copy):
        arrived(adj.at[:, halo], sem)
        product = plane
        for k in range(comps):
            product = product + adj[k, halo] * fwd[k, inner]
        x_out[side] = product
        copy.start()

    @pl.when(near_prev)
    def _():
        send_back(0, 0, 2, 1, back_prev)

    @pl.when(near_next)
    def _():
        send_back(1, 9, 20, 8, back_next)

    @pl.when(leads)
    def _():
        arrived(cols.at[:, pl.ds(0, 7)], 19)
        cells = jnp.concatenate(split(jnp.concatenate([cols[0, :, 0, :], cols[1, :, 0, :]], axis=1)), axis=0)
        for tile in range(16):
            lanes = slice(tile * 256, tile * 256 + 256)
            match = jnp.dot(cells, one_hot[:, lanes], preferred_element_type=F32)
            match = jnp.where(iota((16, 256), 0) == row_of[:, lanes], match[:16] + match[16:], 0.0)
            mine = jnp.sum(match, axis=0, keepdims=True)
            picked[yx, 2 * tile : 2 * tile + 1, :] = mine[:, 0:128]
            picked[yx, 2 * tile + 1 : 2 * tile + 2, :] = mine[:, 128:256]
        for dy in RING_OFFSETS:
            for dx in RING_OFFSETS:
                if (dy, dx) != (0, 0):
                    remote(picked.at[yx], picked.at[yx], 5, device_at(z, wrap(y + dy, 4), wrap(x + dx, 4), 1)).start()
        for core in (0, 1):
            taps_own = cols[core, 0:8, 1, :]
            for k in range(8):
                taps[k, x, core : core + 1, :] = taps_own[k : k + 1, :]
        for dx in (2, 1, 3):
            remote(taps.at[:, x], taps.at[:, x], 6, device_at(z, y, wrap(x + dx, 4), 1)).start()

    @pl.when(has_left)
    def _():
        arrived(y_in.at[0], 4)

    @pl.when(has_right)
    def _():
        arrived(y_in.at[1], 3)

    corr[16:24, :] = jnp.zeros((8, 128), F32)
    for side, row in ((0, 0), (1, 15)):
        edge = jnp.zeros((8, 128), F32)
        for k in range(comps):
            edge = edge + y_in[side, k] * fwd[k, 1:9, row, :]
        corr[16 + side : 17 + side, :] = jnp.sum(edge, axis=0, keepdims=True)

    @pl.when(near_prev)
    def _():
        arrived(x_in.at[0], 11)

    @pl.when(near_next)
    def _():
        arrived(x_in.at[1], 10)

    corr[0:16, :] = corr[0:16, :] + x_in[0] + x_in[1]
    rows = jnp.concatenate([weights_y, y_in[0, comps, 0:1, :], y_in[1, comps, 0:1, :], jnp.zeros((6, 128), F32)], axis=0)
    grad_c[0] = project(corr[...], rows)

    from_mate = remote(grad_c.at[0], grad_c.at[1], 12, mate)
    pl.when(leads)(from_mate.start)

    @pl.when(follows)
    def _():
        from_mate.wait_recv()
        grad_x[x] = grad_c[0] + grad_c[1]
        for dx in (2, 1, 3):
            remote(grad_x.at[x], grad_x.at[x], 13, device_at(z, y, wrap(x + dx, 4), 0)).start()
        arrived(mid_adj, 21)
        arrived(mid_fwd, 22)
        part = pl.ds(y * quarter, quarter)
        for core in (0, 1):
            target = device_at(across, 3 - far_y, x, core)
            pl.when(z_hi == 0)(remote(mid_adj.at[core], adj.at[part, 0], 17, target).start)
            pl.when(z_hi == 1)(remote(mid_adj.at[core], adj.at[part, 9], 17, target).start)
        arrived(mid_weights, 23)
        products = jnp.sum(mid_adj[...] * mid_fwd[...], axis=1)
        grad_plane[yx] = project(products.reshape(32, 128), mid_weights[...].reshape(32, 128))
        for k in range(4):
            target = remote(grad_plane.at[yx], grad_plane.at[yx], 18, device_at(z, far_y, k, 0))
            pl.when(jnp.logical_not(jnp.logical_and(jump, x == k)))(target.start)

    def sum_over_z():
        arrived(grad_x.at[pl.ds(0, 3)], 13)
        grad_z[z_lo] = (grad_x[0] + grad_x[1]) + (grad_x[2] + grad_x[3])

        @pl.when(jump)
        def _():
            arrived(grad_plane.at[pl.ds(0, 15)], 18)
            grad_z[z_lo] = grad_z[z_lo] + jnp.sum(grad_plane[...], axis=0)

        for d in (7, 6, 5, 4, 3, 2, 1, 0):
            for core in (0, 1):
                if (d, core) != (0, 0):
                    remote(grad_z.at[z_lo], grad_z.at[z_lo], 14, (gx, lax.rem(z_lo + d, 8) * 8 + x * 2 + core)).start()

    pl.when(jnp.logical_and(follows, jnp.logical_not(jump)))(sum_over_z)

    knots_z, _, knots_y = coarse.shape
    material = jnp.zeros((16, 128), F32)
    for k in range(knots_z):
        knot = jnp.sum(weights_y[:, 0:knots_y] * coarse[k], axis=1, keepdims=True)
        material = material + knot * weights_z[k : k + 1, :]
    material = time_step * material

    def update(i):
        laps = []
        for k in range(comps):
            lap, _ = laplacian(adj, k, i, y_in[0, k, pl.ds(i - 1, 1), :], y_in[1, k, pl.ds(i - 1, 1), :])
            laps.append(lap)
        for k in range(comps):
            mixed = laps[k]
            for m in range(comps):
                mixed = mixed + coupling[k, m] * laps[m]
            value = adj[k, i]
            updated[k, i - 1] = value + material * mixed - (time_step * damping[0, k]) * value

    @pl.loop(2, 8)
    def _(i):
        update(i)

    pl.when(jnp.logical_and(follows, jump))(sum_over_z)

    flat_row = lax.div(yz, 2)

    @pl.when(leads)
    def _():
        arrived(taps.at[:, pl.ds(0, 3)], 6)
        for k in range(32):
            for core in (0, 1):
                taps_all[core, k : k + 1, :] = taps[k // 4, k % 4, core : core + 1, :]
        first, second = taps_all[0], taps_all[1]
        low_half = iota((32, 128), 1) < 64
        taps_all[0] = jnp.where(low_half, first, pltpu.roll(second, 64, 1))
        taps_all[1] = jnp.where(low_half, pltpu.roll(first, 64, 1), second)

        arrived(picked.at[pl.ds(0, 15)], 5)
        samples = picked[0]
        for k in range(1, 16):
            samples = samples + picked[k]
        impulse[...] = taps_all[0] * samples + taps_all[1]
        flat = jnp.concatenate([impulse[k : k + 1, :] for k in range(32)], axis=1).astype(BF16)
        own_plate.wait()
        arrived(plt_buf.at[pl.ds(0, share)], 7)
        through = lax.dot_general(flat, plt_buf[...], (((1,), (1,)), ((), ())), preferred_element_type=F32)
        react[flat_row] = through + impulse[pl.ds(flat_row, 1), :]
        for dz in NEAR_OFFSETS:
            for dx in RING_OFFSETS:
                for core in (0, 1):
                    if (dz, dx, core) != (0, 0, 1):
                        target = device_at(wrap(z - dz, 16), y, wrap(x + dx, 4), core)
                        remote(react.at[flat_row], react.at[flat_row], 9, target).start()

    @pl.when(lower)
    def _():
        arrived(adj.at[:, 0], 17)

    @pl.when(upper)
    def _():
        arrived(adj.at[:, 9], 17)

    @pl.loop(0, 2)
    def _(side):
        update(1 + 7 * side)

    @pl.when(follows)
    def _():
        arrived(react, 9)

    @pl.when(leads)
    def _():
        arrived(react.at[pl.ds(0, 31)], 9)

    own_row = react[flat_row]
    reaction[...] = jnp.where(follows, own_row[:, 0:64], own_row[:, 64:128])
    head, rest = split(react[...].reshape(32, 128))
    forces = jnp.dot(pick_row, jnp.concatenate([head, rest], axis=0), preferred_element_type=F32)
    forces = jnp.sum(jnp.where(iota((128, 128), 1) == owner_lane, forces, 0.0), axis=1, keepdims=True)
    forces = (time_step * surface_gain) * forces.reshape(8, 16, 1)
    updated[2] = updated[2] + jnp.where(iota((8, 16, 128), 2) == 0, forces, 0.0)

    @pl.when(leads)
    def _():
        arrived(grad_z, 14)

    @pl.when(follows)
    def _():
        arrived(grad_z.at[pl.ds(0, 7)], 14)

    total = grad_z[0]
    for k in range(1, 8):
        total = total + grad_z[k]

    total = total / (grad_norm * 4096.0**0.5)
    for k in range(knots_z):
        grad[k] = total[k : k + 1, 0:knots_y]

    @pl.when(leads)
    def _():
        sent(cols.at[1, pl.ds(0, 8)], 0)
        sent(cols.at[:, pl.ds(0, 7)], 19)
        sent(picked.at[pl.ds(0, 15)], 5)
        sent(taps.at[:, pl.ds(0, 3)], 6)
        sent(react.at[pl.ds(0, 31)], 9)
        sent(react, 9)
        from_mate.wait_send()

    @pl.when(follows)
    def _():
        sent(cols.at[0, pl.ds(0, 9)], 24)
        sent(plt_buf.at[pl.ds(0, share)], 7)
        sent(grad_x.at[pl.ds(0, 3)], 13)
        sent(grad_plane.at[pl.ds(0, 15)], 14)
        sent(grad_plane.at[pl.ds(0, 3)], 18)
        pl.when(jnp.logical_not(jump))(lambda: sent(grad_plane.at[0], 18))
        sent(mid_adj, 17)

    sent(ring_adj, 21)
    sent(ring_fwd, 22)
    sent(weights_out, 23)
    for present, copy in (
        (near_prev, to_prev), (near_next, to_next), (has_left, to_left), (has_right, to_right),
        (near_prev, back_prev), (near_next, back_next),
    ):
        pl.when(present)(copy.wait_send)


    @pl.when(jump)
    def _():
        sent(adj.at[pl.ds(0, 3 * quarter), 0], 15)
        sent(adj.at[pl.ds(0, 3 * quarter), 0], 1)


def store_results(*refs):
    count = len(refs) // 2
    copies = [pltpu.make_async_copy(refs[k], refs[count + k], refs[-1].at[k]) for k in range(count)]
    for copy in copies:
        copy.start()
    for copy in copies:
        copy.wait()


def on_device(adjoint, forward, coarse_model, knot_span, knot_frac, dof_cell, impedance, history, plate, coupling, damping):
    comps, cells_x, cells_y, depth = adjoint.shape
    knots_y, knots_z = coarse_model.shape[1:]
    vmem = pl.BlockSpec(memory_space=pltpu.VMEM)
    hbm = pl.BlockSpec(memory_space=pltpu.HBM)
    updated, grad, reaction = pl.pallas_call(
        kernel,
        out_shape=(
            jax.ShapeDtypeStruct(adjoint.shape, F32),
            jax.ShapeDtypeStruct((knots_z, 1, knots_y), F32),
            jax.ShapeDtypeStruct((1, 64), F32),
        ),
        in_specs=[hbm] * 11,
        out_specs=(vmem, vmem, vmem),
        scratch_shapes=[
            pltpu.VMEM((knots_z, 1, knots_y), F32),
            pltpu.VMEM((1, cells_y), jnp.int32),
            pltpu.VMEM((1, cells_y), F32),
            pltpu.VMEM((1, dof_cell.size), jnp.int32),
            pltpu.VMEM(impedance.shape, F32),
            pltpu.VMEM(history.shape, F32),
            pltpu.SMEM(coupling.shape, F32),
            pltpu.SMEM((1, comps), F32),
            pltpu.VMEM((comps, cells_x + 2, cells_y, depth), F32),
            pltpu.VMEM((comps, cells_x + 2, cells_y, depth), F32),
            pltpu.VMEM((2 * plate.shape[0], plate.shape[1]), BF16),
            pltpu.VMEM((2, 16, 2, 128), F32),
            pltpu.VMEM((8, 4, 2, 128), F32),
            pltpu.VMEM((2, 32, 128), F32),
            pltpu.VMEM((16, 32, 128), F32),
            pltpu.VMEM((32, 128), F32),
            pltpu.VMEM((256, 4096), BF16),
            pltpu.VMEM((1, 4096), jnp.int32),
            pltpu.VMEM((32, 1, 128), F32),
            pltpu.VMEM((2, comps + 1, 8, 128), F32),
            pltpu.VMEM((2, comps + 1, 8, 128), F32),
            pltpu.VMEM((24, 128), F32),
            pltpu.VMEM((2, 16, 128), F32),
            pltpu.VMEM((2, 16, 128), F32),
            pltpu.VMEM((2, 8, 128), F32),
            pltpu.VMEM((4, 8, 128), F32),
            pltpu.VMEM((8, 8, 128), F32),
            pltpu.VMEM((comps // 4, cells_y, depth), F32),
            pltpu.VMEM((comps // 4, cells_y, depth), F32),
            pltpu.VMEM((2, comps // 4, cells_y, depth), F32),
            pltpu.VMEM((2, comps // 4, cells_y, depth), F32),
            pltpu.VMEM((2, cells_y, depth), F32),
            pltpu.VMEM((cells_y, depth), F32),
            pltpu.VMEM((16, 8, 128), F32),
            pltpu.SemaphoreType.DMA((16,)),
            pltpu.SemaphoreType.DMA((25,)),
            pltpu.SemaphoreType.DMA((25,)),
        ],
        compiler_params=pltpu.CompilerParams(collective_id=0, has_side_effects=True, vmem_limit_bytes=VMEM_BYTES),
        name="adjoint_step",
    )(
        *[
            pltpu.with_memory_space_constraint(operand, pltpu.HBM)
            for operand in (
                adjoint, forward, coarse_model.transpose(2, 0, 1), knot_span.reshape(1, -1), knot_frac.reshape(1, -1),
                dof_cell.reshape(1, -1), impedance, history, plate, coupling, damping.reshape(1, -1),
            )
        ]
    )
    results = (updated, grad, reaction)
    updated, grad, reaction = pl.pallas_call(
        store_results,
        out_shape=tuple(jax.ShapeDtypeStruct(a.shape, a.dtype) for a in results),
        in_specs=[vmem] * 3,
        out_specs=(hbm,) * 3,
        scratch_shapes=[pltpu.SemaphoreType.DMA((3,))],
        compiler_params=pltpu.CompilerParams(vmem_limit_bytes=STORE_VMEM_BYTES),
        name="store_results",
    )(*results)
    return updated, grad.transpose(1, 2, 0), reaction.reshape(-1)


def solution(mesh):
    return jax.shard_map(
        on_device,
        mesh=mesh,
        in_specs=(
            P(None, "gx", "yz", None),
            P(None, "gx", "yz", None),
            P("gx", None, None),
            P("yz"),
            P("yz"),
            P(),
            P(None, "yz"),
            P(None, "yz"),
            P("yz", None),
            P(),
            P(),
        ),
        out_specs=(P(None, "gx", "yz", None), P("gx", None, None), P("yz")),
        check_vma=False,
    )
```

```python
import functools

import jax
import jax.numpy as jnp
from jax import lax
from jax.experimental import pallas as pl
from jax.experimental.pallas import tpu as pltpu
from jax.sharding import PartitionSpec as P

MESH = pl.DeviceIdType.MESH
F32 = jnp.float32
BF16 = jnp.bfloat16
HIGH = lax.Precision.HIGHEST

HZ = 32
VMEM_BYTES = 16 * 1024 * 1024
STORE_VMEM_BYTES = 4 * 1024 * 1024
time_step = 0.1
surface_gain = 40.0
grad_norm = 20.0

NEAR_OFFSETS = tuple(sorted(range(-4, 4), key=lambda d: -abs(d)))
RING_OFFSETS = (2, 1, 3, 0)
Z_NEAR = (4, -4, 3, -3, 2, -2, 1, -1)


def bspline_weights(param):
    inverse = 1.0 - param
    return (
        inverse**3 / 6.0,
        (3.0 * param**3 - 6.0 * param**2 + 4.0) / 6.0,
        (-3.0 * param**3 + 3.0 * param**2 + 3.0 * param + 1.0) / 6.0,
        param**3 / 6.0,
    )


def spread_basis(index, span, param):
    total = 0.0
    for shift, weight in enumerate(bspline_weights(param)):
        total = total + jnp.where(index == span + shift, weight, 0.0)
    return total


def iota(shape, dim):
    return lax.broadcasted_iota(jnp.int32, shape, dim)


def split(values):
    head = values.astype(BF16)
    return head, (values - head.astype(F32)).astype(BF16)


def device_at(z, y, x, c):
    return (lax.div(z, 8) * 4 + y, lax.rem(z, 8) * 8 + x * 2 + c)


def wrap(value, count):
    return lax.rem(value + 2 * count, count)


def kernel(
    adjoint, forward, coarse_hbm, span_hbm, frac_hbm, dof_hbm, impedance_hbm, history_hbm, plate, coupling_hbm, damping_hbm,
    updated, grad, reaction,
    coarse, span, frac, dof, impedance, history, coupling, damping,
    adj, fwd, plt_buf, cols, taps, taps_all, picked, impulse, one_hot, row_of, react,
    y_out, y_in, corr, x_out, x_in, grad_c, grad_x, grad_z, ring_adj, ring_fwd, mid_adj, mid_fwd, mid_weights, weights_out, grad_plane,
    load_sems, send_sems, recv_sems,
):
    gx, yz = lax.axis_index("gx"), lax.axis_index("yz")
    z_hi, y = lax.div(gx, 4), lax.rem(gx, 4)
    z_lo, x, c = lax.div(yz, 8), lax.rem(lax.div(yz, 2), 4), lax.rem(yz, 2)
    z = z_hi * 8 + z_lo
    yx = y * 4 + x
    comps = adj.shape[0]
    has_prev, has_next = gx > 0, gx < 7
    has_left, has_right = yz > 0, yz < 63
    mate = (gx, yz + 1 - 2 * c)

    upper, lower = jnp.logical_and(z_hi == 0, y == 3), jnp.logical_and(z_hi == 1, y == 0)
    jump = jnp.logical_or(upper, lower)
    near_prev, near_next = jnp.logical_and(has_prev, jnp.logical_not(lower)), jnp.logical_and(has_next, jnp.logical_not(upper))
    z_half = lax.rem(z_lo + 4, 8)
    half_way, across = z_hi * 8 + z_half, (1 - z_hi) * 8 + z_half
    far_y = jnp.where(z_hi == 0, 3, 0)

    loads = [
        pltpu.make_async_copy(adjoint.at[2], adj.at[2, pl.ds(1, 8)], load_sems.at[0]),
        pltpu.make_async_copy(impedance_hbm, impedance, load_sems.at[8]),
        pltpu.make_async_copy(history_hbm, history, load_sems.at[9]),
        pltpu.make_async_copy(adjoint.at[pl.ds(0, 2)], adj.at[pl.ds(0, 2), pl.ds(1, 8)], load_sems.at[1]),
        pltpu.make_async_copy(adjoint.at[pl.ds(3, 9)], adj.at[pl.ds(3, 9), pl.ds(1, 8)], load_sems.at[2]),
        pltpu.make_async_copy(forward, fwd.at[:, pl.ds(1, 8)], load_sems.at[3]),
        pltpu.make_async_copy(coarse_hbm, coarse, load_sems.at[10]),
        pltpu.make_async_copy(span_hbm, span, load_sems.at[11]),
        pltpu.make_async_copy(frac_hbm, frac, load_sems.at[12]),
        pltpu.make_async_copy(dof_hbm, dof, load_sems.at[13]),
        pltpu.make_async_copy(coupling_hbm, coupling, load_sems.at[14]),
        pltpu.make_async_copy(damping_hbm, damping, load_sems.at[15]),
    ]
    for load in loads[:3]:
        load.start()
    leads, follows = c == 1, c == 0
    share = plate.shape[0]
    own_plate = pltpu.make_async_copy(plate, plt_buf.at[pl.ds(share, share)], load_sems.at[4])

    barrier = pltpu.get_barrier_semaphore()

    def greet(device):
        pl.semaphore_signal(barrier, inc=1, device_id=device, device_id_type=MESH)

    greeted = jnp.where(leads, 24, 26) + has_left.astype(jnp.int32) + has_right.astype(jnp.int32)

    @pl.when(leads)
    def _():
        for d in Z_NEAR:
            greet(device_at(wrap(z + d, 16), y, x, 1))
            greet(device_at(wrap(z + d, 16), y, x, 0))

    @pl.when(follows)
    def _():
        for d in (4, -4):
            greet(device_at(wrap(z + d, 16), y, x, 0))

    for dy in RING_OFFSETS:
        for dx in RING_OFFSETS:
            if (dy, dx) != (0, 0):
                greet(device_at(z, wrap(y + dy, 4), wrap(x + dx, 4), c))
    greet(mate)

    @pl.when(has_left)
    def _():
        greet((gx, yz - 1))

    @pl.when(has_right)
    def _():
        greet((gx, yz + 1))

    for load in loads[3:]:
        load.start()
    pl.when(leads)(own_plate.start)

    loads[1].wait()
    loads[2].wait()
    tail = jnp.sum(impedance[1:, :] * history[...], axis=0, keepdims=True)
    cols[c, z, 1:2, :] = jnp.concatenate([impedance[0:1, :], tail], axis=1)
    loads[0].wait()
    surface = adj[2, 1:9].reshape(128, 128)
    cols[c, z, 0:1, :] = jnp.transpose(surface)[0:1, :]

    pl.semaphore_wait(barrier, greeted)

    def remote(src, dst, sem, device):
        return pltpu.make_async_remote_copy(
            src_ref=src, dst_ref=dst, send_sem=send_sems.at[sem], recv_sem=recv_sems.at[sem], device_id=device, device_id_type=MESH
        )

    def arrived(ref, sem):
        pltpu.make_async_copy(ref, ref, recv_sems.at[sem]).wait()

    def sent(ref, sem):
        pltpu.make_async_copy(ref, ref, send_sems.at[sem]).wait()

    for core, sem in ((1, 0), (0, 24)):
        for d in Z_NEAR:
            pl.when(c == core)(remote(cols.at[core, z], cols.at[core, z], sem, device_at(wrap(z + d, 16), y, x, 1)).start)
    plate_up = remote(plate, plt_buf.at[pl.ds(0, share)], 7, mate)

    @pl.when(follows)
    def _():
        remote(cols.at[0, z], cols.at[0, z], 24, mate).start()

    quarter = comps // 4
    for field, buffer, sem in ((adjoint, ring_adj, 15), (forward, ring_fwd, 1)):
        for ring in (1, 2, 0, 3):
            part = pl.ds(ring * quarter, quarter)
            if ring != 3:
                pl.when(upper)(remote(field.at[part, 7], buffer, sem, (z_hi * 4 + ring, yz)).start)
            if ring != 0:
                pl.when(lower)(remote(field.at[part, 0], buffer, sem, (z_hi * 4 + ring, yz)).start)

    for load in loads[3:]:
        load.wait()
    to_prev = remote(adj.at[:, 1], adj.at[:, 9], 20, (lax.max(gx - 1, 0), yz))
    to_next = remote(adj.at[:, 8], adj.at[:, 0], 2, (lax.min(gx + 1, 7), yz))

    def send_near():
        pl.when(near_prev)(to_prev.start)
        pl.when(near_next)(to_next.start)

    pl.when(follows)(send_near)

    @pl.when(leads)
    def _():
        arrived(cols.at[1, pl.ds(0, 8)], 0)
        arrived(cols.at[0, pl.ds(0, 9)], 24)
        for d, way in ((4, -4), (3, -4), (2, -4), (1, -4), (-3, 4), (-2, 4), (-1, 4)):
            slot = wrap(z + d, 16)
            remote(cols.at[:, slot], cols.at[:, slot], 19, device_at(wrap(z + way, 16), y, x, 1)).start()
        send_near()

    plane = jnp.zeros((16, 128), F32)
    for k in range(comps):
        fwd[k, 0] = plane
        fwd[k, 9] = plane

    @pl.when(gx == 0)
    def _():
        for k in range(comps):
            adj[k, 0] = plane

    @pl.when(gx == 7)
    def _():
        for k in range(comps):
            adj[k, 9] = plane

    @pl.when(jnp.logical_not(near_prev))
    def _():
        x_in[0] = plane

    @pl.when(jnp.logical_not(near_next))
    def _():
        x_in[1] = plane

    diagonal = iota((16, 16), 0) == iota((16, 16), 1)
    span_col = jnp.sum(jnp.where(diagonal, span[...], 0), axis=1, keepdims=True)
    frac_col = jnp.sum(jnp.where(diagonal, frac[...], 0.0), axis=1, keepdims=True)
    weights_y = spread_basis(iota((16, 128), 1), span_col, frac_col)
    depth = iota((8, 128), 1)
    depth_span = lax.div(depth, HZ)
    weights_z = spread_basis(iota((8, 128), 0), depth_span, (depth.astype(F32) + 0.5) / HZ - depth_span.astype(F32))

    for side, row in ((0, 0), (1, 15)):
        for k in range(comps):
            y_out[side, k] = adj[k, 1:9, row, :]
        y_out[side, comps] = jnp.broadcast_to(weights_y[row : row + 1, :], (8, 128))
    to_left = remote(y_out.at[0], y_in.at[1], 3, (gx, lax.max(yz - 1, 0)))
    to_right = remote(y_out.at[1], y_in.at[0], 4, (gx, lax.min(yz + 1, 63)))

    @pl.when(has_left)
    def _():
        to_left.start()

    @pl.when(has_right)
    def _():
        to_right.start()

    @pl.when(yz == 0)
    def _():
        y_in[0] = jnp.zeros_like(y_in[0])

    @pl.when(yz == 63)
    def _():
        y_in[1] = jnp.zeros_like(y_in[1])

    @pl.when(upper)
    def _():
        ring_adj[...] = adj[3 * quarter : 4 * quarter, 8]
        ring_fwd[...] = fwd[3 * quarter : 4 * quarter, 8]

    @pl.when(lower)
    def _():
        ring_adj[...] = adj[0:quarter, 1]
        ring_fwd[...] = fwd[0:quarter, 1]

    @pl.when(jnp.logical_not(jump))
    def _():
        arrived(ring_adj, 15)
        arrived(ring_fwd, 1)

    weights_out[...] = weights_y
    remote(ring_adj, mid_adj.at[c], 21, device_at(half_way, y, x, 0)).start()
    remote(ring_fwd, mid_fwd.at[c], 22, device_at(across, y, x, 0)).start()
    remote(weights_out, mid_weights.at[c], 23, device_at(half_way, y, x, 0)).start()

    pl.when(follows)(plate_up.start)
    cell = dof[...]

    @pl.when(leads)
    def _():
        cell_x, cell_y = lax.shift_right_logical(cell, 10), lax.bitwise_and(cell, 1023)
        lane = lax.bitwise_and(cell_x, 7) * 16 + lax.bitwise_and(cell_y, 15)
        cell_gx, cell_yz = lax.shift_right_logical(cell_x, 3), lax.shift_right_logical(cell_y, 4)
        in_column = jnp.logical_and(lax.bitwise_and(cell_gx, 3) == y, lax.bitwise_and(lax.shift_right_logical(cell_yz, 1), 3) == x)
        depth_of = lax.shift_right_logical(cell_gx, 2) * 8 + lax.shift_right_logical(cell_yz, 3)
        row_of[...] = jnp.where(in_column, depth_of, -1)
        lane = lax.bitwise_and(cell_yz, 1) * 128 + lane
        for tile in range(16):
            lanes = slice(tile * 256, tile * 256 + 256)
            one_hot[:, lanes] = (iota((256, 256), 0) == lane[:, lanes]).astype(F32).astype(BF16)

    def project(cells, rows):
        part = lax.dot_general(weights_z, cells, (((1,), (1,)), ((), ())), precision=HIGH, preferred_element_type=F32)
        return jnp.dot(part, rows, precision=HIGH, preferred_element_type=F32)

    z_first, z_last = iota((16, 128), 1) == 0, iota((16, 128), 1) == 127
    y_first, y_last = iota((16, 128), 0) == 0, iota((16, 128), 0) == 15

    def laplacian(field, k, i, left, right):
        value = field[k, i]
        total = field[k, i - 1] + field[k, i + 1]
        total = total + jnp.where(z_first, 0.0, pltpu.roll(value, 1, 1)) + jnp.where(z_last, 0.0, pltpu.roll(value, 127, 1))
        total = total + jnp.where(y_first, left, pltpu.roll(value, 1, 0)) + jnp.where(y_last, right, pltpu.roll(value, 15, 0))
        return total - 6.0 * value, value

    def correlate(i, carry):
        for k in range(comps):
            lap, _ = laplacian(fwd, k, i, 0.0, 0.0)
            carry = carry + adj[k, i] * lap
        return carry

    corr[0:16, :] = lax.fori_loop(1, 9, correlate, jnp.zeros((16, 128), F32))

    back_prev = remote(x_out.at[0], x_in.at[1], 10, (lax.max(gx - 1, 0), yz))
    back_next = remote(x_out.at[1], x_in.at[0], 11, (lax.min(gx + 1, 7), yz))

    def send_back(side, halo, sem, inner, copy):
        arrived(adj.at[:, halo], sem)
        product = plane
        for k in range(comps):
            product = product + adj[k, halo] * fwd[k, inner]
        x_out[side] = product
        copy.start()

    @pl.when(near_prev)
    def _():
        send_back(0, 0, 2, 1, back_prev)

    @pl.when(near_next)
    def _():
        send_back(1, 9, 20, 8, back_next)

    @pl.when(leads)
    def _():
        arrived(cols.at[:, pl.ds(0, 7)], 19)
        cells = jnp.concatenate(split(jnp.concatenate([cols[0, :, 0, :], cols[1, :, 0, :]], axis=1)), axis=0)
        for tile in range(16):
            lanes = slice(tile * 256, tile * 256 + 256)
            match = jnp.dot(cells, one_hot[:, lanes], preferred_element_type=F32)
            match = jnp.where(iota((16, 256), 0) == row_of[:, lanes], match[:16] + match[16:], 0.0)
            mine = jnp.sum(match, axis=0, keepdims=True)
            picked[yx, 2 * tile : 2 * tile + 1, :] = mine[:, 0:128]
            picked[yx, 2 * tile + 1 : 2 * tile + 2, :] = mine[:, 128:256]
        for dy in RING_OFFSETS:
            for dx in RING_OFFSETS:
                if (dy, dx) != (0, 0):
                    remote(picked.at[yx], picked.at[yx], 5, device_at(z, wrap(y + dy, 4), wrap(x + dx, 4), 1)).start()
        for core in (0, 1):
            taps_own = cols[core, 0:8, 1, :]
            for k in range(8):
                taps[k, x, core : core + 1, :] = taps_own[k : k + 1, :]
        for dx in (2, 1, 3):
            remote(taps.at[:, x], taps.at[:, x], 6, device_at(z, y, wrap(x + dx, 4), 1)).start()

    @pl.when(has_left)
    def _():
        arrived(y_in.at[0], 4)

    @pl.when(has_right)
    def _():
        arrived(y_in.at[1], 3)

    corr[16:24, :] = jnp.zeros((8, 128), F32)
    for side, row in ((0, 0), (1, 15)):
        edge = jnp.zeros((8, 128), F32)
        for k in range(comps):
            edge = edge + y_in[side, k] * fwd[k, 1:9, row, :]
        corr[16 + side : 17 + side, :] = jnp.sum(edge, axis=0, keepdims=True)

    @pl.when(near_prev)
    def _():
        arrived(x_in.at[0], 11)

    @pl.when(near_next)
    def _():
        arrived(x_in.at[1], 10)

    corr[0:16, :] = corr[0:16, :] + x_in[0] + x_in[1]
    rows = jnp.concatenate([weights_y, y_in[0, comps, 0:1, :], y_in[1, comps, 0:1, :], jnp.zeros((6, 128), F32)], axis=0)
    grad_c[0] = project(corr[...], rows)

    from_mate = remote(grad_c.at[0], grad_c.at[1], 12, mate)
    pl.when(leads)(from_mate.start)

    @pl.when(follows)
    def _():
        from_mate.wait_recv()
        grad_x[x] = grad_c[0] + grad_c[1]
        for dx in (2, 1, 3):
            remote(grad_x.at[x], grad_x.at[x], 13, device_at(z, y, wrap(x + dx, 4), 0)).start()
        arrived(mid_adj, 21)
        arrived(mid_fwd, 22)
        part = pl.ds(y * quarter, quarter)
        for core in (0, 1):
            target = device_at(across, 3 - far_y, x, core)
            pl.when(z_hi == 0)(remote(mid_adj.at[core], adj.at[part, 0], 17, target).start)
            pl.when(z_hi == 1)(remote(mid_adj.at[core], adj.at[part, 9], 17, target).start)
        arrived(mid_weights, 23)
        products = jnp.sum(mid_adj[...] * mid_fwd[...], axis=1)
        grad_plane[yx] = project(products.reshape(32, 128), mid_weights[...].reshape(32, 128))
        for k in range(4):
            target = remote(grad_plane.at[yx], grad_plane.at[yx], 18, device_at(z, far_y, k, 0))
            pl.when(jnp.logical_not(jnp.logical_and(jump, x == k)))(target.start)

    def sum_over_z():
        arrived(grad_x.at[pl.ds(0, 3)], 13)
        grad_z[z_lo] = (grad_x[0] + grad_x[1]) + (grad_x[2] + grad_x[3])

        @pl.when(jump)
        def _():
            arrived(grad_plane.at[pl.ds(0, 15)], 18)
            grad_z[z_lo] = grad_z[z_lo] + jnp.sum(grad_plane[...], axis=0)

        for d in (7, 6, 5, 4, 3, 2, 1, 0):
            for core in (0, 1):
                if (d, core) != (0, 0):
                    remote(grad_z.at[z_lo], grad_z.at[z_lo], 14, (gx, lax.rem(z_lo + d, 8) * 8 + x * 2 + core)).start()

    pl.when(jnp.logical_and(follows, jnp.logical_not(jump)))(sum_over_z)

    knots_z, _, knots_y = coarse.shape
    material = jnp.zeros((16, 128), F32)
    for k in range(knots_z):
        knot = jnp.sum(weights_y[:, 0:knots_y] * coarse[k], axis=1, keepdims=True)
        material = material + knot * weights_z[k : k + 1, :]
    material = time_step * material

    def update(i):
        laps = []
        for k in range(comps):
            lap, _ = laplacian(adj, k, i, y_in[0, k, pl.ds(i - 1, 1), :], y_in[1, k, pl.ds(i - 1, 1), :])
            laps.append(lap)
        for k in range(comps):
            mixed = laps[k]
            for m in range(comps):
                mixed = mixed + coupling[k, m] * laps[m]
            value = adj[k, i]
            updated[k, i - 1] = value + material * mixed - (time_step * damping[0, k]) * value

    @pl.loop(2, 8)
    def _(i):
        update(i)

    pl.when(jnp.logical_and(follows, jump))(sum_over_z)

    flat_row = lax.div(yz, 2)

    @pl.when(leads)
    def _():
        arrived(taps.at[:, pl.ds(0, 3)], 6)
        for k in range(32):
            for core in (0, 1):
                taps_all[core, k : k + 1, :] = taps[k // 4, k % 4, core : core + 1, :]
        first, second = taps_all[0], taps_all[1]
        low_half = iota((32, 128), 1) < 64
        taps_all[0] = jnp.where(low_half, first, pltpu.roll(second, 64, 1))
        taps_all[1] = jnp.where(low_half, pltpu.roll(first, 64, 1), second)

        arrived(picked.at[pl.ds(0, 15)], 5)
        samples = picked[0]
        for k in range(1, 16):
            samples = samples + picked[k]
        impulse[...] = taps_all[0] * samples + taps_all[1]
        flat = jnp.concatenate([impulse[k : k + 1, :] for k in range(32)], axis=1).astype(BF16)
        own_plate.wait()
        arrived(plt_buf.at[pl.ds(0, share)], 7)
        through = lax.dot_general(flat, plt_buf[...], (((1,), (1,)), ((), ())), preferred_element_type=F32)
        react[flat_row] = through + impulse[pl.ds(flat_row, 1), :]
        for dz in NEAR_OFFSETS:
            for dx in RING_OFFSETS:
                for core in (0, 1):
                    if (dz, dx, core) != (0, 0, 1):
                        target = device_at(wrap(z - dz, 16), y, wrap(x + dx, 4), core)
                        remote(react.at[flat_row], react.at[flat_row], 9, target).start()

    @pl.when(lower)
    def _():
        arrived(adj.at[:, 0], 17)

    @pl.when(upper)
    def _():
        arrived(adj.at[:, 9], 17)

    @pl.loop(0, 2)
    def _(side):
        update(1 + 7 * side)

    cell_rank = iota((128, 1), 0)
    cell_id = (gx * 8 + lax.shift_right_logical(cell_rank, 4)) * 1024 + yz * 16 + lax.bitwise_and(cell_rank, 15)
    found = jnp.zeros((128, 128), F32)
    for tile in range(32):
        label = (iota((1, 128), 1) + (tile * 128 + 1)).astype(F32)
        found = found + jnp.where(cell[:, tile * 128 : tile * 128 + 128] == cell_id, label, 0.0)
    owner = jnp.sum(found, axis=1, keepdims=True).astype(jnp.int32) - 1
    owner_row = lax.shift_right_arithmetic(owner, 7)
    owner_lane = lax.bitwise_and(owner, 127)
    pick_row = (lax.bitwise_and(iota((128, 64), 1), 31) == owner_row).astype(F32).astype(BF16)

    @pl.when(follows)
    def _():
        arrived(react, 9)

    @pl.when(leads)
    def _():
        arrived(react.at[pl.ds(0, 31)], 9)

    own_row = react[flat_row]
    reaction[...] = jnp.where(follows, own_row[:, 0:64], own_row[:, 64:128])
    head, rest = split(react[...].reshape(32, 128))
    forces = jnp.dot(pick_row, jnp.concatenate([head, rest], axis=0), preferred_element_type=F32)
    forces = jnp.sum(jnp.where(iota((128, 128), 1) == owner_lane, forces, 0.0), axis=1, keepdims=True)
    forces = (time_step * surface_gain) * forces.reshape(8, 16, 1)
    updated[2] = updated[2] + jnp.where(iota((8, 16, 128), 2) == 0, forces, 0.0)

    @pl.when(leads)
    def _():
        arrived(grad_z, 14)

    @pl.when(follows)
    def _():
        arrived(grad_z.at[pl.ds(0, 7)], 14)

    total = grad_z[0]
    for k in range(1, 8):
        total = total + grad_z[k]

    total = total / (grad_norm * 4096.0**0.5)
    for k in range(knots_z):
        grad[k] = total[k : k + 1, 0:knots_y]

    @pl.when(leads)
    def _():
        sent(cols.at[1, pl.ds(0, 8)], 0)
        sent(cols.at[:, pl.ds(0, 7)], 19)
        sent(picked.at[pl.ds(0, 15)], 5)
        sent(taps.at[:, pl.ds(0, 3)], 6)
        sent(react.at[pl.ds(0, 31)], 9)
        sent(react, 9)
        from_mate.wait_send()

    @pl.when(follows)
    def _():
        sent(cols.at[0, pl.ds(0, 9)], 24)
        sent(plt_buf.at[pl.ds(0, share)], 7)
        sent(grad_x.at[pl.ds(0, 3)], 13)
        sent(grad_plane.at[pl.ds(0, 15)], 14)
        sent(grad_plane.at[pl.ds(0, 3)], 18)
        pl.when(jnp.logical_not(jump))(lambda: sent(grad_plane.at[0], 18))
        sent(mid_adj, 17)

    sent(ring_adj, 21)
    sent(ring_fwd, 22)
    sent(weights_out, 23)
    for present, copy in (
        (near_prev, to_prev), (near_next, to_next), (has_left, to_left), (has_right, to_right),
        (near_prev, back_prev), (near_next, back_next),
    ):
        pl.when(present)(copy.wait_send)


    @pl.when(jump)
    def _():
        sent(adj.at[pl.ds(0, 3 * quarter), 0], 15)
        sent(adj.at[pl.ds(0, 3 * quarter), 0], 1)


def store_results(*refs):
    count = len(refs) // 2
    copies = [pltpu.make_async_copy(refs[k], refs[count + k], refs[-1].at[k]) for k in range(count)]
    for copy in copies:
        copy.start()
    for copy in copies:
        copy.wait()


def on_device(adjoint, forward, coarse_model, knot_span, knot_frac, dof_cell, impedance, history, plate, coupling, damping):
    comps, cells_x, cells_y, depth = adjoint.shape
    knots_y, knots_z = coarse_model.shape[1:]
    vmem = pl.BlockSpec(memory_space=pltpu.VMEM)
    hbm = pl.BlockSpec(memory_space=pltpu.HBM)
    updated, grad, reaction = pl.pallas_call(
        kernel,
        out_shape=(
            jax.ShapeDtypeStruct(adjoint.shape, F32),
            jax.ShapeDtypeStruct((knots_z, 1, knots_y), F32),
            jax.ShapeDtypeStruct((1, 64), F32),
        ),
        in_specs=[hbm] * 11,
        out_specs=(vmem, vmem, vmem),
        scratch_shapes=[
            pltpu.VMEM((knots_z, 1, knots_y), F32),
            pltpu.VMEM((1, cells_y), jnp.int32),
            pltpu.VMEM((1, cells_y), F32),
            pltpu.VMEM((1, dof_cell.size), jnp.int32),
            pltpu.VMEM(impedance.shape, F32),
            pltpu.VMEM(history.shape, F32),
            pltpu.SMEM(coupling.shape, F32),
            pltpu.SMEM((1, comps), F32),
            pltpu.VMEM((comps, cells_x + 2, cells_y, depth), F32),
            pltpu.VMEM((comps, cells_x + 2, cells_y, depth), F32),
            pltpu.VMEM((2 * plate.shape[0], plate.shape[1]), BF16),
            pltpu.VMEM((2, 16, 2, 128), F32),
            pltpu.VMEM((8, 4, 2, 128), F32),
            pltpu.VMEM((2, 32, 128), F32),
            pltpu.VMEM((16, 32, 128), F32),
            pltpu.VMEM((32, 128), F32),
            pltpu.VMEM((256, 4096), BF16),
            pltpu.VMEM((1, 4096), jnp.int32),
            pltpu.VMEM((32, 1, 128), F32),
            pltpu.VMEM((2, comps + 1, 8, 128), F32),
            pltpu.VMEM((2, comps + 1, 8, 128), F32),
            pltpu.VMEM((24, 128), F32),
            pltpu.VMEM((2, 16, 128), F32),
            pltpu.VMEM((2, 16, 128), F32),
            pltpu.VMEM((2, 8, 128), F32),
            pltpu.VMEM((4, 8, 128), F32),
            pltpu.VMEM((8, 8, 128), F32),
            pltpu.VMEM((comps // 4, cells_y, depth), F32),
            pltpu.VMEM((comps // 4, cells_y, depth), F32),
            pltpu.VMEM((2, comps // 4, cells_y, depth), F32),
            pltpu.VMEM((2, comps // 4, cells_y, depth), F32),
            pltpu.VMEM((2, cells_y, depth), F32),
            pltpu.VMEM((cells_y, depth), F32),
            pltpu.VMEM((16, 8, 128), F32),
            pltpu.SemaphoreType.DMA((16,)),
            pltpu.SemaphoreType.DMA((25,)),
            pltpu.SemaphoreType.DMA((25,)),
        ],
        compiler_params=pltpu.CompilerParams(collective_id=0, has_side_effects=True, vmem_limit_bytes=VMEM_BYTES),
        name="adjoint_step",
    )(
        *[
            pltpu.with_memory_space_constraint(operand, pltpu.HBM)
            for operand in (
                adjoint, forward, coarse_model.transpose(2, 0, 1), knot_span.reshape(1, -1), knot_frac.reshape(1, -1),
                dof_cell.reshape(1, -1), impedance, history, plate, coupling, damping.reshape(1, -1),
            )
        ]
    )
    results = (updated, grad, reaction)
    updated, grad, reaction = pl.pallas_call(
        store_results,
        out_shape=tuple(jax.ShapeDtypeStruct(a.shape, a.dtype) for a in results),
        in_specs=[vmem] * 3,
        out_specs=(hbm,) * 3,
        scratch_shapes=[pltpu.SemaphoreType.DMA((3,))],
        compiler_params=pltpu.CompilerParams(vmem_limit_bytes=STORE_VMEM_BYTES),
        name="store_results",
    )(*results)
    return updated, grad.transpose(1, 2, 0), reaction.reshape(-1)


def solution(mesh):
    return jax.shard_map(
        on_device,
        mesh=mesh,
        in_specs=(
            P(None, "gx", "yz", None),
            P(None, "gx", "yz", None),
            P("gx", None, None),
            P("yz"),
            P("yz"),
            P(),
            P(None, "yz"),
            P(None, "yz"),
            P("yz", None),
            P(),
            P(),
        ),
        out_specs=(P(None, "gx", "yz", None), P("gx", None, None), P("yz")),
        check_vma=False,
    )
```
